128 devices in a mesh: section: 2 (over y_lo), row: 4 (over x), col: 16 (over y_hi, z, core).
Axes of the slice: x: 4, y: 4 (y_hi: 2, y_lo: 2; y = y_hi * 2 + y_lo), z: 4, core: 2. Of those that a mesh axis runs over, the one named last changes fastest.
Arguments:
- ends_in: bfloat16 [2, 2, 16, 256, 1024], P('section', None, 'col', 'row'), may hold values from -6 to 6
- q_weight: bfloat16 [2, 1024, 1024], P('section', 'col', 'row'), may hold values from -1.5 to 1.5
- key_projection: bfloat16 [2, 1024, 512], P('section', 'col', 'row'), may hold values from -0.1875 to 0.1875
- value_projection: bfloat16 [2, 1024, 512], P('section', 'col', 'row'), may hold values from -0.1875 to 0.1875
- out_weight: bfloat16 [2, 1024, 1024], P('section', 'col', 'row'), may hold values from -3 to 3
- attn_gain: float32 [2, 1024], P('section'), may hold values from 0.5 to 1.5
- moe_gain: float32 [2, 1024], P('section'), may hold values from 0.5 to 1.5
- gate_weight: bfloat16 [2, 32, 1024, 512], P('section', 'col'), may hold values from -0.1875 to 0.1875
- up_weight: bfloat16 [2, 32, 1024, 512], P('section', 'col'), may hold values from -0.1875 to 0.1875
- down_weight: bfloat16 [2, 32, 512, 1024], P('section', 'col'), may hold values from -3 to 3
- routes: int32 [2, 2, 16, 256, 8], P('section', None, 'col', 'row'), may hold values from 0 to 31, all different within a row; in each aligned block of 64 rows (0 to 63, 64 to 127, ..., all dimensions but the last counted through in order) at most 24 rows name the same one
- gates: float32 [2, 2, 16, 256, 8], P('section', None, 'col', 'row'), may hold values from 0.06 to 0.19
- lengths: int32 [2, 16, 4], P(None, 'col'), may hold values from 1 to 193, 256 in all within a row
Outputs:
- ends_out: bfloat16 [2, 2, 16, 256, 1024], P('section', None, 'col', 'row')
- grad_q_weight: float32 [2, 1024, 1024], P('section', 'col', 'row')
- grad_k_weight: float32 [2, 1024, 512], P('section', 'col', 'row')
- grad_v_weight: float32 [2, 1024, 512], P('section', 'col', 'row')
- grad_out_weight: float32 [2, 1024, 1024], P('section', 'col', 'row')
- grad_attn_gain: float32 [2, 1024], P('section')
- grad_moe_gain: float32 [2, 1024], P('section')
- grad_gate_weight: float32 [2, 32, 1024, 512], P('section', 'col', 'row')
- grad_up_weight: float32 [2, 32, 1024, 512], P('section', 'col', 'row')
- grad_down_weight: float32 [2, 32, 512, 1024], P('section', 'col', None, 'row')
The draws below stay inside these ranges and needn't reach their ends.
Inputs may be any that keep to these rules, and one draw needn't show every extreme that they name: In each aligned block of 64 tokens (rows of all leading dimensions in order; the tokens of one device), no expert is named by more than 24 routes, one by exactly 24; a token's 8 routes are different experts. Each pack's 4 lengths sum to 256; the longest is exactly 193.
All inputs are finite; a program needn't handle non-finite values.
Results may differ from the reference program's by a relative error of at most 0.03.
Values may be sent and summed in bfloat16 or wider, within the bound.
A program may use at most 128 MiB of HBM per device.

```python
import math
import jax
import jax.numpy as jnp
import numpy as np
from jax import lax

MODEL_DIMENSION = 1024
QUERY_HEADS = 16
KEY_VALUE_HEADS = 8
HEAD_SIZE = 64
FF = 512
TOP = 8
QTOK = 64
MICRO = 2
NSEQ = 4
EXPERTS = 32
PACK_TOKENS = 256
PACKS = 16
LONGEST = 193
CAP = 24
N_SECTION = 2


def levels(rng, extent, cuts, least, high):
    def one(position, parts):
        steps = jax.random.uniform(jax.random.fold_in(jax.random.fold_in(rng, 6), position), (parts,), jnp.float32, least / len(cuts), high / len(cuts))
        return jnp.repeat(jnp.exp(steps), extent[position] // parts).reshape((-1,) + (1,) * (len(extent) - position - 1))

    factor_of = one(*cuts[0])
    for cut in cuts[1:]:
        factor_of = factor_of * one(*cut)
    return factor_of


def length_profile(number_of, total, bound, skew):
    weights = [(1 << 20) // math.isqrt(standing ** skew) + 1 for standing in range(2, number_of + 1)]
    spare, counts = total - bound - (number_of - 1), [1] * (number_of - 1)
    while spare > 0:
        movable = [i for i in range(number_of - 1) if counts[i] < bound]
        pool, budget = sum([weights[i] for i in movable]), spare
        for i in movable:
            addition = min(bound - counts[i], max(1, budget * weights[i] // pool), spare)
            counts[i] = counts[i] + addition
            spare = spare - addition
    return np.array([bound] + counts)


def ragged(key, amount, total, bound, slope):
    if amount == 2:
        one = jax.random.randint(key, (), max(1, total - bound), min(bound, total - 1) + 1)
        return jnp.stack([one, total - one])
    tallies = jnp.asarray(length_profile(amount, total, bound, slope), jnp.int32)
    pairs = (amount - 1) // 2
    source_of, taker = tallies[1:1 + 2 * pairs:2], tallies[2:2 + 2 * pairs:2]
    room = jnp.minimum(source_of - 1, bound - taker)
    moved = jax.random.randint(jax.random.fold_in(key, 1), (pairs,), 0, 1 << 20) % (room + 1)
    tallies = tallies.at[1:1 + 2 * pairs:2].set(source_of - moved).at[2:2 + 2 * pairs:2].set(taker + moved)
    return tallies[jax.random.permutation(jax.random.fold_in(key, 2), amount)]


def shared_out(stream_key, own, number, rows, count, top, most, lean):
    ranking = jax.random.permutation(stream_key, count)
    crowded, usual = shares(count, rows * top, most, lean, True), shares(count, rows * top, most, lean, False)
    places = jnp.arange(count)

    def named(tallies, offset_by):
        used = int((tallies > 0).sum())
        fixed = max(1, used // 4)
        moved = fixed + (places - fixed + offset_by * (used - fixed)) % max(1, count - fixed)
        return jnp.zeros((count,), jnp.int32).at[ranking[jnp.where(places < fixed, places, moved)]].set(jnp.asarray(tallies, jnp.int32))

    tallies = jnp.where(number % 4 == 0, named(crowded, number // 4), named(usual, number - number // 4 - 1))
    mixed = jax.random.permutation(jax.random.fold_in(own, 3), count)
    donor, taker = mixed[0:count // 2 * 2:2], mixed[1:count // 2 * 2:2]
    room = jnp.minimum(tallies[donor] - 1, most - tallies[taker]) // 2
    room = jnp.where((donor == ranking[0]) | (taker == ranking[0]) | (tallies[taker] == 0), 0, jnp.maximum(room, 0))
    moved = jax.random.randint(jax.random.fold_in(own, 4), (count // 2,), 0, 1 << 20) % (room + 1)
    tallies = tallies.at[donor].add(-moved).at[taker].add(moved)
    members = jnp.searchsorted(jnp.cumsum(tallies), jnp.arange(rows * top), side="right").astype(jnp.int32)
    listing = members.reshape(top, rows).T
    listing = listing[jax.random.permutation(jax.random.fold_in(own, 1), rows)]
    offset_by = jax.random.randint(jax.random.fold_in(own, 2), (rows, 1), 0, top)
    return jnp.take_along_axis(listing, (jnp.arange(top)[None, :] + offset_by) % top, axis=1)


def shares(amount, total, most, slope, full):
    portions = [(1 << 20) // math.isqrt(rank ** slope) + 1 for rank in range(1, amount + 1)]
    largest = most if full else min(most, max(-(-total // amount), total * portions[0] // sum(portions)))
    least = 1 if total - largest >= amount - 1 else 0
    holding, spare = [largest] + [least] * (amount - 1), total - largest - least * (amount - 1)
    while spare > 0:
        candidates = [i for i in range(1, amount) if holding[i] < largest] or [i for i in range(1, amount) if holding[i] < most]
        whole, budget = sum([portions[i] for i in candidates]), spare
        for i in candidates:
            more = min(most - holding[i], max(1, budget * portions[i] // whole), spare)
            holding[i] = holding[i] + more
            spare = spare - more
    return np.array(holding)


def normal_values(rng, shape, deviation, reach, pieces=(), kind=jnp.bfloat16):
    values = jax.random.normal(rng, shape, jnp.float32) * deviation
    if len(pieces) > 0:
        values = levels(rng, shape, pieces, -0.22, 0.18) * values
    return jnp.clip(values, min=-reach, max=reach).astype(kind)


def setup_inputs(seed: int = 0) -> dict:
    key_list = jax.random.split(jax.random.key(seed), 14)
    ends_in = normal_values(key_list[0], (2, MICRO, PACKS, PACK_TOKENS, MODEL_DIMENSION), 1.0, 6.0, ((0, 2), (2, 16), (3, 4)))
    q_weight = normal_values(key_list[1], (N_SECTION, MODEL_DIMENSION, QUERY_HEADS * HEAD_SIZE), (MODEL_DIMENSION * HEAD_SIZE // 4096) ** -0.5, 1.5, ((0, 2), (1, 16), (2, 4)))
    key_projection = normal_values(key_list[2], (N_SECTION, MODEL_DIMENSION, KEY_VALUE_HEADS * HEAD_SIZE), MODEL_DIMENSION ** -0.5, 0.1875, ((0, 2), (1, 16), (2, 4)))
    value_projection = normal_values(key_list[3], (N_SECTION, MODEL_DIMENSION, KEY_VALUE_HEADS * HEAD_SIZE), MODEL_DIMENSION ** -0.5, 0.1875, ((0, 2), (1, 16), (2, 4)))
    out_weight = normal_values(key_list[4], (N_SECTION, MODEL_DIMENSION, QUERY_HEADS * HEAD_SIZE), (HEAD_SIZE // 16) ** -0.5, 3.0, ((0, 2), (1, 16), (2, 4)))
    attn_gain = jnp.clip(1.0 + 0.1 * jax.random.normal(key_list[5], (N_SECTION, MODEL_DIMENSION), jnp.float32), 0.5, 1.5)
    moe_gain = jnp.clip(1.0 + 0.1 * jax.random.normal(key_list[6], (N_SECTION, MODEL_DIMENSION), jnp.float32), 0.5, 1.5)
    gate_weight = normal_values(key_list[7], (N_SECTION, EXPERTS, MODEL_DIMENSION, FF), MODEL_DIMENSION ** -0.5, 0.1875, ((0, 2), (1, 16)))
    up_weight = normal_values(key_list[8], (N_SECTION, EXPERTS, MODEL_DIMENSION, FF), MODEL_DIMENSION ** -0.5, 0.1875, ((0, 2), (1, 16)))
    down_weight = normal_values(key_list[9], (N_SECTION, EXPERTS, FF, MODEL_DIMENSION), (max(1, FF // 128)) ** -0.5, 3.0, ((0, 2), (1, 16)))
    routes_keys = jax.random.split(jax.random.fold_in(key_list[10], 1), N_SECTION * MICRO * PACKS * PACK_TOKENS // QTOK)
    routes_turns = jax.random.permutation(jax.random.fold_in(key_list[10], 3), N_SECTION * MICRO * PACKS * PACK_TOKENS // QTOK)
    routes = jax.vmap(lambda own, number: shared_out(jax.random.fold_in(key_list[10], 2), own, number, QTOK, EXPERTS, TOP, CAP, 1))(routes_keys, routes_turns).reshape((N_SECTION, MICRO, PACKS, PACK_TOKENS, TOP))
    gates = jnp.clip(0.06 + 0.13 * jax.random.uniform(key_list[11], (N_SECTION, MICRO, PACKS, PACK_TOKENS, TOP), jnp.float32) ** levels(key_list[11], (N_SECTION, MICRO, PACKS, PACK_TOKENS, TOP), ((0, 2), (2, 16), (3, 4)), -0.2, 0.2), 0.06, 0.19)
    lengths = jax.vmap(lambda own: ragged(own, NSEQ, PACK_TOKENS, LONGEST, 2))(jax.random.split(key_list[12], MICRO * PACKS)).reshape((MICRO, PACKS, NSEQ)).astype(jnp.int32)
    return dict(ends_in=ends_in, q_weight=q_weight, key_projection=key_projection, value_projection=value_projection, out_weight=out_weight, attn_gain=attn_gain, moe_gain=moe_gain, gate_weight=gate_weight, up_weight=up_weight, down_weight=down_weight, routes=routes, gates=gates, lengths=lengths)


SCORE_MUL = 0.015625
RESID_MUL = 0.22
NORM_EPS = 1e-06
ROPE_THETA = 10000.0
EXACT_PRECISION = lax.Precision.HIGHEST

@jax.custom_vjp
def low(v):
    return lax.optimization_barrier(v.astype(jnp.bfloat16)).astype(jnp.float32)

@jax.custom_vjp
def low_back(v):
    return v

def low_keep(v):
    return (low(v), None)

def low_pass(kept, grad):
    return (grad,)

def back_keep(v):
    return (v, None)

def back_low(kept, grad):
    return (low(grad),)
low.defvjp(low_keep, low_pass)
low_back.defvjp(back_keep, back_low)

def layout_tables(length_row):
    ends_at = jnp.cumsum(length_row).astype(jnp.int32)
    places = jnp.arange(PACK_TOKENS, dtype=jnp.int32)
    passed = places[:, None] >= ends_at[None, :]
    segment = lax.optimization_barrier(jnp.sum(passed.astype(jnp.int32), axis=1)).astype(jnp.int32)
    starts = lax.optimization_barrier(jnp.sum(jnp.where(passed, length_row[None, :], 0), axis=1)).astype(jnp.int32)
    offset = (places - starts).astype(jnp.float32)
    frequency = ROPE_THETA ** (-(jnp.arange(HEAD_SIZE // 2, dtype=jnp.float32) * 2.0 / HEAD_SIZE))
    angles = offset[:, None] * frequency[None, :]
    cosine_table = jnp.concatenate([jnp.cos(angles), jnp.cos(angles)], axis=1)[:, None, :]
    sine_table = jnp.concatenate([jnp.sin(angles), jnp.sin(angles)], axis=1)[:, None, :]
    allowed = (segment[:, None] == segment[None, :]) & (places[None, :] <= places[:, None])
    return (cosine_table, sine_table, allowed)

def turn_half(values):
    middle = values.shape[-1] // 2
    return jnp.concatenate([-values[..., middle:], values[..., :middle]], axis=-1)

def rotary(values, cosine_table, sine_table):
    return values * cosine_table + turn_half(values) * sine_table

def attention_pack(hidden_in, length_row, query_weight, key_matrix, value_matrix, output_weight, gain_row):
    cosine_table, sine_table, allowed = layout_tables(length_row)
    scale_row = lax.rsqrt(lax.optimization_barrier(jnp.mean(hidden_in * hidden_in, axis=1)) + NORM_EPS)
    normed_hidden = low(hidden_in * scale_row[:, None] * gain_row)
    query_pre = jnp.dot(normed_hidden, query_weight, precision=EXACT_PRECISION).reshape(PACK_TOKENS, QUERY_HEADS, HEAD_SIZE)
    key_before_rotary = jnp.dot(normed_hidden, key_matrix, precision=EXACT_PRECISION).reshape(PACK_TOKENS, KEY_VALUE_HEADS, HEAD_SIZE)
    value_before_heads = jnp.dot(normed_hidden, value_matrix, precision=EXACT_PRECISION).reshape(PACK_TOKENS, KEY_VALUE_HEADS, HEAD_SIZE)
    query_token_rows = low(rotary(low_back(query_pre), cosine_table, sine_table))
    key_rows = low(rotary(low_back(key_before_rotary), cosine_table, sine_table))
    value_rows = low(low_back(value_before_heads))
    grouped_heads = query_token_rows.reshape(PACK_TOKENS, KEY_VALUE_HEADS, QUERY_HEADS // KEY_VALUE_HEADS, HEAD_SIZE)
    scores = low_back(jnp.einsum('qhgd,shd->hgqs', grouped_heads, key_rows, precision=EXACT_PRECISION) * SCORE_MUL)
    scores = jnp.where(allowed, scores, -1e+30)
    highest = lax.optimization_barrier(jnp.max(scores, axis=-1, keepdims=True))
    weights = jnp.exp(scores - highest)
    probability = weights / lax.optimization_barrier(jnp.sum(weights, axis=-1, keepdims=True))
    mixed = jnp.einsum('hgqs,shd->qhgd', low(probability), value_rows, precision=EXACT_PRECISION)
    mixed = low(low_back(mixed.reshape(PACK_TOKENS, QUERY_HEADS * HEAD_SIZE)))
    return low_back(jnp.dot(mixed, output_weight.T, precision=EXACT_PRECISION))

def routing(route_rows, gate_rows):
    flat_routes = route_rows.reshape(-1).astype(jnp.int32)
    chosen = (flat_routes[:, None] == jnp.arange(EXPERTS, dtype=jnp.int32)[None, :]).astype(jnp.int32)
    earlier = jnp.cumsum(chosen, axis=0).astype(jnp.int32) - chosen
    slot_index = lax.optimization_barrier(jnp.sum(earlier * chosen, axis=1)).astype(jnp.int32)
    target = flat_routes * CAP + slot_index
    placing = (target[:, None] == jnp.arange(EXPERTS * CAP, dtype=jnp.int32)[None, :]).astype(jnp.float32)
    placing = placing.reshape(QTOK, TOP, EXPERTS * CAP)
    dispatch = lax.optimization_barrier(jnp.sum(placing, axis=1))
    combine = lax.optimization_barrier(jnp.sum(gate_rows[:, :, None] * placing, axis=1))
    return (dispatch, combine)

def expert_block(resid_rows, route_rows, gate_rows, gain_row, gate_mats, up_mats, down_mats):
    scale_row = lax.rsqrt(lax.optimization_barrier(jnp.mean(resid_rows * resid_rows, axis=1)) + NORM_EPS)
    normed_hidden = low(resid_rows * scale_row[:, None] * gain_row)
    dispatch, combine = routing(route_rows, gate_rows)
    sent = low_back(jnp.dot(dispatch.T, normed_hidden, precision=EXACT_PRECISION)).reshape(EXPERTS, CAP, MODEL_DIMENSION)
    gate_pre = low_back(jnp.einsum('ecd,edf->ecf', sent, gate_mats, precision=EXACT_PRECISION))
    up_pre = low_back(jnp.einsum('ecd,edf->ecf', sent, up_mats, precision=EXACT_PRECISION))
    hidden = low(jax.nn.silu(gate_pre) * up_pre)
    produced = low(low_back(jnp.einsum('ecf,efd->ecd', hidden, down_mats, precision=EXACT_PRECISION)))
    mixture = jnp.dot(combine, produced.reshape(EXPERTS * CAP, MODEL_DIMENSION), precision=EXACT_PRECISION)
    return low(low_back(resid_rows + RESID_MUL * mixture))

def layer(hidden_all, length_all, route_all, gate_all, query_weight, key_matrix, value_matrix, output_weight, attn_gain_row, moe_gain_row, gate_mats, up_mats, down_mats):
    flat_rows = hidden_all.reshape(-1, PACK_TOKENS, MODEL_DIMENSION)
    flat_lengths = length_all.reshape(-1, NSEQ)

    def attend_one(pair_items):
        return attention_pack(pair_items[0], pair_items[1], query_weight, key_matrix, value_matrix, output_weight, attn_gain_row)
    attended = lax.map(jax.checkpoint(attend_one), (flat_rows, flat_lengths))
    resid = (flat_rows + RESID_MUL * attended).reshape(-1, QTOK, MODEL_DIMENSION)

    def expert_one(trio_items):
        return expert_block(trio_items[0], trio_items[1], trio_items[2], moe_gain_row, gate_mats, up_mats, down_mats)
    outcome = lax.map(jax.checkpoint(expert_one), (resid, route_all.reshape(-1, QTOK, TOP), gate_all.reshape(-1, QTOK, TOP)))
    return outcome.reshape(hidden_all.shape)

def reference(ends_in, q_weight, key_projection, value_projection, out_weight, attn_gain, moe_gain, gate_weight, up_weight, down_weight, routes, gates, lengths):
    start_rows = ends_in[0].astype(jnp.float32)
    cotangent = ends_in[1].astype(jnp.float32)
    params = tuple((item.astype(jnp.float32) for item in (q_weight, key_projection, value_projection, out_weight, attn_gain, moe_gain, gate_weight, up_weight, down_weight)))

    def forward(hidden_all, query_all, key_all, value_all, output_all, attn_gains, moe_gains, gate_all, up_all, down_all):
        for depth in range(N_SECTION):
            hidden_all = layer(hidden_all, lengths, routes[depth], gates[depth], query_all[depth], key_all[depth], value_all[depth], output_all[depth], attn_gains[depth], moe_gains[depth], gate_all[depth], up_all[depth], down_all[depth])
        return hidden_all
    outcome, pullback = jax.vjp(forward, start_rows, *params)
    grads = pullback(cotangent)
    ends_out = jnp.stack([grads[0], outcome]).astype(jnp.bfloat16)
    return (ends_out, grads[1], grads[2], grads[3], grads[4], grads[5], grads[6], grads[7], grads[8], grads[9])
```

```python
import functools

import jax
import jax.numpy as jnp
from jax import lax
from jax.experimental import pallas as pl
from jax.experimental.pallas import tpu as pltpu
from jax.sharding import PartitionSpec as P

D = 1024
FF = 512
HEAD = 64
TOK = 64
ROWS = 4
COLS = 16
CHIPS = 8
CAP = 24
PACK = 256
SLOTS = COLS * CAP
QUADS = 4

SCORE_MUL = 0.015625
RESID_MUL = 0.22
NORM_EPS = 1e-06
ROPE_THETA = 10000.0
MESH = pl.DeviceIdType.MESH
BF = jnp.bfloat16
F32 = jnp.float32
VM = pl.BlockSpec(memory_space=pltpu.VMEM)
DMA = pltpu.SemaphoreType.DMA


def dot(a, b):
    return jnp.dot(a, b, preferred_element_type=F32)


def dot_rows(a, b):
    return lax.dot_general(a, b, (((0,), (0,)), ((), ())), preferred_element_type=F32)


def dot_cols(a, b):
    return lax.dot_general(a, b, (((1,), (1,)), ((), ())), preferred_element_type=F32)


class Place:
    def __init__(self):
        self.section = lax.axis_index("section")
        self.row = lax.axis_index("row")
        self.col = lax.axis_index("col")
        self.chip = self.col // 2
        self.core = lax.rem(self.col, 2)

    def row_peer(self, step):
        return (self.section, lax.rem(self.row + step, ROWS), self.col)

    def chip_at(self, step):
        return lax.rem(self.chip + step + CHIPS, CHIPS)

    def chip_peer(self, step):
        return (self.section, self.row, self.chip_at(step) * 2 + self.core)

    def buddy(self):
        return (self.section, self.row, self.chip * 2 + 1 - self.core)

    def across(self):
        return (1 - self.section, self.row, self.col)


def greet(partners):
    barrier = pltpu.get_barrier_semaphore()
    for partner in partners:
        pl.semaphore_signal(barrier, inc=1, device_id=partner, device_id_type=MESH)
    pl.semaphore_wait(barrier, len(partners))


def remote(src, dst, send, recv, device):
    return pltpu.make_async_remote_copy(
        src_ref=src, dst_ref=dst, send_sem=send, recv_sem=recv, device_id=device, device_id_type=MESH
    )


def row_partners(me):
    return [me.row_peer(step) for step in (1, 2, 3)]


def col_partners(me):
    return [me.chip_peer(step) for step in range(1, CHIPS)] + [me.buddy()]


ROW_SEMS = [DMA((3,)), DMA((3,))]
COL_SEMS = [DMA((7,)), DMA((7,)), DMA((8,)), DMA((8,))]


def gather_row_start(me, out, sems):
    copies = []
    for step in (2, 1, 3):
        copy = remote(
            out.at[me.row], out.at[me.row], sems[0].at[step - 1], sems[1].at[step - 1], me.row_peer(step)
        )
        copy.start()
        copies.append(copy)
    return copies


def gather_row_finish(me, out, sems, copies):
    for step in (1, 3, 2):
        origin = lax.rem(me.row - step + ROWS, ROWS)
        remote(
            out.at[origin], out.at[origin], sems[0].at[step - 1], sems[1].at[step - 1], me.row_peer(step)
        ).wait_recv()
    for copy in copies:
        copy.wait_send()


def gather_col_start(me, out, sems):
    copies = []
    for step in (4, 2, 6, 5, 3, 7, 1):
        copy = remote(
            out.at[me.col], out.at[me.col], sems[0].at[step - 1], sems[1].at[step - 1], me.chip_peer(step)
        )
        copy.start()
        copies.append(copy)
    copy = remote(out.at[me.col], out.at[me.col], sems[2].at[0], sems[3].at[0], me.buddy())
    copy.start()
    copies.append(copy)
    return copies


def gather_col_finish(me, out, sems, copies):
    for step in (1, 7, 3, 5, 2, 6, 4):
        origin = me.chip_at(-step) * 2 + me.core
        remote(
            out.at[origin], out.at[origin], sems[0].at[step - 1], sems[1].at[step - 1], me.chip_peer(step)
        ).wait_recv()
        copy = remote(out.at[origin], out.at[origin], sems[2].at[step], sems[3].at[step], me.buddy())
        copy.start()
        copies.append(copy)
    for step in range(CHIPS):
        origin = me.chip_at(-step) * 2 + 1 - me.core
        remote(
            out.at[origin], out.at[origin], sems[2].at[step], sems[3].at[step], me.buddy()
        ).wait_recv()
    for copy in copies:
        copy.wait_send()


def sum_row(me, part, landing, sems):
    copies = []
    for step in (2, 1, 3):
        target = lax.rem(me.row + step, ROWS)
        copy = remote(
            part.at[target], landing.at[step - 1], sems[0].at[step - 1], sems[1].at[step - 1], me.row_peer(step)
        )
        copy.start()
        copies.append((step, copy))
    total = part[me.row].astype(F32)
    for step, copy in copies[1:] + copies[:1]:
        copy.wait_recv()
        total = total + landing[step - 1].astype(F32)
    return total, [copy for _, copy in copies]


SUM_STEPS = (4, 2, 6, 5, 3, 7, 1)


def sum_col(me, part, halves, outgoing, landing, sems):
    first = []
    for step in SUM_STEPS + (0,):
        target = me.chip_at(step) * 2 + 1 - me.core
        copy = remote(part.at[target], halves.at[step], sems[2].at[step], sems[3].at[step], me.buddy())
        copy.start()
        first.append(copy)
    second = []
    for step, copy in zip(SUM_STEPS, first):
        copy.wait_recv()
        mine = me.chip_at(step) * 2 + me.core
        outgoing[step - 1] = (part[mine].astype(F32) + halves[step].astype(F32)).astype(BF)
        away = remote(
            outgoing.at[step - 1], landing.at[step - 1], sems[0].at[step - 1], sems[1].at[step - 1], me.chip_peer(step)
        )
        away.start()
        second.append(away)
    first[-1].wait_recv()
    total = part[me.col].astype(F32) + halves[0].astype(F32)
    for step, away in list(zip(SUM_STEPS, second))[::-1]:
        away.wait_recv()
        total = total + landing[step - 1].astype(F32)
    return total, first + second


def finish(copies):
    for copy in copies:
        copy.wait_send()


def sum_col_scratch(width):
    return [
        pltpu.VMEM((8, TOK, width), BF),
        pltpu.VMEM((7, TOK, width), BF),
        pltpu.VMEM((7, TOK, width), BF),
    ]


def start_kernel(w_ref, rg_ref, x_ref, w_out, rg_out, x_out, *sems):
    me = Place()
    greet(row_partners(me) + col_partners(me))
    w_out[me.col] = w_ref[...]
    rg_out[me.col] = rg_ref[...]
    x_out[me.row] = x_ref[...]
    xs = gather_row_start(me, x_out, sems[0:2])
    rs = gather_col_start(me, rg_out, sems[2:6])
    ws = gather_col_start(me, w_out, sems[6:10])
    gather_row_finish(me, x_out, sems[0:2], xs)
    gather_col_finish(me, rg_out, sems[2:6], rs)
    gather_col_finish(me, w_out, sems[6:10], ws)


def attended_kernel(part, packed, gain, resid, out, landing, *sems):
    me = Place()
    greet(row_partners(me) + col_partners(me))
    total, copies = sum_row(me, part, landing, sems[0:2])
    value = packed[me.row].astype(F32) + RESID_MUL * total
    resid[...] = value
    scale = lax.rsqrt(jnp.mean(value * value, axis=1, keepdims=True) + NORM_EPS)
    out[me.col] = (value * scale * gain[...]).astype(BF)
    gathers = gather_col_start(me, out, sems[2:6])
    finish(copies)
    gather_col_finish(me, out, sems[2:6], gathers)


def mixed_kernel(part, resid, coming, nexth, out, arrived, halves, outgoing, landing, *sems):
    me = Place()
    greet(row_partners(me) + col_partners(me) + [me.across()])
    total, copies = sum_col(me, part, halves, outgoing, landing, sems[2:6])
    nexth[...] = (resid[...] + RESID_MUL * total).astype(BF)
    over = remote(nexth, arrived, sems[6].at[0], sems[7].at[0], me.across())
    over.start()
    over.wait_recv()
    out[me.row] = jnp.where(me.section == 0, coming[...], arrived[...])
    gathers = gather_row_start(me, out, sems[0:2])
    finish(copies)
    over.wait_send()
    gather_row_finish(me, out, sems[0:2], gathers)


def last_mixed_kernel(part, resid, coming, nexth, out, halves, outgoing, landing, *sems):
    me = Place()
    greet(col_partners(me))
    total, copies = sum_col(me, part, halves, outgoing, landing, sems[0:4])
    out[me.col] = coming[...]
    gathers = gather_col_start(me, out, sems[4:8])
    nexth[...] = (resid[...] + RESID_MUL * total).astype(BF)
    finish(copies)
    gather_col_finish(me, out, sems[4:8], gathers)


def normed_back_kernel(part, resid, entry, gain, dr, dgain, out, halves, outgoing, landing, *sems):
    me = Place()
    greet(row_partners(me) + col_partners(me))
    total, copies = sum_col(me, part, halves, outgoing, landing, sems[2:6])
    value = resid[...]
    scale = lax.rsqrt(jnp.mean(value * value, axis=1, keepdims=True) + NORM_EPS)
    weighted = total * gain[...]
    inner = jnp.mean(weighted * value, axis=1, keepdims=True)
    grad = entry[...].astype(F32) + scale * weighted - value * (scale * scale * scale) * inner
    out[me.row] = (RESID_MUL * grad).astype(BF)
    gathers = gather_row_start(me, out, sems[0:2])
    dr[...] = grad
    dgain[...] = jnp.sum(total * value * scale, axis=0, keepdims=True)
    finish(copies)
    gather_row_finish(me, out, sems[0:2], gathers)


def input_back_kernel(part, dr, coming, dhin, entry, out, arrived, landing, *sems):
    me = Place()
    greet(row_partners(me) + col_partners(me) + [me.across()])
    total, copies = sum_row(me, part, landing, sems[0:2])
    dhin[...] = (total + dr[...]).astype(BF)
    over = remote(dhin, arrived, sems[6].at[0], sems[7].at[0], me.across())
    over.start()
    over.wait_recv()
    chosen = jnp.where(me.section == 0, arrived[...], coming[...])
    entry[...] = chosen
    out[me.col] = chosen
    gathers = gather_col_start(me, out, sems[2:6])
    finish(copies)
    over.wait_send()
    gather_col_finish(me, out, sems[2:6], gathers)


def last_back_kernel(part, dr, dhin, landing, *sems):
    me = Place()
    greet(row_partners(me))
    total, copies = sum_row(me, part, landing, sems[0:2])
    dhin[...] = (total + dr[...]).astype(BF)
    finish(copies)


def weights_sum_kernel(part, gains, out, gains_out, halves, outgoing, landing, g_one, g_two, g_three, *sems):
    me = Place()
    greet(row_partners(me) + col_partners(me))
    near = remote(gains, g_one, sems[6].at[0], sems[7].at[0], me.buddy())
    near.start()
    total, copies = sum_col(me, part, halves, outgoing, landing, sems[2:6])
    near.wait_recv()
    g_two[7] = gains[...] + g_one[...]
    chips = []
    for step in range(1, CHIPS):
        copy = remote(g_two.at[7], g_two.at[step - 1], sems[6].at[step], sems[7].at[step], me.chip_peer(step))
        copy.start()
        chips.append(copy)
    out[...] = total
    for copy in chips:
        copy.wait_recv()
    g_three[3] = jnp.sum(g_two[...], axis=0)
    rows = []
    for step in (1, 2, 3):
        copy = remote(g_three.at[3], g_three.at[step - 1], sems[0].at[step - 1], sems[1].at[step - 1], me.row_peer(step))
        copy.start()
        rows.append(copy)
    for copy in rows:
        copy.wait_recv()
    gains_out[...] = (g_three[3] + g_three[0]) + (g_three[1] + g_three[2])
    finish(copies + chips + rows + [near])


def call_remote(kernel, ident, outs, scratch, *args):
    return pl.pallas_call(
        kernel,
        out_shape=outs,
        in_specs=[VM] * len(args),
        out_specs=[VM] * len(outs),
        scratch_shapes=scratch,
        compiler_params=pltpu.CompilerParams(
            collective_id=ident, has_side_effects=True, vmem_limit_bytes=48 * 2**20
        ),
        cost_estimate=pl.CostEstimate(flops=10**6, bytes_accessed=40 * 10**6, transcendentals=0),
    )(*args)


def sds(shape, kind):
    return jax.ShapeDtypeStruct(shape, kind)


ACROSS = [DMA((1,)), DMA((1,))]
LAND_ROW = [pltpu.VMEM((3, TOK, D), BF)]
ARRIVED = [pltpu.VMEM((TOK, D), BF)]


def run_start(w, rg, x):
    return call_remote(
        start_kernel, 0,
        [sds((COLS,) + w.shape, BF), sds((COLS,) + rg.shape, F32), sds((ROWS, TOK, D), BF)],
        ROW_SEMS + COL_SEMS + COL_SEMS, w, rg, x,
    )


def run_attended(part, packed, gain):
    return call_remote(
        attended_kernel, 1, [sds((TOK, D), F32), sds((COLS, TOK, D), BF)],
        LAND_ROW + ROW_SEMS + COL_SEMS, part, packed, gain,
    )


def run_mixed(part, resid, coming):
    return call_remote(
        mixed_kernel, 2, [sds((TOK, D), BF), sds((ROWS, TOK, D), BF)],
        ARRIVED + sum_col_scratch(D) + ROW_SEMS + COL_SEMS + ACROSS, part, resid, coming,
    )


def run_last_mixed(part, resid, coming):
    return call_remote(
        last_mixed_kernel, 3, [sds((TOK, D), BF), sds((COLS, TOK, D), BF)],
        sum_col_scratch(D) + COL_SEMS + COL_SEMS, part, resid, coming,
    )


def run_normed_back(part, resid, entry, gain):
    return call_remote(
        normed_back_kernel, 4, [sds((TOK, D), F32), sds((1, D), F32), sds((ROWS, TOK, D), BF)],
        sum_col_scratch(D) + ROW_SEMS + COL_SEMS, part, resid, entry, gain,
    )


def run_input_back(part, dr, coming):
    return call_remote(
        input_back_kernel, 5, [sds((TOK, D), BF), sds((TOK, D), BF), sds((COLS, TOK, D), BF)],
        ARRIVED + LAND_ROW + ROW_SEMS + COL_SEMS + ACROSS, part, dr, coming,
    )


def run_last_back(part, dr):
    return call_remote(last_back_kernel, 6, [sds((TOK, D), BF)], LAND_ROW + ROW_SEMS, part, dr)[0]


def run_weights_sum(part, gains):
    width = part.shape[-1]
    return call_remote(
        weights_sum_kernel, 7, [sds((TOK, width), F32), sds((2, D), F32)],
        sum_col_scratch(width)
        + [pltpu.VMEM((2, D), F32), pltpu.VMEM((8, 2, D), F32), pltpu.VMEM((4, 2, D), F32)]
        + ROW_SEMS + COL_SEMS + [DMA((8,)), DMA((8,))],
        part, gains,
    )


def swap_halves(value):
    width = value.shape[1]
    lane = lax.broadcasted_iota(jnp.int32, value.shape, 1)
    low = lax.rem(lane, HEAD) < HEAD // 2
    up = pltpu.roll(value, HEAD // 2, axis=1)
    down = pltpu.roll(value, width - HEAD // 2, axis=1)
    return low, up, down


def rope(value, cosine, sine):
    low, up, down = swap_halves(value)
    return value * cosine + jnp.where(low, -down, up) * sine


def rope_back(value, cosine, sine):
    low, up, down = swap_halves(value * sine)
    return value * cosine + jnp.where(low, down, -up)


def allowed_mask(seg, seg_t):
    shape = (PACK, PACK)
    query = lax.broadcasted_iota(jnp.int32, shape, 0)
    key = lax.broadcasted_iota(jnp.int32, shape, 1)
    return (seg[...] == seg_t[...]) & (key <= query)


def probabilities(q, k, allowed):
    scores = jnp.where(allowed, dot_cols(q, k) * SCORE_MUL, -1e30)
    weights = jnp.exp(scores - jnp.max(scores, axis=1, keepdims=True))
    return weights / jnp.sum(weights, axis=1, keepdims=True)


def attention_kernel(x_ref, w, gain, cosine, sine, seg, seg_t, part, n1, q_out, kv_out, o_out):
    x = x_ref[...].astype(F32)
    scale = lax.rsqrt(jnp.mean(x * x, axis=1, keepdims=True) + NORM_EPS)
    normed = (x * scale * gain[...]).astype(BF)
    n1[...] = normed
    cos, sin = cosine[...], sine[...]
    pre = dot(normed, w[:, 0:512])
    q = jnp.concatenate(
        [rope(pre[:, 0:128], cos, sin), rope(pre[:, 128:256], cos, sin)], axis=1
    ).astype(BF)
    k = rope(pre[:, 256:384], cos, sin).astype(BF)
    v = pre[:, 384:512].astype(BF)
    q_out[...] = q
    kv_out[:, 0:128] = k
    kv_out[:, 128:256] = v
    allowed = allowed_mask(seg, seg_t)
    heads = []
    for head in range(4):
        at = (head // 2) * HEAD
        prob = probabilities(q[:, head * HEAD:(head + 1) * HEAD], k[:, at:at + HEAD], allowed)
        heads.append(dot(prob.astype(BF), v[:, at:at + HEAD]))
    mixed = jnp.concatenate(heads, axis=1).astype(BF)
    o_out[...] = mixed
    part[...] = dot_cols(mixed, w[:, 512:768]).astype(BF)


def attention_back_kernel(
    da, x_ref, w, gain, cosine, sine, seg, seg_t, q_ref, kv_ref, part, dp_out, dgain
):
    cos, sin = cosine[...], sine[...]
    do = dot(da[...], w[:, 512:768]).astype(BF)
    q = q_ref[...]
    kv = kv_ref[...]
    allowed = allowed_mask(seg, seg_t)
    dqs, dks, dvs = [], [None, None], [None, None]
    for head in range(4):
        group = head // 2
        at = group * HEAD
        qh = q[:, head * HEAD:(head + 1) * HEAD]
        kh = kv[:, at:at + HEAD]
        vh = kv[:, 128 + at:128 + at + HEAD]
        doh = do[:, head * HEAD:(head + 1) * HEAD]
        prob = probabilities(qh, kh, allowed)
        dv = dot_rows(prob.astype(BF), doh)
        dprob = dot_cols(doh, vh)
        ds = (prob * (dprob - jnp.sum(prob * dprob, axis=1, keepdims=True))).astype(BF)
        dqs.append(dot(ds, kh) * SCORE_MUL)
        dk = dot_rows(ds, qh) * SCORE_MUL
        dks[group] = dk if dks[group] is None else dks[group] + dk
        dvs[group] = dv if dvs[group] is None else dvs[group] + dv
    dp = jnp.concatenate(
        [
            rope_back(jnp.concatenate(dqs[0:2], axis=1), cos, sin),
            rope_back(jnp.concatenate(dqs[2:4], axis=1), cos, sin),
            rope_back(jnp.concatenate(dks, axis=1), cos, sin),
            jnp.concatenate(dvs, axis=1),
        ],
        axis=1,
    ).astype(BF)
    dp_out[...] = dp
    dn1 = dot_cols(dp, w[:, 0:512])
    x = x_ref[...].astype(F32)
    scale = lax.rsqrt(jnp.mean(x * x, axis=1, keepdims=True) + NORM_EPS)
    dgain[...] = jnp.sum(dn1 * x * scale, axis=0, keepdims=True)
    weighted = dn1 * gain[...]
    inner = jnp.mean(weighted * x, axis=1, keepdims=True)
    part[...] = (scale * weighted - x * (scale * scale * scale) * inner).astype(BF)


def place_rows(table, rows, out):
    for quad in range(QUADS):
        out[quad * 96:(quad + 1) * 96, :] = dot(
            table[0, quad], rows[quad * 256:(quad + 1) * 256, :]
        ).astype(out.dtype)


def return_rows(table, rows, acc, out):
    expert = pl.program_id(0)
    for quad in range(QUADS):
        span = pl.ds(quad * 256, 256)
        value = dot_rows(table[0, quad], rows[quad * 96:(quad + 1) * 96, :])

        @pl.when(expert == 0)
        def _():
            acc[span, :] = value

        @pl.when(expert == 1)
        def _():
            out[span, :] = (acc[span, :] + value).astype(BF)


def experts_kernel(rows, table, gslot, wg, wu, wd, part, xs, g_out, u_out, acc):
    place_rows(table, rows, xs.at[0])
    x = xs[0]
    g = dot(x, wg[0])
    u = dot(x, wu[0])
    g_out[0] = g
    u_out[0] = u
    z = (g * jax.nn.sigmoid(g) * u).astype(BF)
    y = dot(z, wd[0]).astype(BF).astype(F32)
    y = (y * gslot[0]).astype(BF)
    return_rows(table, y, acc, part)


def experts_back_kernel(
    rows, table, gslot, g_ref, u_ref, wg, wu, wd, part, dy_out, dg_out, du_out, z_out, acc, dy_raw
):
    place_rows(table, rows, dy_raw)
    dy = ((RESID_MUL * gslot[0]) * dy_raw[...]).astype(BF)
    dy_out[0] = dy
    dz = dot_cols(dy, wd[0])
    g, u = g_ref[0], u_ref[0]
    sig = jax.nn.sigmoid(g)
    silu = g * sig
    z_out[0] = (silu * u).astype(BF)
    dg = (dz * u * sig * (1.0 + g * (1.0 - sig))).astype(BF)
    du = (dz * silu).astype(BF)
    dg_out[0] = dg
    du_out[0] = du
    dx = (dot_cols(dg, wg[0]) + dot_cols(du, wu[0])).astype(BF)
    return_rows(table, dx, acc, part)


def expert_weights_kernel(xa, xb, ga, gb, ua, ub, za, zb, ya, yb, out):
    for j in range(ROWS):
        span = slice(j * 256, (j + 1) * 256)
        left_a, left_b = xa[0, :, span], xb[0, :, span]
        out[j, 0, 0] = (dot_rows(left_a, ga[0]) + dot_rows(left_b, gb[0])).astype(BF)
        out[j, 1, 0] = (dot_rows(left_a, ua[0]) + dot_rows(left_b, ub[0])).astype(BF)
        out[j, 2, 0] = (dot_rows(ya[0, :, span], za[0]) + dot_rows(yb[0, :, span], zb[0])).astype(BF)


def attention_weights_kernel(na, nb, pa, pb, da_a, da_b, oa, ob, out):
    out[:, 0:512] = (dot_rows(na[...], pa[...]) + dot_rows(nb[...], pb[...])).astype(BF)
    out[:, 512:768] = (dot_rows(da_a[...], oa[...]) + dot_rows(da_b[...], ob[...])).astype(BF)


def call_local(kernel, outs, flops, *args):
    return pl.pallas_call(
        kernel,
        out_shape=outs,
        in_specs=[VM] * len(args),
        out_specs=[VM] * len(outs),
        compiler_params=pltpu.CompilerParams(vmem_limit_bytes=48 * 2**20),
        cost_estimate=pl.CostEstimate(flops=flops, bytes_accessed=6 * 10**6, transcendentals=0),
    )(*args)


def call_experts(kernel, outs, scratch, flops, args, whole):
    def spec(shape, constant):
        if constant:
            return pl.BlockSpec(shape, lambda e: (0,) * len(shape))
        return pl.BlockSpec((1,) + shape[1:], lambda e: (e,) + (0,) * (len(shape) - 1))

    return pl.pallas_call(
        kernel,
        grid=(2,),
        out_shape=[shape for shape, _ in outs],
        in_specs=[spec(a.shape, c) for a, c in zip(args, whole)],
        out_specs=[spec(shape.shape, c) for shape, c in outs],
        scratch_shapes=scratch,
        compiler_params=pltpu.CompilerParams(
            vmem_limit_bytes=56 * 2**20, dimension_semantics=("arbitrary",)
        ),
        cost_estimate=pl.CostEstimate(flops=flops, bytes_accessed=20 * 10**6, transcendentals=0),
    )(*args)


def run_attention(packed, w, gain, tables):
    return call_local(
        attention_kernel,
        [sds((PACK, D), BF), sds((PACK, D), BF), sds((PACK, 256), BF), sds((PACK, 256), BF), sds((PACK, 256), BF)],
        10**9, packed, w, gain, *tables,
    )


def run_attention_back(da, packed, w, gain, tables, q, kv):
    return call_local(
        attention_back_kernel,
        [sds((PACK, D), BF), sds((PACK, 512), BF), sds((1, D), F32)],
        10**9, da, packed, w, gain, *tables, q, kv,
    )


def run_experts(rows, routing, mats):
    table, gslot = routing
    ff = sds((2, SLOTS, FF), F32)
    return call_experts(
        experts_kernel,
        [(sds((D, D), BF), True), (sds((2, SLOTS, D), BF), False), (ff, False), (ff, False)],
        [pltpu.VMEM((D, D), F32)],
        4 * 10**9,
        (rows, table, gslot) + mats,
        (True, False, False, False, False, False),
    )


def run_experts_back(rows, routing, g, u, mats):
    table, gslot = routing
    ff = sds((2, SLOTS, FF), BF)
    return call_experts(
        experts_back_kernel,
        [(sds((D, D), BF), True), (sds((2, SLOTS, D), BF), False), (ff, False), (ff, False), (ff, False)],
        [pltpu.VMEM((D, D), F32), pltpu.VMEM((SLOTS, D), F32)],
        4 * 10**9,
        (rows, table, gslot, g, u) + mats,
        (True,) + (False,) * 7,
    )


def run_expert_weights(*pairs):
    args = [item for pair in pairs for item in pair]
    out = sds((ROWS, 3, 2, 256, FF), BF)

    def spec(shape):
        return pl.BlockSpec((1,) + shape[1:], lambda e: (e, 0, 0))

    return pl.pallas_call(
        expert_weights_kernel,
        grid=(2,),
        out_shape=out,
        in_specs=[spec(a.shape) for a in args],
        out_specs=pl.BlockSpec((ROWS, 3, 1, 256, FF), lambda e: (0, 0, e, 0, 0)),
        compiler_params=pltpu.CompilerParams(
            vmem_limit_bytes=56 * 2**20, dimension_semantics=("arbitrary",)
        ),
        cost_estimate=pl.CostEstimate(flops=5 * 10**9, bytes_accessed=20 * 10**6, transcendentals=0),
    )(*args)


def layout_tables(length_row):
    ends_at = jnp.cumsum(length_row)
    places = jnp.arange(PACK, dtype=jnp.int32)
    passed = places[:, None] >= ends_at[None, :]
    segment = jnp.sum(passed.astype(jnp.int32), axis=1)
    starts = jnp.sum(jnp.where(passed, length_row[None, :], 0), axis=1)
    offset = (places - starts).astype(F32)
    frequency = ROPE_THETA ** (-(jnp.arange(HEAD // 2, dtype=F32) * 2.0 / HEAD))
    angles = offset[:, None] * frequency[None, :]
    cosine = jnp.tile(jnp.cos(angles), (1, 4))
    sine = jnp.tile(jnp.sin(angles), (1, 4))
    return (cosine, sine, segment[:, None], segment[None, :])


def routing_tables(route_all, gate_all, col):
    mine = col * 2 + jnp.arange(2, dtype=jnp.int32)
    same = route_all[None] == mine[:, None, None, None]
    chosen = jnp.any(same, axis=3)
    gate = jnp.sum(jnp.where(same, gate_all[None], 0.0), axis=3)
    before = (jnp.arange(TOK)[:, None] < jnp.arange(TOK)[None, :]).astype(BF)
    rank = jnp.einsum("est,tu->esu", chosen.astype(BF), before, preferred_element_type=F32)
    slot = jnp.where(chosen, rank, -1.0)
    onehot = slot[:, :, None, :] == jnp.arange(CAP, dtype=F32)[None, None, :, None]
    gslot = jnp.sum(jnp.where(onehot, gate[:, :, None, :], 0.0), axis=3)
    blocks = onehot.reshape(2, QUADS, 4, CAP, 1, TOK)
    diagonal = jnp.eye(4, dtype=jnp.bool_).reshape(1, 1, 4, 1, 4, 1)
    table = (blocks & diagonal).astype(BF).reshape(2, QUADS, 4 * CAP, 4 * TOK)
    return (table, gslot.reshape(2, SLOTS, 1))


def per_device(
    ends_in, q_weight, key_projection, value_projection, out_weight, attn_gain, moe_gain,
    gate_weight, up_weight, down_weight, routes, gates, lengths,
):
    section = lax.axis_index("section")
    col = lax.axis_index("col")
    ends = ends_in[0, :, 0]
    own = jnp.concatenate([q_weight[0], key_projection[0], value_projection[0], out_weight[0]], axis=1)
    mine = jnp.concatenate([routes[0, :, 0].astype(F32).reshape(8, 128), gates[0, :, 0].reshape(8, 128)], axis=0)
    weights, shared, packed0 = run_start(own, mine, ends[0])
    weights = weights.reshape(D, 768)
    route_all = shared[:, 0:8].reshape(COLS, 2, TOK, 8).astype(jnp.int32)
    gate_all = shared[:, 8:16].reshape(COLS, 2, TOK, 8)
    mats = (gate_weight[0], up_weight[0], down_weight[0])
    attn_row, moe_row = attn_gain, moe_gain
    layouts, routings = [], []
    for micro in (section, 1 - section):
        layouts.append(layout_tables(lax.dynamic_index_in_dim(lengths[:, 0], micro, 0, keepdims=False)))
        routings.append(
            routing_tables(
                lax.dynamic_index_in_dim(route_all, micro, 1, keepdims=False),
                lax.dynamic_index_in_dim(gate_all, micro, 1, keepdims=False),
                col,
            )
        )

    kept, forward_rows = [], []
    packed = packed0
    grad_all = None
    for step in range(3):
        which = step % 2
        flat = packed.reshape(PACK, D)
        part, n1, q, kv, mixed = run_attention(flat, weights, attn_row, layouts[which])
        resid, rows = run_attended(part.reshape(ROWS, TOK, D), packed, moe_row)
        part, xs, g, u = run_experts(rows.reshape(D, D), routings[which], mats)
        part = part.reshape(COLS, TOK, D)
        kept.append((flat, n1, q, kv, mixed, resid, xs, g, u))
        if step < 2:
            nexth, packed = run_mixed(part, resid, ends[1 - step])
        else:
            nexth, grad_all = run_last_mixed(part, resid, ends[0])
        forward_rows.append(nexth)

    entry = ends[0]
    backward_rows, pieces, moe_gains, attn_gains = [], [], [], []
    for step in range(3):
        which = (step + 1) % 2
        flat, n1, q, kv, mixed, resid, xs, g, u = kept[1 + step % 2]
        part, dy, dg, du, z = run_experts_back(grad_all.reshape(D, D), routings[which], g, u, mats)
        if step > 0:
            pieces.append((xs, dg, du, z, dy))
        if step == 2:
            expert_part = run_expert_weights(*zip(*pieces))
            expert_sum = lax.psum_scatter(expert_part, "row", scatter_dimension=0, tiled=True)
        dr, dgain, da = run_normed_back(part.reshape(COLS, TOK, D), resid, entry, moe_row)
        da = da.reshape(PACK, D)
        part, dp, again = run_attention_back(da, flat, weights, attn_row, layouts[which], q, kv)
        part = part.reshape(ROWS, TOK, D)
        if step > 0:
            moe_gains.append(dgain)
            attn_gains.append(again)
            pieces[-1] = pieces[-1] + (n1, dp, da, mixed)
        if step < 2:
            dhin, entry, grad_all = run_input_back(part, dr, ends[1 - step])
        else:
            dhin = run_last_back(part, dr)
        backward_rows.append(dhin)

    first, second = pieces[0][5:], pieces[1][5:]
    attn_part = call_local(
        attention_weights_kernel, [sds((D, 768), BF)], 10**9,
        *[item for pair in zip(first, second) for item in pair],
    )[0]
    gains = jnp.concatenate([attn_gains[0] + attn_gains[1], moe_gains[0] + moe_gains[1]], axis=0)
    attn_sum, gain_sum = run_weights_sum(attn_part.reshape(COLS, TOK, 768), gains)
    on_first = section == 0
    ends_out = jnp.stack(
        [jnp.where(on_first, backward_rows[m + 1], forward_rows[m + 1]) for m in range(2)], axis=0
    )[None, :, None]
    expert_sum = expert_sum[0].astype(F32)
    return (
        ends_out,
        attn_sum[None, :, 0:256],
        attn_sum[None, :, 256:384],
        attn_sum[None, :, 384:512],
        attn_sum[None, :, 512:768],
        gain_sum[0:1],
        gain_sum[1:2],
        expert_sum[0][None],
        expert_sum[1][None],
        jnp.swapaxes(expert_sum[2], 1, 2)[None],
    )


def solution(mesh):
    tokens = P("section", None, "col", "row", None)
    mats = P("section", "col", "row")
    gain = P("section", None)
    experts = P("section", "col", None, None)
    by_row = P("section", "col", "row", None)
    return jax.shard_map(
        per_device,
        mesh=mesh,
        in_specs=(tokens, mats, mats, mats, mats, gain, gain, experts, experts, experts, tokens, tokens, P(None, "col", None)),
        out_specs=(tokens, mats, mats, mats, mats, gain, gain, by_row, by_row, P("section", "col", None, "row")),
        check_vma=False,
    )
```

```python
import functools

import jax
import jax.numpy as jnp
from jax import lax
from jax.experimental import pallas as pl
from jax.experimental.pallas import tpu as pltpu
from jax.sharding import PartitionSpec as P

D = 1024
FF = 512
HEAD = 64
TOK = 64
ROWS = 4
COLS = 16
CHIPS = 8
CAP = 24
PACK = 256
SLOTS = COLS * CAP
QUADS = 4

SCORE_MUL = 0.015625
RESID_MUL = 0.22
NORM_EPS = 1e-06
ROPE_THETA = 10000.0
MESH = pl.DeviceIdType.MESH
BF = jnp.bfloat16
F32 = jnp.float32
VM = pl.BlockSpec(memory_space=pltpu.VMEM)
DMA = pltpu.SemaphoreType.DMA


def dot(a, b):
    return jnp.dot(a, b, preferred_element_type=F32)


def dot_rows(a, b):
    return lax.dot_general(a, b, (((0,), (0,)), ((), ())), preferred_element_type=F32)


def dot_cols(a, b):
    return lax.dot_general(a, b, (((1,), (1,)), ((), ())), preferred_element_type=F32)


class Place:
    def __init__(self):
        self.section = lax.axis_index("section")
        self.row = lax.axis_index("row")
        self.col = lax.axis_index("col")
        self.high = self.col // 8
        self.deep = lax.rem(self.col // 2, 4)
        self.core = lax.rem(self.col, 2)

    def row_at(self, step):
        return lax.rem(self.row + step + ROWS, ROWS)

    def row_peer(self, step):
        return (self.section, self.row_at(step), self.col)

    def at(self, high, deep, core=0):
        high = lax.rem(self.high + high, 2)
        deep = lax.rem(self.deep + deep + 4, 4)
        return high * 8 + deep * 2 + lax.rem(self.core + core, 2)

    def peer(self, high, deep, core=0):
        return (self.section, self.row, self.at(high, deep, core))

    def across(self):
        return (1 - self.section, self.row, self.col)


def greet(partners):
    barrier = pltpu.get_barrier_semaphore()
    for partner in partners:
        pl.semaphore_signal(barrier, inc=1, device_id=partner, device_id_type=MESH)
    pl.semaphore_wait(barrier, len(partners))


def remote(src, dst, sems, index, device):
    return pltpu.make_async_remote_copy(
        src_ref=src, dst_ref=dst, send_sem=sems[0].at[index], recv_sem=sems[1].at[index],
        device_id=device, device_id_type=MESH,
    )


def send(src, dst, sems, index, device):
    copy = remote(src, dst, sems, index, device)
    copy.start()
    return copy


def finish(copies):
    for copy in copies:
        copy.wait_send()


def row_partners(me):
    return [me.row_peer(step) for step in (1, 2, 3)]


def col_partners(me):
    return [me.peer(0, 1), me.peer(0, 2), me.peer(0, 3), me.peer(1, 0), me.peer(0, 0, 1)]


def all_chip_partners(me):
    return [me.peer(high, deep) for high in range(2) for deep in range(4) if high or deep]


ROW_SEMS = [DMA((3,)), DMA((3,))]
COL_SEMS = [DMA((7,)), DMA((7,)), DMA((8,)), DMA((8,))]
NEAR = ((1, 0), (3, 1), (2, 2))


def weave(*chains):
    chains = list(chains)
    while chains:
        chains = [chain for chain in chains if next(chain, "end") != "end"]


def gather_row(me, out, sems):
    copies = []
    for step in (2, 1, 3):
        copies.append(send(out.at[me.row], out.at[me.row], sems, step - 1, me.row_peer(step)))
    yield
    for step in (1, 3, 2):
        origin = me.row_at(-step)
        remote(out.at[origin], out.at[origin], sems, step - 1, me.row_peer(step)).wait_recv()
    finish(copies)


def gather_col(me, out, sems):
    main, side = sems[0:2], sems[2:4]
    own = out.at[me.col]
    copies = [send(own, own, main, 3, me.peer(1, 0))]
    for deep, index in NEAR:
        copies.append(send(own, own, main, index, me.peer(0, deep)))
    copies.append(send(own, own, side, 0, me.peer(0, 0, 1)))
    yield
    far = out.at[me.at(1, 0)]
    remote(far, far, main, 3, me.peer(1, 0)).wait_recv()
    for deep, index in NEAR:
        copies.append(send(far, far, main, 4 + index, me.peer(0, deep)))
    copies.append(send(far, far, side, 4, me.peer(0, 0, 1)))
    yield
    for high in range(2):
        for deep, index in NEAR:
            block = out.at[me.at(high, -deep)]
            remote(block, block, main, 4 * high + index, me.peer(0, deep)).wait_recv()
            copies.append(send(block, block, side, 4 * high + 1 + index, me.peer(0, 0, 1)))
    yield
    for high in range(2):
        for deep, index in ((0, -1),) + NEAR:
            block = out.at[me.at(high, -deep, 1)]
            remote(block, block, side, 4 * high + 1 + index, me.peer(0, 0, 1)).wait_recv()
    finish(copies)


def sum_row(me, part, landing, sems, done):
    copies = []
    for step in (2, 1, 3):
        copies.append(send(part.at[me.row_at(step)], landing.at[step - 1], sems, step - 1, me.row_peer(step)))
    yield
    total = part[me.row].astype(F32)
    for copy, step in zip(copies[1:] + copies[:1], (1, 3, 2)):
        copy.wait_recv()
        total = total + landing[step - 1].astype(F32)
    yield from done(total)
    finish(copies)


def sum_col(me, part, halves, outgoing, landing, sems, done):
    main, side = sems[0:2], sems[2:4]
    order = [(high, deep) for high in (1, 0) for deep in (2, 1, 3, 0)]
    first = {}
    for high, deep in order:
        index = 4 * high + deep
        first[index] = send(part.at[me.at(high, deep, 1)], halves.at[index], side, index, me.peer(0, 0, 1))
    yield
    away = {}
    for high in (1, 0):
        for deep in (2, 1, 3):
            index, slot = 4 * high + deep, 3 * high + deep - 1
            first[index].wait_recv()
            outgoing[slot] = (part[me.at(high, deep)].astype(F32) + halves[index].astype(F32)).astype(BF)
            away[slot] = send(outgoing.at[slot], landing.at[slot], main, slot, me.peer(0, deep))
    yield
    first[4].wait_recv()
    total = part[me.at(1, 0)].astype(F32) + halves[4].astype(F32)
    for slot in (3, 5, 4):
        away[slot].wait_recv()
        total = total + landing[slot].astype(F32)
    outgoing[6] = total.astype(BF)
    away[6] = send(outgoing.at[6], landing.at[6], main, 6, me.peer(1, 0))
    yield
    first[0].wait_recv()
    total = part[me.col].astype(F32) + halves[0].astype(F32)
    for slot in (0, 2, 1, 6):
        away[slot].wait_recv()
        total = total + landing[slot].astype(F32)
    yield from done(total)
    finish(list(first.values()) + list(away.values()))


def sum_col_scratch(width):
    return [
        pltpu.VMEM((8, TOK, width), BF),
        pltpu.VMEM((7, TOK, width), BF),
        pltpu.VMEM((7, TOK, width), BF),
    ]


def store(ref):
    def done(total):
        ref[...] = total
        yield

    return done


def after_attention(me, h_ref, gain, other, resid, out, sems):
    def done(total):
        value = h_ref[me.row].astype(F32) + RESID_MUL * total
        resid[...] = value
        scale = lax.rsqrt(jnp.mean(value * value, axis=1, keepdims=True) + NORM_EPS)
        normed = (value * scale * gain[...]).astype(BF)
        if other is not None:
            normed = jnp.where(me.section == 0, normed, other[...])
        out[me.col] = normed
        yield from gather_col(me, out, sems)

    return done


def after_experts(me, resid, coming, nexth, out, arrived, over_sems, sems):
    def done(total):
        nexth[...] = (resid[...] + RESID_MUL * total).astype(BF)
        if out is not None:
            over = send(nexth, arrived, over_sems, 0, me.across())
            yield
            over.wait_recv()
            out[me.row] = jnp.where(me.section == 0, coming[...], arrived[...])
            yield from gather_row(me, out, sems)
            over.wait_send()
        else:
            yield

    return done


def after_experts_back(me, resid, entry, gain, dr, dgain, out, sems):
    def done(total):
        value = resid[...]
        scale = lax.rsqrt(jnp.mean(value * value, axis=1, keepdims=True) + NORM_EPS)
        weighted = total * gain[...]
        inner = jnp.mean(weighted * value, axis=1, keepdims=True)
        grad = entry[...].astype(F32) + scale * weighted - value * (scale * scale * scale) * inner
        out[me.row] = (RESID_MUL * grad).astype(BF)
        gather = gather_row(me, out, sems)
        next(gather)
        dr[...] = grad
        dgain[...] = jnp.sum(total * value * scale, axis=0, keepdims=True)
        yield
        yield from gather

    return done


def after_attention_back(me, dr, coming, dhin, entry, out, arrived, over_sems, sems):
    def done(total):
        dhin[...] = (total + dr[...]).astype(BF)
        if out is not None:
            over = send(dhin, arrived, over_sems, 0, me.across())
            yield
            over.wait_recv()
            chosen = jnp.where(me.section == 0, arrived[...], coming[...])
            entry[...] = chosen
            out[me.col] = chosen
            yield from gather_col(me, out, sems)
            over.wait_send()
        else:
            yield

    return done


def start_kernel(w_ref, rg_ref, x_ref, w_out, rg_out, x_out, *sems):
    me = Place()
    greet(row_partners(me) + col_partners(me))
    w_out[me.col] = w_ref[...]
    rg_out[me.col] = rg_ref[...]
    x_out[me.row] = x_ref[...]
    weave(
        gather_col(me, w_out, sems[6:10]),
        gather_row(me, x_out, sems[0:2]),
        gather_col(me, rg_out, sems[2:6]),
    )


def first_attended_kernel(part, packed, gain, other, resid, out, landing, *sems):
    me = Place()
    greet(row_partners(me) + col_partners(me))
    done = after_attention(me, packed, gain, other, resid, out, sems[2:6])
    weave(sum_row(me, part, landing, sems[0:2], done))


def attended_kernel(part, packed, gain, resid, out, landing, *sems):
    first_attended_kernel(part, packed, gain, None, resid, out, landing, *sems)


def mixed_kernel(part, resid, coming, nexth, out, arrived, halves, outgoing, landing, *sems):
    me = Place()
    greet(row_partners(me) + col_partners(me) + [me.across()])
    done = after_experts(me, resid, coming, nexth, out, arrived, sems[6:8], sems[0:2])
    weave(sum_col(me, part, halves, outgoing, landing, sems[2:6], done))


def turn_one_kernel(
    part_f, packed, part_b, resid_b, entry, gain, resid, out, dr, dgain, da,
    landing_row, halves, outgoing, landing, *sems,
):
    me = Place()
    greet(row_partners(me) + col_partners(me))
    done_f = after_attention(me, packed, gain, None, resid, out, sems[2:6])
    done_b = after_experts_back(me, resid_b, entry, gain, dr, dgain, da, sems[6:8])
    weave(
        sum_row(me, part_f, landing_row, sems[0:2], done_f),
        sum_col(me, part_b, halves, outgoing, landing, sems[8:12], done_b),
    )


def turn_two_kernel(
    part_f, resid, part_b, dr, coming, nexth, dhin, entry, out,
    arrived, landing_row, halves, outgoing, landing, *sems,
):
    me = Place()
    greet(row_partners(me) + col_partners(me) + [me.across()])
    done_f = after_experts(me, resid, None, nexth, None, None, None, None)
    done_b = after_attention_back(me, dr, coming, dhin, entry, out, arrived, sems[12:14], sems[2:6])
    weave(
        sum_row(me, part_b, landing_row, sems[0:2], done_b),
        sum_col(me, part_f, halves, outgoing, landing, sems[8:12], done_f),
    )


def normed_back_kernel(part, resid, entry, gain, dr, dgain, out, halves, outgoing, landing, *sems):
    me = Place()
    greet(row_partners(me) + col_partners(me))
    done = after_experts_back(me, resid, entry, gain, dr, dgain, out, sems[0:2])
    weave(sum_col(me, part, halves, outgoing, landing, sems[2:6], done))


def input_back_kernel(part, dr, coming, dhin, entry, out, arrived, landing, *sems):
    me = Place()
    greet(row_partners(me) + col_partners(me) + [me.across()])
    done = after_attention_back(me, dr, coming, dhin, entry, out, arrived, sems[6:8], sems[2:6])
    weave(sum_row(me, part, landing, sems[0:2], done))


def sum_gains(me, gains, out, one, two, three, sems):
    near = send(gains, one, sems, 0, me.peer(0, 0, 1))
    yield
    near.wait_recv()
    two[0] = gains[...] + one[...]
    chips = []
    for high in range(2):
        for deep in range(4):
            if high or deep:
                index = high * 4 + deep
                chips.append(send(two.at[0], two.at[index], sems, index, me.peer(high, deep)))
    yield
    for copy in chips:
        copy.wait_recv()
    three[0] = jnp.sum(two[...], axis=0)
    rows = []
    for step in (1, 2, 3):
        rows.append(send(three.at[0], three.at[step], sems, 7 + step, me.row_peer(step)))
    yield
    for copy in rows:
        copy.wait_recv()
    out[...] = jnp.sum(three[...], axis=0)
    finish([near] + chips + rows)


def last_kernel(
    part_x, dr, part, gains, dhin, out, gains_out, landing_row, halves, outgoing, landing, one, two, three, *sems
):
    me = Place()
    greet(row_partners(me) + all_chip_partners(me) + [me.peer(0, 0, 1)])
    done = after_attention_back(me, dr, None, dhin, None, None, None, None, None)
    weave(
        sum_col(me, part, halves, outgoing, landing, sems[2:6], store(out)),
        sum_row(me, part_x, landing_row, sems[0:2], done),
        sum_gains(me, gains, gains_out, one, two, three, sems[6:8]),
    )


def call_remote(kernel, ident, outs, scratch, *args):
    return pl.pallas_call(
        kernel,
        out_shape=outs,
        in_specs=[VM] * len(args),
        out_specs=[VM] * len(outs),
        scratch_shapes=scratch,
        compiler_params=pltpu.CompilerParams(
            collective_id=ident, has_side_effects=True, vmem_limit_bytes=20 * 2**20
        ),
        cost_estimate=pl.CostEstimate(flops=10**6, bytes_accessed=40 * 10**6, transcendentals=0),
    )(*args)


def sds(shape, kind):
    return jax.ShapeDtypeStruct(shape, kind)


ACROSS = [DMA((1,)), DMA((1,))]
LAND_ROW = [pltpu.VMEM((3, TOK, D), BF)]
ARRIVED = [pltpu.VMEM((TOK, D), BF)]
TOKEN_ROWS = sds((TOK, D), BF)
TOKEN_WIDE = sds((TOK, D), F32)
ROW_BLOCKS = sds((ROWS, TOK, D), BF)
COL_BLOCKS = sds((COLS, TOK, D), BF)
GAIN = sds((1, D), F32)


def run_start(w, rg, x):
    return call_remote(
        start_kernel, 0, [sds((COLS,) + w.shape, BF), sds((COLS,) + rg.shape, F32), ROW_BLOCKS],
        ROW_SEMS + COL_SEMS + COL_SEMS, w, rg, x,
    )


def run_first_attended(part, packed, gain, other):
    return call_remote(
        first_attended_kernel, 1, [TOKEN_WIDE, COL_BLOCKS], LAND_ROW + ROW_SEMS + COL_SEMS,
        part, packed, gain, other,
    )


def run_attended(part, packed, gain):
    return call_remote(
        attended_kernel, 2, [TOKEN_WIDE, COL_BLOCKS], LAND_ROW + ROW_SEMS + COL_SEMS, part, packed, gain
    )


def run_mixed(part, resid, coming):
    return call_remote(
        mixed_kernel, 3, [TOKEN_ROWS, ROW_BLOCKS],
        ARRIVED + sum_col_scratch(D) + ROW_SEMS + COL_SEMS + ACROSS, part, resid, coming,
    )


def run_turn_one(part_f, packed, part_b, resid_b, entry, gain):
    return call_remote(
        turn_one_kernel, 4, [TOKEN_WIDE, COL_BLOCKS, TOKEN_WIDE, GAIN, ROW_BLOCKS],
        LAND_ROW + sum_col_scratch(D) + ROW_SEMS + COL_SEMS + ROW_SEMS + COL_SEMS,
        part_f, packed, part_b, resid_b, entry, gain,
    )


def run_turn_two(part_f, resid, part_b, dr, coming):
    return call_remote(
        turn_two_kernel, 5, [TOKEN_ROWS, TOKEN_ROWS, TOKEN_ROWS, COL_BLOCKS],
        ARRIVED + LAND_ROW + sum_col_scratch(D) + ROW_SEMS + COL_SEMS + ROW_SEMS + COL_SEMS + ACROSS,
        part_f, resid, part_b, dr, coming,
    )


def run_normed_back(part, resid, entry, gain):
    return call_remote(
        normed_back_kernel, 6, [TOKEN_WIDE, GAIN, ROW_BLOCKS],
        sum_col_scratch(D) + ROW_SEMS + COL_SEMS, part, resid, entry, gain,
    )


def run_input_back(part, dr, coming):
    return call_remote(
        input_back_kernel, 7, [TOKEN_ROWS, TOKEN_ROWS, COL_BLOCKS],
        ARRIVED + LAND_ROW + ROW_SEMS + COL_SEMS + ACROSS, part, dr, coming,
    )


def run_last(part_x, dr, part, gains):
    width = part.shape[-1]
    return call_remote(
        last_kernel, 8, [TOKEN_ROWS, sds((TOK, width), F32), sds((2, D), F32)],
        LAND_ROW + sum_col_scratch(width)
        + [pltpu.VMEM((2, D), F32), pltpu.VMEM((8, 2, D), F32), pltpu.VMEM((4, 2, D), F32)]
        + ROW_SEMS + COL_SEMS + [DMA((11,)), DMA((11,))],
        part_x, dr, part, gains,
    )


def swap_halves(value):
    width = value.shape[1]
    lane = lax.broadcasted_iota(jnp.int32, value.shape, 1)
    low = lax.rem(lane, HEAD) < HEAD // 2
    up = pltpu.roll(value, HEAD // 2, axis=1)
    down = pltpu.roll(value, width - HEAD // 2, axis=1)
    return low, up, down


def rope(value, cosine, sine):
    low, up, down = swap_halves(value)
    return value * cosine + jnp.where(low, -down, up) * sine


def rope_back(value, cosine, sine):
    low, up, down = swap_halves(value * sine)
    return value * cosine + jnp.where(low, down, -up)


def allowed_mask(seg, seg_t):
    shape = (PACK, PACK)
    query = lax.broadcasted_iota(jnp.int32, shape, 0)
    key = lax.broadcasted_iota(jnp.int32, shape, 1)
    return (seg[...] == seg_t[...]) & (key <= query)


def probabilities(q, k, allowed):
    scores = jnp.where(allowed, dot_cols(q, k) * SCORE_MUL, -1e30)
    weights = jnp.exp(scores - jnp.max(scores, axis=1, keepdims=True))
    return weights / jnp.sum(weights, axis=1, keepdims=True)


def attention_kernel(x_ref, w, gain, cosine, sine, seg, seg_t, part, n1, q_out, kv_out, o_out):
    x = x_ref[...].astype(F32)
    scale = lax.rsqrt(jnp.mean(x * x, axis=1, keepdims=True) + NORM_EPS)
    normed = (x * scale * gain[...]).astype(BF)
    n1[...] = normed
    cos, sin = cosine[...], sine[...]
    pre = dot(normed, w[:, 0:512])
    q = jnp.concatenate(
        [rope(pre[:, 0:128], cos, sin), rope(pre[:, 128:256], cos, sin)], axis=1
    ).astype(BF)
    k = rope(pre[:, 256:384], cos, sin).astype(BF)
    v = pre[:, 384:512].astype(BF)
    q_out[...] = q
    kv_out[:, 0:128] = k
    kv_out[:, 128:256] = v
    allowed = allowed_mask(seg, seg_t)
    heads = []
    for head in range(4):
        at = (head // 2) * HEAD
        prob = probabilities(q[:, head * HEAD:(head + 1) * HEAD], k[:, at:at + HEAD], allowed)
        heads.append(dot(prob.astype(BF), v[:, at:at + HEAD]))
    mixed = jnp.concatenate(heads, axis=1).astype(BF)
    o_out[...] = mixed
    part[...] = dot_cols(mixed, w[:, 512:768]).astype(BF)


def attention_back_kernel(
    da, x_ref, w, gain, cosine, sine, seg, seg_t, q_ref, kv_ref, part, dp_out, dgain
):
    cos, sin = cosine[...], sine[...]
    do = dot(da[...], w[:, 512:768]).astype(BF)
    q = q_ref[...]
    kv = kv_ref[...]
    allowed = allowed_mask(seg, seg_t)
    dqs, dks, dvs = [], [None, None], [None, None]
    for head in range(4):
        group = head // 2
        at = group * HEAD
        qh = q[:, head * HEAD:(head + 1) * HEAD]
        kh = kv[:, at:at + HEAD]
        vh = kv[:, 128 + at:128 + at + HEAD]
        doh = do[:, head * HEAD:(head + 1) * HEAD]
        prob = probabilities(qh, kh, allowed)
        dv = dot_rows(prob.astype(BF), doh)
        dprob = dot_cols(doh, vh)
        ds = (prob * (dprob - jnp.sum(prob * dprob, axis=1, keepdims=True))).astype(BF)
        dqs.append(dot(ds, kh) * SCORE_MUL)
        dk = dot_rows(ds, qh) * SCORE_MUL
        dks[group] = dk if dks[group] is None else dks[group] + dk
        dvs[group] = dv if dvs[group] is None else dvs[group] + dv
    dp = jnp.concatenate(
        [
            rope_back(jnp.concatenate(dqs[0:2], axis=1), cos, sin),
            rope_back(jnp.concatenate(dqs[2:4], axis=1), cos, sin),
            rope_back(jnp.concatenate(dks, axis=1), cos, sin),
            jnp.concatenate(dvs, axis=1),
        ],
        axis=1,
    ).astype(BF)
    dp_out[...] = dp
    dn1 = dot_cols(dp, w[:, 0:512])
    x = x_ref[...].astype(F32)
    scale = lax.rsqrt(jnp.mean(x * x, axis=1, keepdims=True) + NORM_EPS)
    dgain[...] = jnp.sum(dn1 * x * scale, axis=0, keepdims=True)
    weighted = dn1 * gain[...]
    inner = jnp.mean(weighted * x, axis=1, keepdims=True)
    part[...] = (scale * weighted - x * (scale * scale * scale) * inner).astype(BF)


def place_rows(table, rows, out):
    for quad in range(QUADS):
        value = dot(table[quad], rows[quad * 256:(quad + 1) * 256, :]).astype(BF)
        out[0, quad * 96:(quad + 1) * 96, :] = value[0:96]
        out[1, quad * 96:(quad + 1) * 96, :] = value[96:192]


def return_rows(table, value, out):
    for quad in range(QUADS):
        out[quad * 256:(quad + 1) * 256, :] = dot(table[quad], value[quad]).astype(BF)


def keep_rows(out, expert, value):
    for quad in range(QUADS):
        out[quad, expert * 96:(expert + 1) * 96, :] = value[quad * 96:(quad + 1) * 96]


def experts_kernel(rows, table, table_t, gslot, wg, wu, wd, part, xs, g_out, u_out, kept):
    place_rows(table, rows, xs)
    for expert in range(2):
        x = xs[expert]
        g = dot(x, wg[expert])
        u = dot(x, wu[expert])
        g_out[expert] = g
        u_out[expert] = u
        z = (g * jax.nn.sigmoid(g) * u).astype(BF)
        y = dot(z, wd[expert]).astype(BF).astype(F32)
        keep_rows(kept, expert, (y * gslot[expert]).astype(BF))
    return_rows(table_t, kept, part)


def experts_back_kernel(
    rows, table, table_t, gslot, g_ref, u_ref, wg, wu, wd, part, dy_out, dgu_out, z_out, kept
):
    place_rows(table, rows, dy_out)
    for expert in range(2):
        dy = ((RESID_MUL * gslot[expert]) * dy_out[expert].astype(F32)).astype(BF)
        dy_out[expert] = dy
        dz = dot_cols(dy, wd[expert])
        g, u = g_ref[expert], u_ref[expert]
        sig = jax.nn.sigmoid(g)
        silu = g * sig
        z_out[expert] = (silu * u).astype(BF)
        dg = (dz * u * sig * (1.0 + g * (1.0 - sig))).astype(BF)
        du = (dz * silu).astype(BF)
        dgu_out[expert, :, 0:FF] = dg
        dgu_out[expert, :, FF:2 * FF] = du
        keep_rows(kept, expert, (dot_cols(dg, wg[expert]) + dot_cols(du, wu[expert])).astype(BF))
    return_rows(table_t, kept, part)


def expert_weights_kernel(xa, xb, ga, gb, za, zb, ya, yb, gate_up, down, gate_up_buf, down_buf, sems):
    copies = []
    for j in range(ROWS):
        span = slice(j * 256, (j + 1) * 256)
        for expert in range(2):
            both = dot_rows(xa[expert, :, span], ga[expert]) + dot_rows(xb[expert, :, span], gb[expert])
            both = both.astype(BF)
            gate_up_buf[j, 0, expert] = both[:, 0:FF]
            gate_up_buf[j, 1, expert] = both[:, FF:2 * FF]
            down_buf[j, expert] = (
                dot_rows(za[expert], ya[expert, :, span]) + dot_rows(zb[expert], yb[expert, :, span])
            ).astype(BF)
        for index, (source, target) in enumerate(((gate_up_buf, gate_up), (down_buf, down))):
            copy = pltpu.make_async_copy(source.at[j], target.at[j], sems.at[2 * j + index])
            copy.start()
            copies.append(copy)
    for copy in copies:
        copy.wait()


def attention_weights_kernel(na, nb, pa, pb, da_a, da_b, oa, ob, out):
    out[:, 0:512] = (dot_rows(na[...], pa[...]) + dot_rows(nb[...], pb[...])).astype(BF)
    out[:, 512:768] = (dot_rows(da_a[...], oa[...]) + dot_rows(da_b[...], ob[...])).astype(BF)


def call_local(kernel, outs, flops, *args, scratch=(), limit=20):
    return pl.pallas_call(
        kernel,
        out_shape=outs,
        in_specs=[VM] * len(args),
        out_specs=[VM] * len(outs),
        scratch_shapes=list(scratch),
        compiler_params=pltpu.CompilerParams(vmem_limit_bytes=limit * 2**20),
        cost_estimate=pl.CostEstimate(flops=flops, bytes_accessed=6 * 10**6, transcendentals=0),
    )(*args)


def run_attention(packed, w, gain, tables):
    return call_local(
        attention_kernel,
        [sds((PACK, D), BF), sds((PACK, D), BF), sds((PACK, 256), BF), sds((PACK, 256), BF), sds((PACK, 256), BF)],
        10**9, packed, w, gain, *tables,
    )


def run_attention_back(da, packed, w, gain, tables, q, kv):
    return call_local(
        attention_back_kernel,
        [sds((PACK, D), BF), sds((PACK, 512), BF), sds((1, D), F32)],
        10**9, da, packed, w, gain, *tables, q, kv,
    )


KEPT = [pltpu.VMEM((QUADS, 2 * 96, D), BF)]


def run_experts(rows, routing, mats):
    ff = sds((2, SLOTS, FF), F32)
    return call_local(
        experts_kernel, [sds((D, D), BF), sds((2, SLOTS, D), BF), ff, ff],
        4 * 10**9, rows, *routing, *mats, scratch=KEPT, limit=30,
    )


def run_experts_back(rows, routing, g, u, mats):
    wide = sds((2, SLOTS, D), BF)
    return call_local(
        experts_back_kernel, [sds((D, D), BF), wide, wide, sds((2, SLOTS, FF), BF)],
        4 * 10**9, rows, *routing, g, u, *mats, scratch=KEPT, limit=30,
    )


def run_expert_weights(*pairs):
    args = [item for pair in pairs for item in pair]
    outs = [sds((ROWS, 2, 2, 256, FF), BF), sds((ROWS, 2, FF, 256), BF)]
    return pl.pallas_call(
        expert_weights_kernel,
        out_shape=outs,
        in_specs=[VM] * len(args),
        out_specs=[pl.BlockSpec(memory_space=pl.ANY)] * 2,
        scratch_shapes=[pltpu.VMEM(item.shape, BF) for item in outs] + [DMA((2 * ROWS,))],
        compiler_params=pltpu.CompilerParams(vmem_limit_bytes=30 * 2**20),
        cost_estimate=pl.CostEstimate(flops=5 * 10**9, bytes_accessed=20 * 10**6, transcendentals=0),
    )(*args)


def layout_tables(length_row):
    ends_at = jnp.cumsum(length_row)
    places = jnp.arange(PACK, dtype=jnp.int32)
    passed = places[:, None] >= ends_at[None, :]
    segment = jnp.sum(passed.astype(jnp.int32), axis=1)
    starts = jnp.sum(jnp.where(passed, length_row[None, :], 0), axis=1)
    offset = (places - starts).astype(F32)
    frequency = ROPE_THETA ** (-(jnp.arange(HEAD // 2, dtype=F32) * 2.0 / HEAD))
    angles = offset[:, None] * frequency[None, :]
    cosine = jnp.tile(jnp.cos(angles), (1, 4))
    sine = jnp.tile(jnp.sin(angles), (1, 4))
    return (cosine, sine, segment[:, None], segment[None, :])


def routing_tables(route_all, gate_all, col):
    mine = col * 2 + jnp.arange(2, dtype=jnp.int32)
    same = route_all[None] == mine[:, None, None, None]
    chosen = jnp.any(same, axis=3)
    gate = jnp.sum(jnp.where(same, gate_all[None], 0.0), axis=3)
    before = (jnp.arange(TOK)[:, None] < jnp.arange(TOK)[None, :]).astype(BF)
    rank = jnp.einsum("est,tu->esu", chosen.astype(BF), before, preferred_element_type=F32)
    slot = jnp.where(chosen, rank, -1.0)
    onehot = slot[:, :, None, :] == jnp.arange(CAP, dtype=F32)[None, None, :, None]
    gslot = jnp.sum(jnp.where(onehot, gate[:, :, None, :], 0.0), axis=3)
    blocks = jnp.swapaxes(onehot.reshape(2, QUADS, 4, CAP, 1, TOK), 0, 1)
    diagonal = jnp.eye(4, dtype=jnp.bool_).reshape(1, 1, 4, 1, 4, 1)
    table = (blocks & diagonal).astype(BF).reshape(QUADS, 2 * 4 * CAP, 4 * TOK)
    return (table, jnp.swapaxes(table, 1, 2), gslot.reshape(2, SLOTS, 1))


def per_device(
    ends_in, q_weight, key_projection, value_projection, out_weight, attn_gain, moe_gain,
    gate_weight, up_weight, down_weight, routes, gates, lengths,
):
    section = lax.axis_index("section")
    col = lax.axis_index("col")
    ends = ends_in[0, :, 0]
    own = jnp.concatenate([q_weight[0], key_projection[0], value_projection[0], out_weight[0]], axis=1)
    mine = jnp.concatenate([routes[0, :, 0].astype(F32).reshape(8, 128), gates[0, :, 0].reshape(8, 128)], axis=0)
    weights, shared, packed0 = run_start(own, mine, ends[0])
    weights = weights.reshape(D, 768)
    route_all = shared[:, 0:8].reshape(COLS, 2, TOK, 8).astype(jnp.int32)
    gate_all = shared[:, 8:16].reshape(COLS, 2, TOK, 8)
    mats = (gate_weight[0], up_weight[0], down_weight[0])
    attn_row, moe_row = attn_gain, moe_gain
    layouts, routings = [], []
    for micro in (section, 1 - section):
        layouts.append(layout_tables(lax.dynamic_index_in_dim(lengths[:, 0], micro, 0, keepdims=False)))
        routings.append(
            routing_tables(
                lax.dynamic_index_in_dim(route_all, micro, 1, keepdims=False),
                lax.dynamic_index_in_dim(gate_all, micro, 1, keepdims=False),
                col,
            )
        )

    kept = {}

    def forward_attention(step, packed):
        flat = packed.reshape(PACK, D)
        part, n1, q, kv, mixed = run_attention(flat, weights, attn_row, layouts[step % 2])
        kept[step] = [flat, n1, q, kv, mixed]
        return part.reshape(ROWS, TOK, D)

    def forward_experts(step, resid, rows):
        part, xs, g, u = run_experts(rows.reshape(D, D), routings[step % 2], mats)
        kept[step] += [resid, xs, g, u]
        return part.reshape(COLS, TOK, D)

    pieces, moe_gains, attn_gains = {}, {}, {}

    def backward_experts(step, grad_all):
        flat, n1, q, kv, mixed, resid, xs, g, u = kept[1 + step % 2]
        part, dy, dgu, z = run_experts_back(grad_all.reshape(D, D), routings[(step + 1) % 2], g, u, mats)
        pieces[step] = (xs, dgu, z, dy)
        return part.reshape(COLS, TOK, D), resid

    def backward_attention(step, da):
        flat, n1, q, kv, mixed = kept[1 + step % 2][0:5]
        da = da.reshape(PACK, D)
        part, dp, attn_gains[step] = run_attention_back(
            da, flat, weights, attn_row, layouts[(step + 1) % 2], q, kv
        )
        pieces[step] += (n1, dp, da, mixed)
        return part.reshape(ROWS, TOK, D)

    def both(items):
        return [item for pair in zip(*items) for item in pair]

    part = forward_attention(0, packed0)
    resid, grad_rows = run_first_attended(part, packed0, moe_row, ends[0])
    part = forward_experts(0, resid, grad_rows)
    _, packed = run_mixed(part, resid, ends[1])

    part = forward_attention(1, packed)
    resid, rows = run_attended(part, packed, moe_row)
    part = forward_experts(1, resid, rows)
    forward_one, packed = run_mixed(part, resid, ends[0])

    part = forward_attention(2, packed)
    part_b, resid_b = backward_experts(0, grad_rows)
    resid, rows, dr, _, da = run_turn_one(part, packed, part_b, resid_b, ends[0], moe_row)
    part = forward_experts(2, resid, rows)
    part_b = backward_attention(0, da)
    forward_two, _, entry, grad_rows = run_turn_two(part, resid, part_b, dr, ends[1])

    part, resid = backward_experts(1, grad_rows)
    dr, moe_gains[1], da = run_normed_back(part, resid, entry, moe_row)
    part = backward_attention(1, da)
    backward_one, entry, grad_rows = run_input_back(part, dr, ends[0])

    part, resid = backward_experts(2, grad_rows)
    gate_up, down = run_expert_weights(*zip(pieces[1][0:4], pieces[2][0:4]))
    gate_up = lax.psum_scatter(gate_up, "row", scatter_dimension=0, tiled=True)
    down = lax.psum_scatter(down, "row", scatter_dimension=0, tiled=True)
    dr, moe_gains[2], da = run_normed_back(part, resid, entry, moe_row)
    part_x = backward_attention(2, da)
    attn_part = call_local(
        attention_weights_kernel, [sds((D, 768), BF)], 10**9, *both((pieces[1][4:], pieces[2][4:]))
    )[0]
    gains = jnp.concatenate([attn_gains[1] + attn_gains[2], moe_gains[1] + moe_gains[2]], axis=0)
    backward_two, attn_sum, gain_sum = run_last(part_x, dr, attn_part.reshape(COLS, TOK, 768), gains)
    on_first = section == 0
    ends_out = jnp.stack(
        [jnp.where(on_first, backward_one, forward_one), jnp.where(on_first, backward_two, forward_two)], axis=0
    )[None, :, None]
    gate_up = gate_up.astype(F32)
    return (
        ends_out,
        attn_sum[None, :, 0:256],
        attn_sum[None, :, 256:384],
        attn_sum[None, :, 384:512],
        attn_sum[None, :, 512:768],
        gain_sum[0:1],
        gain_sum[1:2],
        gate_up[:, 0],
        gate_up[:, 1],
        down.astype(F32),
    )


def solution(mesh):
    tokens = P("section", None, "col", "row", None)
    mats = P("section", "col", "row")
    gain = P("section", None)
    experts = P("section", "col", None, None)
    by_row = P("section", "col", "row", None)
    return jax.shard_map(
        per_device,
        mesh=mesh,
        in_specs=(tokens, mats, mats, mats, mats, gain, gain, experts, experts, experts, tokens, tokens, P(None, "col", None)),
        out_specs=(tokens, mats, mats, mats, mats, gain, gain, by_row, by_row, P("section", "col", None, "row")),
        check_vma=False,
    )
```

```python
import math
import types

import jax
import jax.numpy as jnp
from jax import lax
from jax.experimental import pallas as pl
from jax.experimental.pallas import tpu as pltpu
from jax.sharding import PartitionSpec as P

D = 1024
FF = 512
HEAD = 64
TOK = 64
ROWS = 4
COLS = 16
EXPERTS = 32
CAP = 24
PACK = 256
SLOTS = COLS * CAP
QUADS = 4

SCORE_MUL = 0.015625
RESID_MUL = 0.22
NORM_EPS = 1e-06
ROPE_THETA = 10000.0
MESH = pl.DeviceIdType.MESH
BF = jnp.bfloat16
F32 = jnp.float32
VM = pl.BlockSpec(memory_space=pltpu.VMEM)
DMA = pltpu.SemaphoreType.DMA


def dot(a, b):
    return jnp.dot(a, b, preferred_element_type=F32)


def dot_rows(a, b):
    return lax.dot_general(a, b, (((0,), (0,)), ((), ())), preferred_element_type=F32)


def dot_cols(a, b):
    return lax.dot_general(a, b, (((1,), (1,)), ((), ())), preferred_element_type=F32)


class Place:
    def __init__(self):
        self.section = lax.axis_index("section")
        self.row = lax.axis_index("row")
        self.col = lax.axis_index("col")
        self.high = self.col // 8
        self.deep = lax.rem(self.col // 2, 4)
        self.core = lax.rem(self.col, 2)

    def row_at(self, step):
        return lax.rem(self.row + step + ROWS, ROWS)

    def row_peer(self, step):
        return (self.section, self.row_at(step), self.col)

    def at(self, high, deep, core=0):
        high = lax.rem(self.high + high, 2)
        deep = lax.rem(self.deep + deep + 4, 4)
        return high * 8 + deep * 2 + lax.rem(self.core + core, 2)

    def peer(self, high, deep, core=0):
        return (self.section, self.row, self.at(high, deep, core))

    def across(self):
        return (1 - self.section, self.row, self.col)


class Greeting:
    def __init__(self, partners):
        self.barrier = pltpu.get_barrier_semaphore()
        self.count = len(partners)
        for partner in partners:
            pl.semaphore_signal(self.barrier, inc=1, device_id=partner, device_id_type=MESH)

    def wait(self):
        pl.semaphore_wait(self.barrier, self.count)


class Sems:
    def __init__(self, sends, recvs, base=0):
        self.sends, self.recvs, self.base = sends, recvs, base

    def part(self, base):
        return Sems(self.sends, self.recvs, self.base + base)


def remote(src, dst, sems, index, device):
    return pltpu.make_async_remote_copy(
        src_ref=src, dst_ref=dst, send_sem=sems.sends.at[sems.base + index], recv_sem=sems.recvs.at[sems.base + index],
        device_id=device, device_id_type=MESH,
    )


def send(src, dst, sems, index, device):
    copy = remote(src, dst, sems, index, device)
    copy.start()
    return copy


def finish(copies):
    for copy in copies:
        copy.wait_send()


def row_partners(me):
    return [me.row_peer(step) for step in (1, 2, 3)]


def col_partners(me):
    return [me.peer(0, 1), me.peer(0, 2), me.peer(0, 3), me.peer(1, 0), me.peer(0, 0, 1)]


def all_chip_partners(me):
    return [me.peer(high, deep) for high in range(2) for deep in range(4) if high or deep]


CUTS = ((0, 32, True), (32, 32, False))
PARTS = len(CUTS)
ROW_SEMS = [DMA((3 * PARTS,))] * 2
COL_SEMS = [DMA((7 * PARTS,))] * 2 + [DMA((8 * PARTS,))] * 2
NEAR = ((1, 0), (3, 1), (2, 2))


class Cut:
    def __init__(self, index):
        low, rows, self.z_first = CUTS[index]
        self.index = index
        self.span = pl.ds(low, rows)
        self.first = index == 0

    def row(self, sems):
        return Sems(sems[0], sems[1], 3 * self.index)

    def col(self, sems):
        return Sems(sems[0], sems[1], 7 * self.index), Sems(sems[2], sems[3], 8 * self.index)

    def one(self, sems):
        return Sems(sems[0], sems[1], self.index)


ALL_CUTS = [Cut(index) for index in range(PARTS)]


def weave(*chains):
    chains = list(chains)
    while chains:
        chains = [chain for chain in chains if next(chain, "end") != "end"]


def gather_row(me, out, cut, sems):
    sems = cut.row(sems)
    own = out.at[me.row, cut.span]
    copies = []
    for step in (2, 1, 3):
        copies.append(send(own, own, sems, step - 1, me.row_peer(step)))
    yield
    for step in (1, 3, 2):
        block = out.at[me.row_at(-step), cut.span]
        remote(block, block, sems, step - 1, me.row_peer(step)).wait_recv()
    finish(copies)


def gather_col(me, out, cut, sems):
    main, side = cut.col(sems)
    over, near = me.peer(1, 0), me.peer(0, 0, 1)
    own = out.at[me.col, cut.span]
    copies = []
    if cut.z_first:
        for deep, index in NEAR:
            copies.append(send(own, own, main, index, me.peer(0, deep)))
        copies.append(send(own, own, main, 3, over))
    else:
        copies.append(send(own, own, main, 3, over))
        for deep, index in NEAR:
            copies.append(send(own, own, main, index, me.peer(0, deep)))
    copies.append(send(own, own, side, 0, near))
    yield
    if cut.z_first:
        for deep, index in NEAR:
            block = out.at[me.at(0, -deep), cut.span]
            remote(block, block, main, index, over).wait_recv()
            copies.append(send(block, block, main, 4 + index, over))
            copies.append(send(block, block, side, 1 + index, near))
        yield
    far = out.at[me.at(1, 0), cut.span]
    remote(far, far, main, 3, over).wait_recv()
    if not cut.z_first:
        for deep, index in NEAR:
            copies.append(send(far, far, main, 4 + index, me.peer(0, deep)))
    copies.append(send(far, far, side, 4, near))
    yield
    for high in range(2):
        if high == 0 and cut.z_first:
            continue
        for deep, index in NEAR:
            block = out.at[me.at(high, -deep), cut.span]
            remote(block, block, main, 4 * high + index, over).wait_recv()
            copies.append(send(block, block, side, 4 * high + 1 + index, near))
    yield
    for high in range(2):
        for deep, index in ((0, -1),) + NEAR:
            block = out.at[me.at(high, -deep, 1), cut.span]
            remote(block, block, side, 4 * high + 1 + index, near).wait_recv()
    finish(copies)


def sum_row(me, part, landing, cut, sems, done):
    sems = cut.row(sems)
    copies = []
    for step in (2, 1, 3):
        copies.append(
            send(part.at[me.row_at(step), cut.span], landing.at[step - 1, cut.span], sems, step - 1, me.row_peer(step))
        )
    yield
    total = part[me.row, cut.span].astype(F32)
    for copy, step in zip(copies[1:] + copies[:1], (1, 3, 2)):
        copy.wait_recv()
        total = total + landing[step - 1, cut.span].astype(F32)
    yield from done(total, cut)
    finish(copies)


def sum_col(me, part, halves, outgoing, landing, cut, sems, done):
    main, side = cut.col(sems)
    over, near, span = me.peer(1, 0), me.peer(0, 0, 1), cut.span
    first, away = {}, {}
    for high in (1, 0):
        for deep in (2, 1, 3, 0):
            index = 4 * high + deep
            first[index] = send(part.at[me.at(high, deep, 1), span], halves.at[index, span], side, index, near)

    def pair(high, deep):
        index = 4 * high + deep
        first[index].wait_recv()
        return part[me.at(high, deep), span].astype(F32) + halves[index, span].astype(F32)

    def pass_on(slot, value, device):
        outgoing[slot, span] = value.astype(BF)
        away[slot] = send(outgoing.at[slot, span], landing.at[slot, span], main, slot, device)

    def landed(slot):
        away[slot].wait_recv()
        return landing[slot, span].astype(F32)

    yield
    if cut.z_first:
        for high in (1, 0):
            for deep in (2, 1, 3):
                pass_on(3 * high + deep - 1, pair(high, deep), me.peer(0, deep))
        yield
        total = pair(1, 0)
        for slot in (3, 5, 4):
            total = total + landed(slot)
        pass_on(6, total, over)
        yield
        total = pair(0, 0)
        for slot in (0, 2, 1, 6):
            total = total + landed(slot)
    else:
        for deep in (2, 1, 3, 0):
            pass_on(deep, pair(1, deep), over)
        yield
        for deep in (2, 1, 3):
            pass_on(3 + deep, pair(0, deep) + landed(deep), me.peer(0, deep))
        yield
        total = pair(0, 0) + landed(0)
        for slot in (4, 6, 5):
            total = total + landed(slot)
    yield from done(total, cut)
    finish(list(first.values()) + list(away.values()))


def sum_col_scratch(width):
    return dict(
        halves=pltpu.VMEM((8, TOK, width), BF),
        outgoing=pltpu.VMEM((7, TOK, width), BF),
        landing=pltpu.VMEM((7, TOK, width), BF),
    )


def store(ref):
    def done(total, cut):
        ref[cut.span, :] = total
        yield

    return done


def after_attention(me, h_ref, gain, other, resid, out, sems):
    def done(total, cut):
        span = cut.span
        value = h_ref[me.row, span].astype(F32) + RESID_MUL * total
        resid[span, :] = value
        scale = lax.rsqrt(jnp.mean(value * value, axis=1, keepdims=True) + NORM_EPS)
        normed = (value * scale * gain[...]).astype(BF)
        if other is not None:
            normed = jnp.where(me.section == 0, normed, other[span, :])
        out[me.col, span] = normed
        yield from gather_col(me, out, cut, sems)

    return done


def after_experts(me, resid, coming, nexth, out, arrived, over_sems, sems):
    def done(total, cut):
        span = cut.span
        nexth[span, :] = (resid[span, :] + RESID_MUL * total).astype(BF)
        if out is not None:
            over = send(nexth.at[span], arrived.at[span], cut.one(over_sems), 0, me.across())
            yield
            over.wait_recv()
            out[me.row, span] = jnp.where(me.section == 0, coming[span, :], arrived[span, :])
            yield from gather_row(me, out, cut, sems)
            over.wait_send()
        else:
            yield

    return done


def after_experts_back(me, resid, entry, gain, dr, dgain, out, sems):
    def done(total, cut):
        span = cut.span
        value = resid[span, :]
        scale = lax.rsqrt(jnp.mean(value * value, axis=1, keepdims=True) + NORM_EPS)
        weighted = total * gain[...]
        inner = jnp.mean(weighted * value, axis=1, keepdims=True)
        grad = entry[span, :].astype(F32) + scale * weighted - value * (scale * scale * scale) * inner
        out[me.row, span] = (RESID_MUL * grad).astype(BF)
        gather = gather_row(me, out, cut, sems)
        next(gather)
        dr[span, :] = grad
        term = jnp.sum(total * value * scale, axis=0, keepdims=True)
        dgain[...] = term if cut.first else dgain[...] + term
        yield
        yield from gather

    return done


def after_attention_back(me, dr, coming, dhin, entry, out, arrived, over_sems, sems):
    def done(total, cut):
        span = cut.span
        dhin[span, :] = (total + dr[span, :]).astype(BF)
        if out is not None:
            over = send(dhin.at[span], arrived.at[span], cut.one(over_sems), 0, me.across())
            yield
            over.wait_recv()
            chosen = jnp.where(me.section == 0, arrived[span, :], coming[span, :])
            entry[span, :] = chosen
            out[me.col, span] = chosen
            yield from gather_col(me, out, cut, sems)
            over.wait_send()
        else:
            yield

    return done


def sum_gains(me, gains, out, one, two, three, sems):
    sems = Sems(*sems)
    near = send(gains, one, sems, 0, me.peer(0, 0, 1))
    yield
    near.wait_recv()
    two[0] = gains[...] + one[...]
    chips = []
    for high in range(2):
        for deep in range(4):
            if high or deep:
                index = high * 4 + deep
                chips.append(send(two.at[0], two.at[index], sems, index, me.peer(high, deep)))
    yield
    for copy in chips:
        copy.wait_recv()
    three[0] = jnp.sum(two[...], axis=0)
    rows = []
    for step in (1, 2, 3):
        rows.append(send(three.at[0], three.at[step], sems, 7 + step, me.row_peer(step)))
    yield
    for copy in rows:
        copy.wait_recv()
    out[...] = jnp.sum(three[...], axis=0)
    finish([near] + chips + rows)


def reduce_blocks(me, blocks, land, total_out, sems, make=None):
    pieces, half = blocks.shape[0], blocks.shape[2] // 2
    passing, sums, final = land
    sems = Sems(*sems)
    low, high = pl.ds(0, half), pl.ds(half, half)
    up, down = me.row_peer(1), me.row_peer(3)
    near_up, near_down, far = me.row_at(1), me.row_at(3), me.row_at(2)
    copies = []
    yield
    for piece in range(pieces):
        if make is not None:
            make(piece)
        part = sems.part(6 * piece)
        copies.append(
            [
                send(blocks.at[piece, far, low], passing.at[piece, 0], part, 0, up),
                send(blocks.at[piece, far, high], passing.at[piece, 1], part, 1, down),
                send(blocks.at[piece, near_up, high], final.at[piece, 0, high], part, 2, up),
                send(blocks.at[piece, near_down, low], final.at[piece, 1, low], part, 3, down),
            ]
        )
        yield
    for piece in range(pieces):
        part = sems.part(6 * piece)
        copies[piece][0].wait_recv()
        value = blocks[piece, near_up, low].astype(F32) + passing[piece, 0].astype(F32)
        sums[piece, 0] = value.astype(BF)
        copies[piece].append(send(sums.at[piece, 0], final.at[piece, 0, low], part, 4, up))
        copies[piece][1].wait_recv()
        value = blocks[piece, near_down, high].astype(F32) + passing[piece, 1].astype(F32)
        sums[piece, 1] = value.astype(BF)
        copies[piece].append(send(sums.at[piece, 1], final.at[piece, 1, high], part, 5, down))
    yield
    for piece in range(pieces):
        for copy in copies[piece][2:]:
            copy.wait_recv()
        total_out[piece] = (
            blocks[piece, me.row].astype(F32) + final[piece, 0].astype(F32) + final[piece, 1].astype(F32)
        )
        finish(copies[piece])


def reduce_scratch(pieces, rows, width):
    return [
        pltpu.VMEM((pieces, 2, rows // 2, width), BF),
        pltpu.VMEM((pieces, 2, rows // 2, width), BF),
        pltpu.VMEM((pieces, 2, rows, width), BF),
    ]


def sds(shape, kind):
    return jax.ShapeDtypeStruct(shape, kind)


def call_remote(body, ident, ins, outs, scratch, limit, flops=10**7):
    flat, places = [], {}
    for name, item in scratch.items():
        if isinstance(item, list):
            places[name] = (len(flat), len(item))
            flat += item
        else:
            places[name] = (len(flat), None)
            flat.append(item)
    names = list(ins) + list(outs)

    def kernel(*refs):
        given = dict(zip(names, refs))
        rest = refs[len(names):]
        for name, (start, count) in places.items():
            given[name] = rest[start] if count is None else list(rest[start:start + count])
        body(types.SimpleNamespace(**given))

    results = pl.pallas_call(
        kernel,
        out_shape=list(outs.values()),
        in_specs=[VM] * len(ins),
        out_specs=[VM] * len(outs),
        scratch_shapes=flat,
        compiler_params=pltpu.CompilerParams(
            collective_id=ident, has_side_effects=True, vmem_limit_bytes=limit * 2**20
        ),
        cost_estimate=pl.CostEstimate(flops=flops, bytes_accessed=40 * 10**6, transcendentals=0),
    )(*ins.values())
    return types.SimpleNamespace(**dict(zip(outs, results)))


TOKEN_ROWS = sds((TOK, D), BF)
TOKEN_WIDE = sds((TOK, D), F32)
ROW_BLOCKS = sds((ROWS, TOK, D), BF)
COL_BLOCKS = sds((COLS, TOK, D), BF)
GAIN = sds((1, D), F32)
HEADS = sds((PACK, 256), BF)
WIDE_SLOTS = sds((2, SLOTS, D), BF)
FF_SLOTS = sds((2, SLOTS, FF), BF)
LAND_ROW = pltpu.VMEM((3, TOK, D), BF)
ARRIVED = pltpu.VMEM((TOK, D), BF)
ACROSS = [DMA((PARTS,))] * 2
ROW_PART = pltpu.VMEM((ROWS, TOK, D), BF)
COL_PART = pltpu.VMEM((COLS, TOK, D), BF)
KEPT = pltpu.VMEM((QUADS, 2 * 96, D), BF)
ATTENTION_OUTS = dict(n1=sds((PACK, D), BF), q=HEADS, kv=HEADS, o=HEADS)
EXPERT_OUTS = dict(xs=WIDE_SLOTS, g=FF_SLOTS, u=FF_SLOTS)
BACK_OUTS = dict(dy=WIDE_SLOTS, dgu=WIDE_SLOTS, z=sds((2, SLOTS, FF), BF))
ATTENTION_BACK_OUTS = dict(dp=sds((PACK, 512), BF), again=GAIN)


def attention_body(r, slot):
    attention_kernel(
        slot, r.packed, r.w, r.attn_gain, r.cosine, r.sine, r.seg, r.seg_t, r.part_x, r.n1, r.q, r.kv, r.o
    )


def experts_body(r):
    experts_kernel(
        r.rows, r.table, r.table_t, r.gslot, r.wg, r.wu, r.wd, r.part, r.xs, r.g, r.u, r.kept
    )


def experts_back_body(r):
    experts_back_kernel(
        r.grad_rows, r.table, r.table_t, r.gslot, r.g_in, r.u_in, r.wg, r.wu, r.wd,
        r.part_b, r.dy, r.dgu, r.z, r.kept,
    )


def attention_back_body(r, slot):
    attention_back_kernel(
        slot, r.da, r.packed_b, r.w, r.attn_gain, r.cosine, r.sine, r.seg, r.seg_t, r.q_in, r.kv_in,
        r.part_y, r.dp, r.again,
    )


def run_start(w, rg, x):
    def body(r):
        me = Place()
        Greeting(row_partners(me) + col_partners(me)).wait()
        r.w_out[me.col] = r.w[...]
        r.rg_out[me.col] = r.rg[...]
        r.x_out[me.row] = r.x[...]
        weave(
            *[gather_col(me, r.w_out, cut, r.col_w) for cut in ALL_CUTS],
            *[gather_row(me, r.x_out, cut, r.row) for cut in ALL_CUTS],
            *[gather_col(me, r.rg_out, cut, r.col_rg) for cut in ALL_CUTS],
        )

    return call_remote(
        body, 0, dict(w=w, rg=rg, x=x),
        dict(w_out=sds((COLS,) + w.shape, BF), rg_out=sds((COLS,) + rg.shape, F32), x_out=ROW_BLOCKS),
        dict(row=ROW_SEMS, col_w=COL_SEMS, col_rg=COL_SEMS), 8,
    )


def run_forward_attention(ident, slot, packed, other, common):
    def body(r):
        me = Place()
        greeting = Greeting(row_partners(me) + col_partners(me))
        attention_body(r, slot)
        greeting.wait()
        done = after_attention(me, r.packed, r.moe_gain, None if other is None else r.other, r.resid, r.rows, r.col)
        weave(*[sum_row(me, r.part_x, r.landing_x, cut, r.row, done) for cut in ALL_CUTS])

    extra = {} if other is None else dict(other=other)
    return call_remote(
        body, ident, dict(packed=packed, **common, **extra),
        dict(resid=TOKEN_WIDE, rows=COL_BLOCKS, **ATTENTION_OUTS),
        dict(part_x=ROW_PART, landing_x=LAND_ROW, row=ROW_SEMS, col=COL_SEMS), 8,
    )


def run_forward_experts(ident, rows, resid, coming, expert_in):
    def body(r):
        me = Place()
        greeting = Greeting(row_partners(me) + col_partners(me) + [me.across()])
        experts_body(r)
        greeting.wait()
        done = after_experts(me, r.resid, r.coming, r.nexth, r.out, r.arrived, r.over, r.row)
        weave(*[sum_col(me, r.part, r.halves, r.outgoing, r.landing, cut, r.col, done) for cut in ALL_CUTS])

    return call_remote(
        body, ident, dict(rows=rows, resid=resid, coming=coming, **expert_in),
        dict(nexth=TOKEN_ROWS, out=ROW_BLOCKS, **EXPERT_OUTS),
        dict(part=COL_PART, kept=KEPT, arrived=ARRIVED, row=ROW_SEMS, col=COL_SEMS, over=ACROSS, **sum_col_scratch(D)),
        12, 4 * 10**9,
    )


def run_turn_one(ident, slot, packed, grad_rows, resid_b, entry, kept_f, common, expert_in):
    def body(r):
        me = Place()
        greeting = Greeting(row_partners(me) + col_partners(me))
        attention_body(r, slot)
        experts_back_body(r)
        greeting.wait()
        done_f = after_attention(me, r.packed, r.moe_gain, None, r.resid, r.rows, r.col)
        done_b = after_experts_back(me, r.resid_b, r.entry, r.moe_gain, r.dr, r.dgain, r.da, r.row_b)
        weave(
            *[sum_row(me, r.part_x, r.landing_x, cut, r.row, done_f) for cut in ALL_CUTS],
            *[sum_col(me, r.part_b, r.halves, r.outgoing, r.landing, cut, r.col_b, done_b) for cut in ALL_CUTS],
        )

    return call_remote(
        body, ident,
        dict(packed=packed, grad_rows=grad_rows, resid_b=resid_b, entry=entry, **kept_f, **common, **expert_in),
        dict(
            resid=TOKEN_WIDE, rows=COL_BLOCKS, dr=TOKEN_WIDE, dgain=GAIN, da=ROW_BLOCKS,
            **ATTENTION_OUTS, **BACK_OUTS,
        ),
        dict(
            part_x=ROW_PART, landing_x=LAND_ROW, row=ROW_SEMS, col=COL_SEMS, part_b=COL_PART, kept=KEPT,
            row_b=ROW_SEMS, col_b=COL_SEMS, **sum_col_scratch(D),
        ),
        14, 5 * 10**9,
    )


def run_turn_two(ident, slot, rows, resid, da, packed_b, dr, coming, kept_f, common, expert_in):
    def body(r):
        me = Place()
        greeting = Greeting(row_partners(me) + col_partners(me) + [me.across()])
        attention_back_body(r, slot)
        experts_body(r)
        greeting.wait()
        done_f = after_experts(me, r.resid, None, r.nexth, None, None, None, None)
        done_b = after_attention_back(me, r.dr, r.coming, r.dhin, r.entry, r.out, r.arrived, r.over, r.col)
        weave(
            *[sum_row(me, r.part_y, r.landing_x, cut, r.row, done_b) for cut in ALL_CUTS],
            *[sum_col(me, r.part, r.halves, r.outgoing, r.landing, cut, r.col_b, done_f) for cut in ALL_CUTS],
        )

    return call_remote(
        body, ident,
        dict(rows=rows, resid=resid, da=da, packed_b=packed_b, dr=dr, coming=coming, **kept_f, **common, **expert_in),
        dict(
            nexth=TOKEN_ROWS, dhin=TOKEN_ROWS, entry=TOKEN_ROWS, out=COL_BLOCKS,
            **EXPERT_OUTS, **ATTENTION_BACK_OUTS,
        ),
        dict(
            part_y=ROW_PART, landing_x=LAND_ROW, arrived=ARRIVED, row=ROW_SEMS, col=COL_SEMS, over=ACROSS,
            part=COL_PART, kept=KEPT, col_b=COL_SEMS, **sum_col_scratch(D),
        ),
        14, 5 * 10**9,
    )


def run_backward_experts(ident, grad_rows, resid, entry, kept_f, moe_gain, expert_in):
    def body(r):
        me = Place()
        greeting = Greeting(row_partners(me) + col_partners(me))
        experts_back_body(r)
        greeting.wait()
        done = after_experts_back(me, r.resid, r.entry, r.moe_gain, r.dr, r.dgain, r.da, r.row)
        weave(*[sum_col(me, r.part_b, r.halves, r.outgoing, r.landing, cut, r.col, done) for cut in ALL_CUTS])

    return call_remote(
        body, ident, dict(grad_rows=grad_rows, resid=resid, entry=entry, moe_gain=moe_gain, **kept_f, **expert_in),
        dict(dr=TOKEN_WIDE, dgain=GAIN, da=ROW_BLOCKS, **BACK_OUTS),
        dict(part_b=COL_PART, kept=KEPT, row=ROW_SEMS, col=COL_SEMS, **sum_col_scratch(D)), 14, 4 * 10**9,
    )


def run_backward_attention(ident, slot, da, packed_b, dr, coming, kept_f, common):
    def body(r):
        me = Place()
        greeting = Greeting(row_partners(me) + col_partners(me) + [me.across()])
        attention_back_body(r, slot)
        greeting.wait()
        done = after_attention_back(me, r.dr, r.coming, r.dhin, r.entry, r.out, r.arrived, r.over, r.col)
        weave(*[sum_row(me, r.part_y, r.landing_x, cut, r.row, done) for cut in ALL_CUTS])

    return call_remote(
        body, ident, dict(da=da, packed_b=packed_b, dr=dr, coming=coming, **kept_f, **common),
        dict(dhin=TOKEN_ROWS, entry=TOKEN_ROWS, out=COL_BLOCKS, **ATTENTION_BACK_OUTS),
        dict(part_y=ROW_PART, landing_x=LAND_ROW, arrived=ARRIVED, row=ROW_SEMS, col=COL_SEMS, over=ACROSS), 8,
    )


EARLY = 3


def run_last_experts(ident, grad_rows, resid, entry, kept_f, earlier, moe_gain, expert_in):
    def body(r):
        me = Place()
        greeting = Greeting(row_partners(me) + col_partners(me))
        experts_back_body(r)
        greeting.wait()
        done = after_experts_back(me, r.resid, r.entry, r.moe_gain, r.dr, r.dgain, r.da, r.row)

        def product(piece):
            kind, expert = divmod(piece, 2)
            span = slice(kind * FF, (kind + 1) * FF)
            value = dot_rows(r.xs_a[expert], r.dgu_a[expert, :, span]) + dot_rows(
                r.xs_b[expert], r.dgu[expert, :, span]
            )
            return value.astype(BF).reshape(ROWS, 256, FF)

        def make(piece):
            r.blocks[piece] = product(piece)

        def others():
            yield
            yield
            yield
            for piece in range(EARLY, 4):
                r.late[piece - EARLY] = product(piece)
            for expert in range(2):
                value = (dot_rows(r.z_a[expert], r.dy_a[expert]) + dot_rows(r.z[expert], r.dy[expert])).astype(BF)
                for row in range(ROWS):
                    r.down[expert, row] = value[:, row * 256:(row + 1) * 256]
                yield

        weave(
            *[sum_col(me, r.part_b, r.halves, r.outgoing, r.landing, cut, r.col, done) for cut in ALL_CUTS],
            reduce_blocks(me, r.blocks, r.landing_w, r.early_sum, r.big, make),
            others(),
        )

    return call_remote(
        body, ident,
        dict(grad_rows=grad_rows, resid=resid, entry=entry, moe_gain=moe_gain, **kept_f, **earlier, **expert_in),
        dict(
            dr=TOKEN_WIDE, dgain=GAIN, da=ROW_BLOCKS, early_sum=sds((EARLY, 256, FF), F32),
            late=sds((4 - EARLY, ROWS, 256, FF), BF), down=sds((2, ROWS, FF, 256), BF),
        ),
        dict(
            dy=pltpu.VMEM((2, SLOTS, D), BF), dgu=pltpu.VMEM((2, SLOTS, D), BF), z=pltpu.VMEM((2, SLOTS, FF), BF),
            blocks=pltpu.VMEM((EARLY, ROWS, 256, FF), BF), landing_w=reduce_scratch(EARLY, 256, FF),
            big=[DMA((6 * EARLY,))] * 2,
            part_b=COL_PART, kept=KEPT, row=ROW_SEMS, col=COL_SEMS, **sum_col_scratch(D),
        ),
        24, 9 * 10**9,
    )


def run_last(ident, slot, da, packed_b, dr, kept_f, late, down, weights_in, gains, common):
    late_count = late.shape[0]

    def body(r):
        me = Place()
        greeting = Greeting(row_partners(me) + all_chip_partners(me) + [me.peer(0, 0, 1)])
        greeting.wait()
        late_chain = reduce_blocks(me, r.late, r.landing_l, r.late_sum, r.big_l)
        down_chain = reduce_blocks(me, r.down, r.landing_d, r.down_sum, r.big_d)
        for _ in range(1 + late_count):
            next(late_chain)
        for _ in range(1 + 2):
            next(down_chain)
        attention_back_body(r, slot)
        attention_weights_kernel(r.n1_a, r.n1_b, r.dp_a, r.dp, r.da_a, r.da, r.o_a, r.o_b, r.weight_part)
        r.gains[0:1] = r.again_a[...] + r.again[...]
        r.gains[1:2] = r.dgain_a[...] + r.dgain_b[...]
        done = after_attention_back(me, r.dr, None, r.dhin, None, None, None, None, None)
        weave(
            *[sum_col(me, r.weight_part, r.halves, r.outgoing, r.landing, cut, r.col, store(r.weight_sum)) for cut in ALL_CUTS],
            *[sum_row(me, r.part_y, r.landing_x, cut, r.row, done) for cut in ALL_CUTS],
            sum_gains(me, r.gains, r.gain_sum, r.one, r.two, r.three, r.gain_sems),
        )
        weave(late_chain, down_chain)

    return call_remote(
        body, ident,
        dict(da=da, packed_b=packed_b, dr=dr, late=late, down=down, **kept_f, **weights_in, **gains, **common),
        dict(
            dhin=TOKEN_ROWS, weight_sum=sds((TOK, 768), F32), gain_sum=sds((2, D), F32),
            late_sum=sds((late_count, 256, FF), F32), down_sum=sds((2, FF, 256), F32),
        ),
        dict(
            part_y=ROW_PART, landing_x=LAND_ROW, dp=pltpu.VMEM((PACK, 512), BF), again=pltpu.VMEM((1, D), F32),
            weight_part=pltpu.VMEM((COLS, TOK, 768), BF), gains=pltpu.VMEM((2, D), F32),
            one=pltpu.VMEM((2, D), F32), two=pltpu.VMEM((8, 2, D), F32), three=pltpu.VMEM((4, 2, D), F32),
            landing_l=reduce_scratch(late_count, 256, FF), landing_d=reduce_scratch(2, FF, 256),
            big_l=[DMA((6 * late_count,))] * 2, big_d=[DMA((12,))] * 2, gain_sems=[DMA((11,))] * 2,
            row=ROW_SEMS, col=COL_SEMS, **sum_col_scratch(768),
        ),
        14, 2 * 10**9,
    )


def swap_halves(value):
    width = value.shape[1]
    lane = lax.broadcasted_iota(jnp.int32, value.shape, 1)
    low = lax.rem(lane, HEAD) < HEAD // 2
    up = pltpu.roll(value, HEAD // 2, axis=1)
    down = pltpu.roll(value, width - HEAD // 2, axis=1)
    return low, up, down


def rope(value, cosine, sine):
    low, up, down = swap_halves(value)
    return value * cosine + jnp.where(low, -down, up) * sine


def rope_back(value, cosine, sine):
    low, up, down = swap_halves(value * sine)
    return value * cosine + jnp.where(low, down, -up)


def allowed_mask(seg, seg_t):
    shape = (PACK, PACK)
    query = lax.broadcasted_iota(jnp.int32, shape, 0)
    key = lax.broadcasted_iota(jnp.int32, shape, 1)
    return (seg == seg_t) & (key <= query)


def probabilities(q, k, allowed):
    scores = jnp.where(allowed, dot_cols(q, k) * SCORE_MUL, -1e30)
    weights = jnp.exp(scores - jnp.max(scores, axis=1, keepdims=True))
    return weights / jnp.sum(weights, axis=1, keepdims=True)


def attention_kernel(slot, x_ref, w, gain, cosine, sine, seg, seg_t, part, n1, q_out, kv_out, o_out):
    x = x_ref[...].reshape(PACK, D).astype(F32)
    scale = lax.rsqrt(jnp.mean(x * x, axis=1, keepdims=True) + NORM_EPS)
    normed = (x * scale * gain[...]).astype(BF)
    n1[...] = normed
    cos, sin = cosine[slot], sine[slot]
    pre = dot(normed, w[:, 0:512])
    q = jnp.concatenate(
        [rope(pre[:, 0:128], cos, sin), rope(pre[:, 128:256], cos, sin)], axis=1
    ).astype(BF)
    k = rope(pre[:, 256:384], cos, sin).astype(BF)
    v = pre[:, 384:512].astype(BF)
    q_out[...] = q
    kv_out[:, 0:128] = k
    kv_out[:, 128:256] = v
    allowed = allowed_mask(seg[slot], seg_t[slot])
    heads = []
    for head in range(4):
        at = (head // 2) * HEAD
        prob = probabilities(q[:, head * HEAD:(head + 1) * HEAD], k[:, at:at + HEAD], allowed)
        heads.append(dot(prob.astype(BF), v[:, at:at + HEAD]))
    mixed = jnp.concatenate(heads, axis=1).astype(BF)
    o_out[...] = mixed
    part[...] = dot_cols(mixed, w[:, 512:768]).astype(BF).reshape(ROWS, TOK, D)


def attention_back_kernel(
    slot, da, x_ref, w, gain, cosine, sine, seg, seg_t, q_ref, kv_ref, part, dp_out, dgain
):
    cos, sin = cosine[slot], sine[slot]
    do = dot(da[...].reshape(PACK, D), w[:, 512:768]).astype(BF)
    q = q_ref[...]
    kv = kv_ref[...]
    allowed = allowed_mask(seg[slot], seg_t[slot])
    dqs, dks, dvs = [], [None, None], [None, None]
    for head in range(4):
        group = head // 2
        at = group * HEAD
        qh = q[:, head * HEAD:(head + 1) * HEAD]
        kh = kv[:, at:at + HEAD]
        vh = kv[:, 128 + at:128 + at + HEAD]
        doh = do[:, head * HEAD:(head + 1) * HEAD]
        prob = probabilities(qh, kh, allowed)
        dv = dot_rows(prob.astype(BF), doh)
        dprob = dot_cols(doh, vh)
        ds = (prob * (dprob - jnp.sum(prob * dprob, axis=1, keepdims=True))).astype(BF)
        dqs.append(dot(ds, kh) * SCORE_MUL)
        dk = dot_rows(ds, qh) * SCORE_MUL
        dks[group] = dk if dks[group] is None else dks[group] + dk
        dvs[group] = dv if dvs[group] is None else dvs[group] + dv
    dp = jnp.concatenate(
        [
            rope_back(jnp.concatenate(dqs[0:2], axis=1), cos, sin),
            rope_back(jnp.concatenate(dqs[2:4], axis=1), cos, sin),
            rope_back(jnp.concatenate(dks, axis=1), cos, sin),
            jnp.concatenate(dvs, axis=1),
        ],
        axis=1,
    ).astype(BF)
    dp_out[...] = dp
    dn1 = dot_cols(dp, w[:, 0:512])
    x = x_ref[...].reshape(PACK, D).astype(F32)
    scale = lax.rsqrt(jnp.mean(x * x, axis=1, keepdims=True) + NORM_EPS)
    dgain[...] = jnp.sum(dn1 * x * scale, axis=0, keepdims=True)
    weighted = dn1 * gain[...]
    inner = jnp.mean(weighted * x, axis=1, keepdims=True)
    part[...] = (scale * weighted - x * (scale * scale * scale) * inner).astype(BF).reshape(ROWS, TOK, D)


def place_rows(table, rows, out):
    for quad in range(QUADS):
        value = dot(table[quad], rows[quad * 4:(quad + 1) * 4].reshape(4 * TOK, D)).astype(BF)
        out[0, quad * 96:(quad + 1) * 96, :] = value[0:96]
        out[1, quad * 96:(quad + 1) * 96, :] = value[96:192]


def return_rows(table, value, out):
    for quad in range(QUADS):
        out[quad * 4:(quad + 1) * 4] = dot(table[quad], value[quad]).astype(BF).reshape(4, TOK, D)


def keep_rows(out, expert, value):
    for quad in range(QUADS):
        out[quad, expert * 96:(expert + 1) * 96, :] = value[quad * 96:(quad + 1) * 96]


def experts_kernel(rows, table, table_t, gslot, wg, wu, wd, part, xs, g_out, u_out, kept):
    place_rows(table, rows, xs)
    for expert in range(2):
        x = xs[expert]
        g = dot(x, wg[expert])
        u = dot(x, wu[expert])
        g_out[expert] = g.astype(BF)
        u_out[expert] = u.astype(BF)
        z = (g * jax.nn.sigmoid(g) * u).astype(BF)
        y = dot(z, wd[expert]).astype(BF).astype(F32)
        keep_rows(kept, expert, (y * gslot[expert]).astype(BF))
    return_rows(table_t, kept, part)


def experts_back_kernel(
    rows, table, table_t, gslot, g_ref, u_ref, wg, wu, wd, part, dy_out, dgu_out, z_out, kept
):
    place_rows(table, rows, dy_out)
    for expert in range(2):
        dy = ((RESID_MUL * gslot[expert]) * dy_out[expert].astype(F32)).astype(BF)
        dy_out[expert] = dy
        dz = dot_cols(dy, wd[expert])
        g, u = g_ref[expert].astype(F32), u_ref[expert].astype(F32)
        sig = jax.nn.sigmoid(g)
        silu = g * sig
        z_out[expert] = (silu * u).astype(BF)
        dg = (dz * u * sig * (1.0 + g * (1.0 - sig))).astype(BF)
        du = (dz * silu).astype(BF)
        dgu_out[expert, :, 0:FF] = dg
        dgu_out[expert, :, FF:2 * FF] = du
        keep_rows(kept, expert, (dot_cols(dg, wg[expert]) + dot_cols(du, wu[expert])).astype(BF))
    return_rows(table_t, kept, part)


def attention_weights_kernel(na, nb, pa, pb, da_a, da_b, oa, ob, out):
    one = (dot_rows(na[...], pa[...]) + dot_rows(nb[...], pb[...])).astype(BF)
    two = (
        dot_rows(da_a[...].reshape(PACK, D), oa[...]) + dot_rows(da_b[...].reshape(PACK, D), ob[...])
    ).astype(BF)
    out[:, :, 0:512] = one.reshape(COLS, TOK, 512)
    out[:, :, 512:768] = two.reshape(COLS, TOK, 256)


def call_local(kernel, outs, flops, *args, scratch=(), limit=20):
    return pl.pallas_call(
        kernel,
        out_shape=outs,
        in_specs=[VM] * len(args),
        out_specs=[VM] * len(outs),
        scratch_shapes=list(scratch),
        compiler_params=pltpu.CompilerParams(vmem_limit_bytes=limit * 2**20),
        cost_estimate=pl.CostEstimate(flops=flops, bytes_accessed=6 * 10**6, transcendentals=0),
    )(*args)


def owner_kernel(lengths, routes, gates, rank_gate, cosine, sine, seg, seg_t):
    section = lax.axis_index("section")
    expert = lax.broadcasted_iota(jnp.int32, (EXPERTS, TOK), 0)
    before = (
        lax.broadcasted_iota(jnp.int32, (TOK, TOK), 0) < lax.broadcasted_iota(jnp.int32, (TOK, TOK), 1)
    ).astype(BF)
    place = lax.broadcasted_iota(jnp.int32, (PACK, 128), 0)
    place_t = lax.broadcasted_iota(jnp.int32, (8, PACK), 1)
    lane = lax.rem(lax.broadcasted_iota(jnp.int32, (PACK, 128), 1), HEAD // 2).astype(F32)
    frequency = jnp.exp(lane * (-2.0 / HEAD * math.log(ROPE_THETA)))
    for slot in range(2):
        micro = section if slot == 0 else 1 - section
        chosen = jnp.zeros((EXPERTS, TOK), F32)
        gate = jnp.zeros((EXPERTS, TOK), F32)
        for k in range(8):
            same = expert == routes[micro, k:k + 1, :]
            chosen = chosen + jnp.where(same, 1.0, 0.0)
            gate = gate + jnp.where(same, gates[micro, k:k + 1, :], 0.0)
        rank = jnp.where(chosen > 0.5, dot(chosen.astype(BF), before), -1.0)
        rank_gate[slot * EXPERTS:(slot + 1) * EXPERTS, :] = jnp.concatenate([rank, gate], axis=1)
        segment = jnp.zeros((PACK, 128), jnp.int32)
        segment_t = jnp.zeros((8, PACK), jnp.int32)
        start = jnp.zeros((PACK, 128), jnp.int32)
        end = jnp.int32(0)
        for k in range(4):
            size = lengths[micro, k]
            end = end + size
            segment = segment + jnp.where(place >= end, 1, 0)
            segment_t = segment_t + jnp.where(place_t >= end, 1, 0)
            start = start + jnp.where(place >= end, size, 0)
        angles = (place - start).astype(F32) * frequency
        cosine[slot] = jnp.cos(angles)
        sine[slot] = jnp.sin(angles)
        seg[slot] = segment[:, 0:1]
        seg_t[slot] = segment_t[0:1, :]


def run_owner(lengths, routes, gates):
    return pl.pallas_call(
        owner_kernel,
        out_shape=[
            sds((2 * EXPERTS, 128), F32), sds((2, PACK, 128), F32), sds((2, PACK, 128), F32),
            sds((2, PACK, 1), jnp.int32), sds((2, 1, PACK), jnp.int32),
        ],
        in_specs=[pl.BlockSpec(memory_space=pltpu.SMEM), VM, VM],
        out_specs=[VM] * 5,
    )(lengths, routes, gates)


def tables_kernel(shared, *outs):
    col = lax.axis_index("col")
    shape = (4 * CAP, 4 * TOK)
    line = lax.broadcasted_iota(jnp.int32, shape, 0)
    column = lax.broadcasted_iota(jnp.int32, shape, 1)
    own_group = (line // CAP) == (column // TOK)
    wanted = lax.rem(line, CAP).astype(F32)
    for slot in range(2):
        table, table_t, gslot = outs[3 * slot:3 * slot + 3]
        for quad in range(QUADS):
            for expert in range(2):
                rows = [
                    shared[4 * quad + index, pl.ds(slot * EXPERTS + 2 * col + expert, 1), :] for index in range(4)
                ]
                rank = jnp.concatenate([row[:, 0:TOK] for row in rows], axis=1)
                gate = jnp.concatenate([row[:, TOK:2 * TOK] for row in rows], axis=1)
                mark = jnp.where(own_group & (rank == wanted), 1.0, 0.0)
                table[quad, expert * 96:(expert + 1) * 96, :] = mark.astype(BF)
                table_t[quad, :, expert * 96:(expert + 1) * 96] = mark.T.astype(BF)
                gslot[expert, quad * 96:(quad + 1) * 96, :] = jnp.sum(mark * gate, axis=1, keepdims=True)


def run_tables(shared):
    outs = [sds((QUADS, 8 * CAP, 4 * TOK), BF), sds((QUADS, 4 * TOK, 8 * CAP), BF), sds((2, SLOTS, 1), F32)]
    outs = call_local(tables_kernel, outs + outs, 10**7, shared)
    return [outs[0:3], outs[3:6]]


def per_device(
    ends_in, q_weight, key_projection, value_projection, out_weight, attn_gain, moe_gain,
    gate_weight, up_weight, down_weight, routes, gates, lengths,
):
    section = lax.axis_index("section")
    ends = ends_in[0, :, 0]
    own = jnp.concatenate([q_weight[0], key_projection[0], value_projection[0], out_weight[0]], axis=1)
    rank_gate, cosine, sine, seg, seg_t = run_owner(
        lengths[:, 0], jnp.swapaxes(routes[0, :, 0], 1, 2), jnp.swapaxes(gates[0, :, 0], 1, 2)
    )
    started = run_start(own, rank_gate, ends[0])
    routings = [
        dict(zip(("table", "table_t", "gslot"), tables), wg=gate_weight[0], wu=up_weight[0], wd=down_weight[0])
        for tables in run_tables(started.rg_out)
    ]
    moe_only = dict(moe_gain=moe_gain)
    back_common = dict(
        w=started.w_out.reshape(D, 768), attn_gain=attn_gain, cosine=cosine, sine=sine, seg=seg, seg_t=seg_t
    )
    common = dict(back_common, **moe_only)

    def attention_kept(step):
        return dict(q_in=step.q, kv_in=step.kv)

    def expert_kept(step):
        return dict(g_in=step.g, u_in=step.u)

    att0 = run_forward_attention(1, 0, started.x_out, ends[0], common)
    exp0 = run_forward_experts(2, att0.rows, att0.resid, ends[1], routings[0])
    att1 = run_forward_attention(3, 1, exp0.out, None, common)
    exp1 = run_forward_experts(2, att1.rows, att1.resid, ends[0], routings[1])
    one = run_turn_one(4, 0, exp1.out, att0.rows, att1.resid, ends[0], expert_kept(exp1), common, routings[1])
    two = run_turn_two(
        5, 1, one.rows, one.resid, one.da, exp0.out, one.dr, ends[1], attention_kept(att1), back_common, routings[0]
    )
    back1 = run_backward_experts(6, two.out, one.resid, two.entry, expert_kept(two), moe_gain, routings[0])
    end1 = run_backward_attention(7, 0, back1.da, exp1.out, back1.dr, ends[0], attention_kept(one), back_common)
    earlier = dict(xs_a=two.xs, dgu_a=back1.dgu, z_a=back1.z, dy_a=back1.dy, xs_b=exp1.xs)
    back2 = run_last_experts(
        8, end1.out, att1.resid, end1.entry, expert_kept(exp1), earlier, moe_gain, routings[1]
    )
    weights_in = dict(
        n1_a=one.n1, n1_b=att1.n1, dp_a=end1.dp, da_a=back1.da, o_a=one.o, o_b=att1.o
    )
    gains = dict(again_a=end1.again, dgain_a=back1.dgain, dgain_b=back2.dgain)
    last = run_last(
        9, 1, back2.da, exp0.out, back2.dr, attention_kept(att1), back2.late, back2.down, weights_in, gains, back_common
    )
    forward_one, forward_two = exp1.nexth, two.nexth
    backward_one, backward_two = end1.dhin, last.dhin
    attn_sum, gain_sum = last.weight_sum, last.gain_sum
    on_first = section == 0
    ends_out = jnp.stack(
        [jnp.where(on_first, backward_one, forward_one), jnp.where(on_first, backward_two, forward_two)], axis=0
    )[None, :, None]
    return (
        ends_out,
        attn_sum[None, :, 0:256],
        attn_sum[None, :, 256:384],
        attn_sum[None, :, 384:512],
        attn_sum[None, :, 512:768],
        gain_sum[0:1],
        gain_sum[1:2],
        back2.early_sum[None, 0:2],
        jnp.concatenate([back2.early_sum[2:], last.late_sum], axis=0)[None],
        last.down_sum[None],
    )


def solution(mesh):
    tokens = P("section", None, "col", "row", None)
    mats = P("section", "col", "row")
    gain = P("section", None)
    experts = P("section", "col", None, None)
    by_row = P("section", "col", "row", None)
    return jax.shard_map(
        per_device,
        mesh=mesh,
        in_specs=(tokens, mats, mats, mats, mats, gain, gain, experts, experts, experts, tokens, tokens, P(None, "col", None)),
        out_specs=(tokens, mats, mats, mats, mats, gain, gain, by_row, by_row, P("section", "col", None, "row")),
        check_vma=False,
    )
```

```python
import math
import types

import jax
import jax.numpy as jnp
from jax import lax
from jax.experimental import pallas as pl
from jax.experimental.pallas import tpu as pltpu
from jax.sharding import PartitionSpec as P

D = 1024
FF = 512
HEAD = 64
TOK = 64
ROWS = 4
COLS = 16
EXPERTS = 32
CAP = 24
PACK = 256
SLOTS = COLS * CAP
QUADS = 4

SCORE_MUL = 0.015625
RESID_MUL = 0.22
NORM_EPS = 1e-06
ROPE_THETA = 10000.0
MESH = pl.DeviceIdType.MESH
BF = jnp.bfloat16
F32 = jnp.float32
VM = pl.BlockSpec(memory_space=pltpu.VMEM)
DMA = pltpu.SemaphoreType.DMA


def dot(a, b):
    return jnp.dot(a, b, preferred_element_type=F32)


def dot_rows(a, b):
    return lax.dot_general(a, b, (((0,), (0,)), ((), ())), preferred_element_type=F32)


def dot_cols(a, b):
    return lax.dot_general(a, b, (((1,), (1,)), ((), ())), preferred_element_type=F32)


class Place:
    def __init__(self):
        self.section = lax.axis_index("section")
        self.row = lax.axis_index("row")
        self.col = lax.axis_index("col")
        self.high = self.col // 8
        self.deep = lax.rem(self.col // 2, 4)
        self.core = lax.rem(self.col, 2)

    def row_at(self, step):
        return lax.rem(self.row + step + ROWS, ROWS)

    def row_peer(self, step):
        return (self.section, self.row_at(step), self.col)

    def at(self, high, deep, core=0):
        high = lax.rem(self.high + high, 2)
        deep = lax.rem(self.deep + deep + 4, 4)
        return high * 8 + deep * 2 + lax.rem(self.core + core, 2)

    def peer(self, high, deep, core=0):
        return (self.section, self.row, self.at(high, deep, core))

    def across(self):
        return (1 - self.section, self.row, self.col)


class Greeting:
    def __init__(self, partners):
        self.barrier = pltpu.get_barrier_semaphore()
        self.count = len(partners)
        for partner in partners:
            pl.semaphore_signal(self.barrier, inc=1, device_id=partner, device_id_type=MESH)

    def wait(self):
        pl.semaphore_wait(self.barrier, self.count)


class Sems:
    def __init__(self, sends, recvs, base=0):
        self.sends, self.recvs, self.base = sends, recvs, base

    def part(self, base):
        return Sems(self.sends, self.recvs, self.base + base)


def remote(src, dst, sems, index, device):
    return pltpu.make_async_remote_copy(
        src_ref=src, dst_ref=dst, send_sem=sems.sends.at[sems.base + index], recv_sem=sems.recvs.at[sems.base + index],
        device_id=device, device_id_type=MESH,
    )


def send(src, dst, sems, index, device):
    copy = remote(src, dst, sems, index, device)
    copy.start()
    return copy


def finish(copies):
    for copy in copies:
        copy.wait_send()


def row_partners(me):
    return [me.row_peer(step) for step in (1, 2, 3)]


def col_partners(me):
    return [me.peer(0, 1), me.peer(0, 2), me.peer(0, 3), me.peer(1, 0), me.peer(0, 0, 1)]


def all_chip_partners(me):
    return [me.peer(high, deep) for high in range(2) for deep in range(4) if high or deep]


CUTS = ((0, 32, True), (32, 32, False))
PARTS = len(CUTS)
ROW_SEMS = [DMA((3 * PARTS,))] * 2
COL_SEMS = [DMA((7 * PARTS,))] * 2 + [DMA((8 * PARTS,))] * 2
NEAR = ((1, 0), (3, 1), (2, 2))


class Cut:
    def __init__(self, index):
        low, rows, self.z_first = CUTS[index]
        self.index = index
        self.span = pl.ds(low, rows)
        self.first = index == 0

    def row(self, sems):
        return Sems(sems[0], sems[1], 3 * self.index)

    def col(self, sems):
        return Sems(sems[0], sems[1], 7 * self.index), Sems(sems[2], sems[3], 8 * self.index)

    def one(self, sems):
        return Sems(sems[0], sems[1], self.index)


ALL_CUTS = [Cut(index) for index in range(PARTS)]


def weave(*chains):
    chains = list(chains)
    while chains:
        chains = [chain for chain in chains if next(chain, "end") != "end"]


def gather_row(me, out, cut, sems):
    sems = cut.row(sems)
    own = out.at[me.row, cut.span]
    copies = []
    for step in (2, 1, 3):
        copies.append(send(own, own, sems, step - 1, me.row_peer(step)))
    yield
    for step in (1, 3, 2):
        block = out.at[me.row_at(-step), cut.span]
        remote(block, block, sems, step - 1, me.row_peer(step)).wait_recv()
    finish(copies)


def gather_col(me, out, cut, sems):
    main, side = cut.col(sems)
    over, near = me.peer(1, 0), me.peer(0, 0, 1)
    own = out.at[me.col, cut.span]
    copies = []
    if cut.z_first:
        for deep, index in NEAR:
            copies.append(send(own, own, main, index, me.peer(0, deep)))
        copies.append(send(own, own, main, 3, over))
    else:
        copies.append(send(own, own, main, 3, over))
        for deep, index in NEAR:
            copies.append(send(own, own, main, index, me.peer(0, deep)))
    copies.append(send(own, own, side, 0, near))
    yield
    if cut.z_first:
        for deep, index in NEAR:
            block = out.at[me.at(0, -deep), cut.span]
            remote(block, block, main, index, over).wait_recv()
            copies.append(send(block, block, main, 4 + index, over))
            copies.append(send(block, block, side, 1 + index, near))
        yield
    far = out.at[me.at(1, 0), cut.span]
    remote(far, far, main, 3, over).wait_recv()
    if not cut.z_first:
        for deep, index in NEAR:
            copies.append(send(far, far, main, 4 + index, me.peer(0, deep)))
    copies.append(send(far, far, side, 4, near))
    yield
    for high in range(2):
        if high == 0 and cut.z_first:
            continue
        for deep, index in NEAR:
            block = out.at[me.at(high, -deep), cut.span]
            remote(block, block, main, 4 * high + index, over).wait_recv()
            copies.append(send(block, block, side, 4 * high + 1 + index, near))
    yield
    for high in range(2):
        for deep, index in ((0, -1),) + NEAR:
            block = out.at[me.at(high, -deep, 1), cut.span]
            remote(block, block, side, 4 * high + 1 + index, near).wait_recv()
    finish(copies)


def sum_row(me, part, landing, cut, sems, done):
    sems = cut.row(sems)
    copies = []
    for step in (2, 1, 3):
        copies.append(
            send(part.at[me.row_at(step), cut.span], landing.at[step - 1, cut.span], sems, step - 1, me.row_peer(step))
        )
    yield
    total = part[me.row, cut.span].astype(F32)
    for copy, step in zip(copies[1:] + copies[:1], (1, 3, 2)):
        copy.wait_recv()
        total = total + landing[step - 1, cut.span].astype(F32)
    yield from done(total, cut)
    finish(copies)


def sum_col(me, part, halves, outgoing, landing, cut, sems, done):
    main, side = cut.col(sems)
    over, near, span = me.peer(1, 0), me.peer(0, 0, 1), cut.span
    first, away = {}, {}
    for high in (1, 0):
        for deep in (2, 1, 3, 0):
            index = 4 * high + deep
            first[index] = send(part.at[me.at(high, deep, 1), span], halves.at[index, span], side, index, near)

    def pair(high, deep):
        index = 4 * high + deep
        first[index].wait_recv()
        return part[me.at(high, deep), span].astype(F32) + halves[index, span].astype(F32)

    def pass_on(slot, value, device):
        outgoing[slot, span] = value.astype(BF)
        away[slot] = send(outgoing.at[slot, span], landing.at[slot, span], main, slot, device)

    def landed(slot):
        away[slot].wait_recv()
        return landing[slot, span].astype(F32)

    yield
    if cut.z_first:
        for high in (1, 0):
            for deep in (2, 1, 3):
                pass_on(3 * high + deep - 1, pair(high, deep), me.peer(0, deep))
        yield
        total = pair(1, 0)
        for slot in (3, 5, 4):
            total = total + landed(slot)
        pass_on(6, total, over)
        yield
        total = pair(0, 0)
        for slot in (0, 2, 1, 6):
            total = total + landed(slot)
    else:
        for deep in (2, 1, 3, 0):
            pass_on(deep, pair(1, deep), over)
        yield
        for deep in (2, 1, 3):
            pass_on(3 + deep, pair(0, deep) + landed(deep), me.peer(0, deep))
        yield
        total = pair(0, 0) + landed(0)
        for slot in (4, 6, 5):
            total = total + landed(slot)
    yield from done(total, cut)
    finish(list(first.values()) + list(away.values()))


def sum_col_scratch(width):
    return dict(
        halves=pltpu.VMEM((8, TOK, width), BF),
        outgoing=pltpu.VMEM((7, TOK, width), BF),
        landing=pltpu.VMEM((7, TOK, width), BF),
    )


def store(ref):
    def done(total, cut):
        ref[cut.span, :] = total
        yield

    return done


def after_attention(me, h_ref, gain, other, resid, out, sems):
    def done(total, cut):
        span = cut.span
        value = h_ref[me.row, span].astype(F32) + RESID_MUL * total
        resid[span, :] = value
        scale = lax.rsqrt(jnp.mean(value * value, axis=1, keepdims=True) + NORM_EPS)
        normed = (value * scale * gain[...]).astype(BF)
        if other is not None:
            normed = jnp.where(me.section == 0, normed, other[span, :])
        out[me.col, span] = normed
        yield from gather_col(me, out, cut, sems)

    return done


def after_experts(me, resid, coming, nexth, out, arrived, over_sems, sems):
    def done(total, cut):
        span = cut.span
        nexth[span, :] = (resid[span, :] + RESID_MUL * total).astype(BF)
        if out is not None:
            over = send(nexth.at[span], arrived.at[span], cut.one(over_sems), 0, me.across())
            yield
            over.wait_recv()
            out[me.row, span] = jnp.where(me.section == 0, coming[span, :], arrived[span, :])
            yield from gather_row(me, out, cut, sems)
            over.wait_send()
        else:
            yield

    return done


def after_experts_back(me, resid, entry, gain, dr, dgain, out, sems):
    def done(total, cut):
        span = cut.span
        value = resid[span, :]
        scale = lax.rsqrt(jnp.mean(value * value, axis=1, keepdims=True) + NORM_EPS)
        weighted = total * gain[...]
        inner = jnp.mean(weighted * value, axis=1, keepdims=True)
        grad = entry[span, :].astype(F32) + scale * weighted - value * (scale * scale * scale) * inner
        out[me.row, span] = (RESID_MUL * grad).astype(BF)
        gather = gather_row(me, out, cut, sems)
        next(gather)
        dr[span, :] = grad
        term = jnp.sum(total * value * scale, axis=0, keepdims=True)
        dgain[...] = term if cut.first else dgain[...] + term
        yield
        yield from gather

    return done


def after_attention_back(me, dr, coming, dhin, entry, out, arrived, over_sems, sems):
    def done(total, cut):
        span = cut.span
        dhin[span, :] = (total + dr[span, :]).astype(BF)
        if out is not None:
            over = send(dhin.at[span], arrived.at[span], cut.one(over_sems), 0, me.across())
            yield
            over.wait_recv()
            chosen = jnp.where(me.section == 0, arrived[span, :], coming[span, :])
            entry[span, :] = chosen
            out[me.col, span] = chosen
            yield from gather_col(me, out, cut, sems)
            over.wait_send()
        else:
            yield

    return done


def sum_gains(me, gains, out, one, two, three, sems):
    sems = Sems(*sems)
    near = send(gains, one, sems, 0, me.peer(0, 0, 1))
    yield
    near.wait_recv()
    two[0] = gains[...] + one[...]
    chips = []
    for high in range(2):
        for deep in range(4):
            if high or deep:
                index = high * 4 + deep
                chips.append(send(two.at[0], two.at[index], sems, index, me.peer(high, deep)))
    yield
    for copy in chips:
        copy.wait_recv()
    three[0] = jnp.sum(two[...], axis=0)
    rows = []
    for step in (1, 2, 3):
        rows.append(send(three.at[0], three.at[step], sems, 7 + step, me.row_peer(step)))
    yield
    for copy in rows:
        copy.wait_recv()
    out[...] = jnp.sum(three[...], axis=0)
    finish([near] + chips + rows)


class RingSum:
    def __init__(self, me, blocks, land, total_out, sems):
        self.me, self.blocks, self.total_out = me, blocks, total_out
        self.passing, self.final = land
        self.sems = Sems(*sems)
        half = blocks.shape[2] // 2
        self.low, self.high = pl.ds(0, half), pl.ds(half, half)
        self.up, self.down = me.row_peer(1), me.row_peer(3)
        self.near_up, self.near_down, self.far = me.row_at(1), me.row_at(3), me.row_at(2)
        self.copies = {}

    def begin(self, piece):
        part, blocks = self.sems.part(6 * piece), self.blocks
        self.copies[piece] = [
            send(blocks.at[piece, self.far, self.low], self.passing.at[piece, 0], part, 0, self.up),
            send(blocks.at[piece, self.far, self.high], self.passing.at[piece, 1], part, 1, self.down),
            send(blocks.at[piece, self.near_up, self.high], self.final.at[piece, 0, self.high], part, 2, self.up),
            send(blocks.at[piece, self.near_down, self.low], self.final.at[piece, 1, self.low], part, 3, self.down),
        ]

    def pass_on(self, piece):
        part, copies = self.sems.part(6 * piece), self.copies[piece]
        for side, near, span, peer in ((0, self.near_up, self.low, self.up), (1, self.near_down, self.high, self.down)):
            copies[side].wait_recv()
            value = self.blocks[piece, near, span].astype(F32) + self.passing[piece, side].astype(F32)
            self.blocks[piece, near, span] = value.astype(BF)
            copies.append(send(self.blocks.at[piece, near, span], self.final.at[piece, side, span], part, 4 + side, peer))

    def end(self, piece):
        for copy in self.copies[piece][2:]:
            copy.wait_recv()
        self.total_out[piece] = (
            self.blocks[piece, self.me.row].astype(F32)
            + self.final[piece, 0].astype(F32)
            + self.final[piece, 1].astype(F32)
        ).astype(BF)
        finish(self.copies[piece])


def reduce_scratch(pieces, rows, width):
    return [
        pltpu.VMEM((pieces, 2, rows // 2, width), BF),
        pltpu.VMEM((pieces, 2, rows, width), BF),
    ]


def sds(shape, kind):
    return jax.ShapeDtypeStruct(shape, kind)


def call_remote(body, ident, ins, outs, scratch, limit, flops=10**7):
    flat, places = [], {}
    for name, item in scratch.items():
        if isinstance(item, list):
            places[name] = (len(flat), len(item))
            flat += item
        else:
            places[name] = (len(flat), None)
            flat.append(item)
    names = list(ins) + list(outs)

    def kernel(*refs):
        given = dict(zip(names, refs))
        rest = refs[len(names):]
        for name, (start, count) in places.items():
            given[name] = rest[start] if count is None else list(rest[start:start + count])
        body(types.SimpleNamespace(**given))

    results = pl.pallas_call(
        kernel,
        out_shape=list(outs.values()),
        in_specs=[VM] * len(ins),
        out_specs=[VM] * len(outs),
        scratch_shapes=flat,
        compiler_params=pltpu.CompilerParams(
            collective_id=ident, has_side_effects=True, vmem_limit_bytes=limit * 2**20
        ),
        cost_estimate=pl.CostEstimate(flops=flops, bytes_accessed=40 * 10**6, transcendentals=0),
    )(*ins.values())
    return types.SimpleNamespace(**dict(zip(outs, results)))


TOKEN_ROWS = sds((TOK, D), BF)
TOKEN_WIDE = sds((TOK, D), F32)
ROW_BLOCKS = sds((ROWS, TOK, D), BF)
COL_BLOCKS = sds((COLS, TOK, D), BF)
GAIN = sds((1, D), F32)
HEADS = sds((PACK, 256), BF)
WIDE_SLOTS = sds((2, SLOTS, D), BF)
FF_SLOTS = sds((2, SLOTS, FF), BF)
LAND_ROW = pltpu.VMEM((3, TOK, D), BF)
ARRIVED = pltpu.VMEM((TOK, D), BF)
ACROSS = [DMA((PARTS,))] * 2
ROW_PART = pltpu.VMEM((ROWS, TOK, D), BF)
COL_PART = pltpu.VMEM((COLS, TOK, D), BF)
KEPT = pltpu.VMEM((QUADS, 2 * 96, D), BF)
ATTENTION_OUTS = dict(n1=sds((PACK, D), BF), q=HEADS, kv=HEADS, o=HEADS)
EXPERT_OUTS = dict(xs=WIDE_SLOTS, g=FF_SLOTS, u=FF_SLOTS)
BACK_OUTS = dict(dy=WIDE_SLOTS, dgu=WIDE_SLOTS, z=sds((2, SLOTS, FF), BF))
ATTENTION_BACK_OUTS = dict(dp=sds((PACK, 512), BF), again=GAIN)


def attention_body(r, slot):
    attention_kernel(
        slot, r.packed, r.w, r.attn_gain, r.cosine, r.sine, r.seg, r.seg_t, r.part_x, r.n1, r.q, r.kv, r.o
    )


def tables_of(r, slot):
    return [getattr(r, name + str(slot)) for name in ("table", "table_t", "gslot")]


def experts_body(r, slot):
    experts_kernel(r.rows, *tables_of(r, slot), r.wg, r.wu, r.wd, r.part, r.xs, r.g, r.u, r.kept)


def experts_back_body(r, slot):
    experts_back_kernel(
        r.grad_rows, *tables_of(r, slot), r.g_in, r.u_in, r.wg, r.wu, r.wd, r.part_b, r.dy, r.dgu, r.z, r.kept
    )


def attention_back_body(r, slot):
    attention_back_kernel(
        slot, r.da, r.packed_b, r.w, r.attn_gain, r.cosine, r.sine, r.seg, r.seg_t, r.q_in, r.kv_in,
        r.part_y, r.dp, r.again,
    )


def run_start(w, rg, x):
    def body(r):
        me = Place()
        greeting = Greeting(row_partners(me) + col_partners(me))
        r.w_out[me.col] = r.w[...]
        r.rg_out[me.col] = r.rg[...]
        r.x_out[me.row] = r.x[...]
        greeting.wait()
        weave(
            *[gather_col(me, r.w_out, cut, r.col_w) for cut in ALL_CUTS],
            *[gather_row(me, r.x_out, cut, r.row) for cut in ALL_CUTS],
            *[gather_col(me, r.rg_out, cut, r.col_rg) for cut in ALL_CUTS],
        )

    return call_remote(
        body, 0, dict(w=w, rg=rg, x=x),
        dict(w_out=sds((COLS, TOK, 768), BF), rg_out=sds((COLS,) + rg.shape, F32), x_out=ROW_BLOCKS),
        dict(row=ROW_SEMS, col_w=COL_SEMS, col_rg=COL_SEMS), 8,
    )


TABLE_OUTS = {
    name + str(slot): shape
    for slot in range(2)
    for name, shape in (
        ("table", sds((QUADS, 8 * CAP, 4 * TOK), BF)),
        ("table_t", sds((QUADS, 4 * TOK, 8 * CAP), BF)),
        ("gslot", sds((2, SLOTS, 1), F32)),
    )
}


def run_forward(ident, slot, packed, coming, common, experts, other=None, shared=None, tables=None):
    first = other is not None

    def body(r):
        me = Place()
        greeting = Greeting(row_partners(me) + col_partners(me) + [me.across()])
        attention_body(r, slot)
        greeting.wait()
        done = after_attention(me, r.packed, r.moe_gain, r.other if first else None, r.resid, r.rows, r.col)

        def make_tables():
            for index in range(2):
                yield
                tables_kernel(index, r.shared, *tables_of(r, index))

        weave(
            *[sum_row(me, r.part_x, r.landing_x, cut, r.row, done) for cut in ALL_CUTS],
            *([make_tables()] if first else []),
        )
        experts_body(r, slot)
        done = after_experts(me, r.resid, r.coming, r.nexth, r.out, r.arrived, r.over, r.row_b)
        weave(*[sum_col(me, r.part, r.halves, r.outgoing, r.landing, cut, r.col_b, done) for cut in ALL_CUTS])

    extra = dict(other=other, shared=shared) if first else tables
    return call_remote(
        body, ident, dict(packed=packed, coming=coming, **common, **experts, **extra),
        dict(
            resid=TOKEN_WIDE, rows=COL_BLOCKS, nexth=TOKEN_ROWS, out=ROW_BLOCKS,
            **ATTENTION_OUTS, **EXPERT_OUTS, **(TABLE_OUTS if first else {}),
        ),
        dict(
            part_x=ROW_PART, landing_x=LAND_ROW, row=ROW_SEMS, col=COL_SEMS,
            part=COL_PART, kept=KEPT, arrived=ARRIVED, row_b=ROW_SEMS, col_b=COL_SEMS, over=ACROSS, **sum_col_scratch(D),
        ),
        LIMITS[0], 4 * 10**9,
    )


def run_turn(ident, packed, grad_rows, resid_b, entry_in, packed_b, coming, kept_f, common, experts, tables):
    def body(r):
        me = Place()
        greeting = Greeting(row_partners(me) + col_partners(me) + [me.across()])
        attention_body(r, 0)
        experts_back_body(r, 1)
        greeting.wait()
        done_f = after_attention(me, r.packed, r.moe_gain, None, r.resid, r.rows, r.col)
        done_b = after_experts_back(me, r.resid_b, r.entry_in, r.moe_gain, r.dr, r.dgain, r.da, r.row_b)
        weave(
            *[sum_row(me, r.part_x, r.landing_x, cut, r.row, done_f) for cut in ALL_CUTS],
            *[sum_col(me, r.part_b, r.halves, r.outgoing, r.landing, cut, r.col_b, done_b) for cut in ALL_CUTS],
        )
        attention_back_body(r, 1)
        experts_body(r, 0)
        done_f = after_experts(me, r.resid, None, r.nexth, None, None, None, None)
        done_b = after_attention_back(me, r.dr, r.coming, r.dhin, r.entry, r.out, r.arrived, r.over, r.col_c)
        weave(
            *[sum_row(me, r.part_y, r.landing_y, cut, r.row_c, done_b) for cut in ALL_CUTS],
            *[sum_col(me, r.part, r.halves_b, r.outgoing_b, r.landing_b, cut, r.col_d, done_f) for cut in ALL_CUTS],
        )

    second = {name + "_b": item for name, item in sum_col_scratch(D).items()}
    return call_remote(
        body, ident,
        dict(
            packed=packed, grad_rows=grad_rows, resid_b=resid_b, entry_in=entry_in, packed_b=packed_b, coming=coming,
            **kept_f, **common, **experts, **tables,
        ),
        dict(
            resid=TOKEN_WIDE, nexth=TOKEN_ROWS, dhin=TOKEN_ROWS, entry=TOKEN_ROWS, out=COL_BLOCKS,
            **ATTENTION_OUTS, **EXPERT_OUTS,
        ),
        dict(
            part_x=ROW_PART, landing_x=LAND_ROW, row=ROW_SEMS, col=COL_SEMS, part_b=COL_PART, kept=KEPT,
            row_b=ROW_SEMS, col_b=COL_SEMS, **sum_col_scratch(D), **second,
            part_y=ROW_PART, landing_y=LAND_ROW, arrived=ARRIVED, row_c=ROW_SEMS, col_c=COL_SEMS, over=ACROSS,
            part=COL_PART, col_d=COL_SEMS,
            **{name: pltpu.VMEM(item.shape, item.dtype) for name, item in dict(
                rows=COL_BLOCKS, dr=TOKEN_WIDE, dgain=GAIN, da=ROW_BLOCKS, **BACK_OUTS, **ATTENTION_BACK_OUTS
            ).items()},
        ),
        LIMITS[1], 10**10,
    )


def run_backward(ident, slot, grad_rows, resid, entry_in, packed_b, coming, kept_f, common, experts, tables):
    def body(r):
        me = Place()
        greeting = Greeting(row_partners(me) + col_partners(me) + [me.across()])
        experts_back_body(r, slot)
        greeting.wait()
        done = after_experts_back(me, r.resid, r.entry_in, r.moe_gain, r.dr, r.dgain, r.da, r.row)
        weave(*[sum_col(me, r.part_b, r.halves, r.outgoing, r.landing, cut, r.col, done) for cut in ALL_CUTS])
        attention_back_body(r, slot)
        done = after_attention_back(me, r.dr, r.coming, r.dhin, r.entry, r.out, r.arrived, r.over, r.col_b)
        weave(*[sum_row(me, r.part_y, r.landing_x, cut, r.row_b, done) for cut in ALL_CUTS])

    return call_remote(
        body, ident,
        dict(
            grad_rows=grad_rows, resid=resid, entry_in=entry_in, packed_b=packed_b, coming=coming,
            **kept_f, **common, **experts, **tables,
        ),
        dict(
            dgain=GAIN, da=ROW_BLOCKS, dhin=TOKEN_ROWS, entry=TOKEN_ROWS, out=COL_BLOCKS,
            **BACK_OUTS, **ATTENTION_BACK_OUTS,
        ),
        dict(
            part_b=COL_PART, kept=KEPT, row=ROW_SEMS, col=COL_SEMS, **sum_col_scratch(D),
            dr=pltpu.VMEM((TOK, D), F32),
            part_y=ROW_PART, landing_x=LAND_ROW, arrived=ARRIVED, row_b=ROW_SEMS, col_b=COL_SEMS, over=ACROSS,
        ),
        LIMITS[2], 5 * 10**9,
    )


def run_final(ident, slot, grad_rows, resid, entry_in, packed_b, kept_f, earlier, common, experts, tables):
    def body(r):
        me = Place()
        greeting = Greeting(row_partners(me) + all_chip_partners(me) + [me.peer(0, 0, 1)])
        experts_back_body(r, slot)
        greeting.wait()
        done = after_experts_back(me, r.resid, r.entry_in, r.moe_gain, r.dr, r.dgain, r.da, r.row)
        ring = RingSum(me, r.blocks, r.land_blocks, r.gate_up_sum, r.ring_sems)
        ring_down = RingSum(me, r.down, r.land_down, r.down_sum, r.ring_down_sems)

        def make(piece):
            kind, expert = divmod(piece, 2)
            span = slice(kind * FF, (kind + 1) * FF)
            value = dot_rows(r.xs_a[expert], r.dgu_a[expert, :, span]) + dot_rows(
                r.xs_b[expert], r.dgu[expert, :, span]
            )
            r.blocks[piece] = value.astype(BF).reshape(ROWS, 256, FF)
            ring.begin(piece)

        def make_down(expert):
            value = (dot_rows(r.z_a[expert], r.dy_a[expert]) + dot_rows(r.z[expert], r.dy[expert])).astype(BF)
            for row in range(ROWS):
                r.down[expert, row] = value[:, row * 256:(row + 1) * 256]
            ring_down.begin(expert)

        def grads():
            make(0)
            yield
            make(1)
            yield
            ring.pass_on(0)
            make(2)
            yield
            ring.pass_on(1)
            make(3)
            yield
            ring.pass_on(2)
            make_down(0)
            yield
            ring.pass_on(3)
            make_down(1)

        weave(
            *[sum_col(me, r.part_b, r.halves, r.outgoing, r.landing, cut, r.col, done) for cut in ALL_CUTS],
            grads(),
        )
        attention_back_body(r, slot)
        weight_part = r.part_b.at[:, :, 0:768]
        attention_weights_kernel(r.n1_a, r.n1_b, r.dp_a, r.dp, r.da_a, r.da, r.o_a, r.o_b, r.part_b)
        r.gains[0:1] = r.again_a[...] + r.again[...]
        r.gains[1:2] = r.dgain_a[...] + r.dgain[...]
        done = after_attention_back(me, r.dr, None, r.dhin, None, None, None, None, None)

        def rest():
            ring_down.pass_on(0)
            yield
            ring_down.pass_on(1)
            yield
            for piece in range(4):
                ring.end(piece)
            yield
            for piece in range(2):
                ring_down.end(piece)

        weave(
            *[sum_col(me, weight_part, r.halves_b, r.outgoing_b, r.landing_b, cut, r.col_b, store(r.weight_sum)) for cut in ALL_CUTS],
            *[sum_row(me, r.part_y, r.landing_x, cut, r.row_b, done) for cut in ALL_CUTS],
            sum_gains(me, r.gains, r.gain_sum, r.one, r.two, r.three, r.gain_sems),
            rest(),
        )

    second = {name + "_b": item for name, item in sum_col_scratch(768).items()}
    return call_remote(
        body, ident,
        dict(
            grad_rows=grad_rows, resid=resid, entry_in=entry_in, packed_b=packed_b,
            **kept_f, **earlier, **common, **experts, **tables,
        ),
        dict(
            dhin=TOKEN_ROWS, weight_sum=sds((TOK, 768), F32), gain_sum=sds((2, D), F32),
            gate_up_sum=sds((4, 256, FF), BF), down_sum=sds((2, FF, 256), BF),
        ),
        dict(
            blocks=pltpu.VMEM((4, ROWS, 256, FF), BF), land_blocks=reduce_scratch(4, 256, FF), ring_sems=[DMA((24,))] * 2,
            down=pltpu.VMEM((2, ROWS, FF, 256), BF), land_down=reduce_scratch(2, FF, 256), ring_down_sems=[DMA((12,))] * 2,
            part_b=COL_PART, kept=KEPT, row=ROW_SEMS, col=COL_SEMS, **sum_col_scratch(D), **second,
            part_y=ROW_PART, landing_x=LAND_ROW, row_b=ROW_SEMS, col_b=COL_SEMS,
            gains=pltpu.VMEM((2, D), F32),
            one=pltpu.VMEM((2, D), F32), two=pltpu.VMEM((8, 2, D), F32), three=pltpu.VMEM((4, 2, D), F32),
            gain_sems=[DMA((11,))] * 2,
            **{name: pltpu.VMEM(item.shape, item.dtype) for name, item in dict(
                dr=TOKEN_WIDE, dgain=GAIN, da=ROW_BLOCKS, **BACK_OUTS, **ATTENTION_BACK_OUTS
            ).items()},
        ),
        LIMITS[3], 10**10,
    )


LIMITS = (16, 26, 18, 34)


def swap_halves(value):
    width = value.shape[1]
    lane = lax.broadcasted_iota(jnp.int32, value.shape, 1)
    low = lax.rem(lane, HEAD) < HEAD // 2
    up = pltpu.roll(value, HEAD // 2, axis=1)
    down = pltpu.roll(value, width - HEAD // 2, axis=1)
    return low, up, down


def rope(value, cosine, sine):
    low, up, down = swap_halves(value)
    return value * cosine + jnp.where(low, -down, up) * sine


def rope_back(value, cosine, sine):
    low, up, down = swap_halves(value * sine)
    return value * cosine + jnp.where(low, down, -up)


def allowed_mask(seg, seg_t):
    shape = (PACK, PACK)
    query = lax.broadcasted_iota(jnp.int32, shape, 0)
    key = lax.broadcasted_iota(jnp.int32, shape, 1)
    return (seg == seg_t) & (key <= query)


def probabilities(q, k, allowed):
    scores = jnp.where(allowed, dot_cols(q, k) * SCORE_MUL, -1e30)
    weights = jnp.exp(scores - jnp.max(scores, axis=1, keepdims=True))
    return weights / jnp.sum(weights, axis=1, keepdims=True)


def attention_kernel(slot, x_ref, w, gain, cosine, sine, seg, seg_t, part, n1, q_out, kv_out, o_out):
    x = x_ref[...].reshape(PACK, D).astype(F32)
    scale = lax.rsqrt(jnp.mean(x * x, axis=1, keepdims=True) + NORM_EPS)
    normed = (x * scale * gain[...]).astype(BF)
    n1[...] = normed
    cos, sin = cosine[slot], sine[slot]
    pre = dot(normed, w[:, 0:512])
    q = jnp.concatenate(
        [rope(pre[:, 0:128], cos, sin), rope(pre[:, 128:256], cos, sin)], axis=1
    ).astype(BF)
    k = rope(pre[:, 256:384], cos, sin).astype(BF)
    v = pre[:, 384:512].astype(BF)
    q_out[...] = q
    kv_out[:, 0:128] = k
    kv_out[:, 128:256] = v
    allowed = allowed_mask(seg[slot], seg_t[slot])
    heads = []
    for head in range(4):
        at = (head // 2) * HEAD
        prob = probabilities(q[:, head * HEAD:(head + 1) * HEAD], k[:, at:at + HEAD], allowed)
        heads.append(dot(prob.astype(BF), v[:, at:at + HEAD]))
    mixed = jnp.concatenate(heads, axis=1).astype(BF)
    o_out[...] = mixed
    part[...] = dot_cols(mixed, w[:, 512:768]).astype(BF).reshape(ROWS, TOK, D)


def attention_back_kernel(
    slot, da, x_ref, w, gain, cosine, sine, seg, seg_t, q_ref, kv_ref, part, dp_out, dgain
):
    cos, sin = cosine[slot], sine[slot]
    do = dot(da[...].reshape(PACK, D), w[:, 512:768]).astype(BF)
    q = q_ref[...]
    kv = kv_ref[...]
    allowed = allowed_mask(seg[slot], seg_t[slot])
    dqs, dks, dvs = [], [None, None], [None, None]
    for head in range(4):
        group = head // 2
        at = group * HEAD
        qh = q[:, head * HEAD:(head + 1) * HEAD]
        kh = kv[:, at:at + HEAD]
        vh = kv[:, 128 + at:128 + at + HEAD]
        doh = do[:, head * HEAD:(head + 1) * HEAD]
        prob = probabilities(qh, kh, allowed)
        dv = dot_rows(prob.astype(BF), doh)
        dprob = dot_cols(doh, vh)
        ds = (prob * (dprob - jnp.sum(prob * dprob, axis=1, keepdims=True))).astype(BF)
        dqs.append(dot(ds, kh) * SCORE_MUL)
        dk = dot_rows(ds, qh) * SCORE_MUL
        dks[group] = dk if dks[group] is None else dks[group] + dk
        dvs[group] = dv if dvs[group] is None else dvs[group] + dv
    dp = jnp.concatenate(
        [
            rope_back(jnp.concatenate(dqs[0:2], axis=1), cos, sin),
            rope_back(jnp.concatenate(dqs[2:4], axis=1), cos, sin),
            rope_back(jnp.concatenate(dks, axis=1), cos, sin),
            jnp.concatenate(dvs, axis=1),
        ],
        axis=1,
    ).astype(BF)
    dp_out[...] = dp
    dn1 = dot_cols(dp, w[:, 0:512])
    x = x_ref[...].reshape(PACK, D).astype(F32)
    scale = lax.rsqrt(jnp.mean(x * x, axis=1, keepdims=True) + NORM_EPS)
    dgain[...] = jnp.sum(dn1 * x * scale, axis=0, keepdims=True)
    weighted = dn1 * gain[...]
    inner = jnp.mean(weighted * x, axis=1, keepdims=True)
    part[...] = (scale * weighted - x * (scale * scale * scale) * inner).astype(BF).reshape(ROWS, TOK, D)


def place_rows(table, rows, out):
    for quad in range(QUADS):
        value = dot(table[quad], rows[quad * 4:(quad + 1) * 4].reshape(4 * TOK, D)).astype(BF)
        out[0, quad * 96:(quad + 1) * 96, :] = value[0:96]
        out[1, quad * 96:(quad + 1) * 96, :] = value[96:192]


def return_rows(table, value, out):
    for quad in range(QUADS):
        out[quad * 4:(quad + 1) * 4] = dot(table[quad], value[quad]).astype(BF).reshape(4, TOK, D)


def keep_rows(out, expert, value):
    for quad in range(QUADS):
        out[quad, expert * 96:(expert + 1) * 96, :] = value[quad * 96:(quad + 1) * 96]


def experts_kernel(rows, table, table_t, gslot, wg, wu, wd, part, xs, g_out, u_out, kept):
    place_rows(table, rows, xs)
    for expert in range(2):
        x = xs[expert]
        g = dot(x, wg[expert])
        u = dot(x, wu[expert])
        g_out[expert] = g.astype(BF)
        u_out[expert] = u.astype(BF)
        z = (g * jax.nn.sigmoid(g) * u).astype(BF)
        y = dot(z, wd[expert]).astype(BF).astype(F32)
        keep_rows(kept, expert, (y * gslot[expert]).astype(BF))
    return_rows(table_t, kept, part)


def experts_back_kernel(
    rows, table, table_t, gslot, g_ref, u_ref, wg, wu, wd, part, dy_out, dgu_out, z_out, kept
):
    place_rows(table, rows, dy_out)
    for expert in range(2):
        dy = ((RESID_MUL * gslot[expert]) * dy_out[expert].astype(F32)).astype(BF)
        dy_out[expert] = dy
        dz = dot_cols(dy, wd[expert])
        g, u = g_ref[expert].astype(F32), u_ref[expert].astype(F32)
        sig = jax.nn.sigmoid(g)
        silu = g * sig
        z_out[expert] = (silu * u).astype(BF)
        dg = (dz * u * sig * (1.0 + g * (1.0 - sig))).astype(BF)
        du = (dz * silu).astype(BF)
        dgu_out[expert, :, 0:FF] = dg
        dgu_out[expert, :, FF:2 * FF] = du
        keep_rows(kept, expert, (dot_cols(dg, wg[expert]) + dot_cols(du, wu[expert])).astype(BF))
    return_rows(table_t, kept, part)


def attention_weights_kernel(na, nb, pa, pb, da_a, da_b, oa, ob, out):
    one = (dot_rows(na[...], pa[...]) + dot_rows(nb[...], pb[...])).astype(BF)
    two = (
        dot_rows(da_a[...].reshape(PACK, D), oa[...]) + dot_rows(da_b[...].reshape(PACK, D), ob[...])
    ).astype(BF)
    out[:, :, 0:512] = one.reshape(COLS, TOK, 512)
    out[:, :, 512:768] = two.reshape(COLS, TOK, 256)


def owner_kernel(lengths, routes, gates, rank_gate, cosine, sine, seg, seg_t):
    section = lax.axis_index("section")
    expert = lax.broadcasted_iota(jnp.int32, (EXPERTS, TOK), 0)
    before = (
        lax.broadcasted_iota(jnp.int32, (TOK, TOK), 0) < lax.broadcasted_iota(jnp.int32, (TOK, TOK), 1)
    ).astype(BF)
    place = lax.broadcasted_iota(jnp.int32, (PACK, 128), 0)
    place_t = lax.broadcasted_iota(jnp.int32, (8, PACK), 1)
    lane = lax.rem(lax.broadcasted_iota(jnp.int32, (PACK, 128), 1), HEAD // 2).astype(F32)
    frequency = jnp.exp(lane * (-2.0 / HEAD * math.log(ROPE_THETA)))
    for slot in range(2):
        micro = section if slot == 0 else 1 - section
        chosen = jnp.zeros((EXPERTS, TOK), F32)
        gate = jnp.zeros((EXPERTS, TOK), F32)
        for k in range(8):
            same = expert == routes[micro, k:k + 1, :]
            chosen = chosen + jnp.where(same, 1.0, 0.0)
            gate = gate + jnp.where(same, gates[micro, k:k + 1, :], 0.0)
        rank = jnp.where(chosen > 0.5, dot(chosen.astype(BF), before), -1.0)
        rank_gate[slot * EXPERTS:(slot + 1) * EXPERTS, :] = jnp.concatenate([rank, gate], axis=1)
        segment = jnp.zeros((PACK, 128), jnp.int32)
        segment_t = jnp.zeros((8, PACK), jnp.int32)
        start = jnp.zeros((PACK, 128), jnp.int32)
        end = jnp.int32(0)
        for k in range(4):
            size = lengths[micro, k]
            end = end + size
            segment = segment + jnp.where(place >= end, 1, 0)
            segment_t = segment_t + jnp.where(place_t >= end, 1, 0)
            start = start + jnp.where(place >= end, size, 0)
        angles = (place - start).astype(F32) * frequency
        cosine[slot] = jnp.cos(angles)
        sine[slot] = jnp.sin(angles)
        seg[slot] = segment[:, 0:1]
        seg_t[slot] = segment_t[0:1, :]


def run_owner(lengths, routes, gates):
    return pl.pallas_call(
        owner_kernel,
        out_shape=[
            sds((2 * EXPERTS, 128), F32), sds((2, PACK, 128), F32), sds((2, PACK, 128), F32),
            sds((2, PACK, 1), jnp.int32), sds((2, 1, PACK), jnp.int32),
        ],
        in_specs=[pl.BlockSpec(memory_space=pltpu.SMEM), VM, VM],
        out_specs=[VM] * 5,
        compiler_params=pltpu.CompilerParams(vmem_limit_bytes=8 * 2**20),
    )(lengths, routes, gates)


def tables_kernel(slot, shared, table, table_t, gslot):
    col = lax.axis_index("col")
    shape = (4 * CAP, 4 * TOK)
    line = lax.broadcasted_iota(jnp.int32, shape, 0)
    column = lax.broadcasted_iota(jnp.int32, shape, 1)
    own_group = (line // CAP) == (column // TOK)
    wanted = lax.rem(line, CAP).astype(F32)
    for quad in range(QUADS):
        for expert in range(2):
            rows = [
                shared[4 * quad + index, pl.ds(slot * EXPERTS + 2 * col + expert, 1), :] for index in range(4)
            ]
            rank = jnp.concatenate([row[:, 0:TOK] for row in rows], axis=1)
            gate = jnp.concatenate([row[:, TOK:2 * TOK] for row in rows], axis=1)
            mark = jnp.where(own_group & (rank == wanted), 1.0, 0.0)
            table[quad, expert * 96:(expert + 1) * 96, :] = mark.astype(BF)
            table_t[quad, :, expert * 96:(expert + 1) * 96] = mark.T.astype(BF)
            gslot[expert, quad * 96:(quad + 1) * 96, :] = jnp.sum(mark * gate, axis=1, keepdims=True)


def per_device(
    ends_in, q_weight, key_projection, value_projection, out_weight, attn_gain, moe_gain,
    gate_weight, up_weight, down_weight, routes, gates, lengths,
):
    section = lax.axis_index("section")
    ends = ends_in[0, :, 0]
    rank_gate, cosine, sine, seg, seg_t = run_owner(
        lengths[:, 0], jnp.swapaxes(routes[0, :, 0], 1, 2), jnp.swapaxes(gates[0, :, 0], 1, 2)
    )
    own = jnp.concatenate([q_weight[0], key_projection[0], value_projection[0], out_weight[0]], axis=1)
    started = run_start(own, rank_gate, ends[0])
    experts = dict(wg=gate_weight[0], wu=up_weight[0], wd=down_weight[0])
    common = dict(
        w=started.w_out.reshape(D, 768), attn_gain=attn_gain, moe_gain=moe_gain,
        cosine=cosine, sine=sine, seg=seg, seg_t=seg_t,
    )

    zero = run_forward(1, 0, started.x_out, ends[1], common, experts, other=ends[0], shared=started.rg_out)
    tables = {name: getattr(zero, name) for name in TABLE_OUTS}
    slots = [{name: item for name, item in tables.items() if name[-1] == str(slot)} for slot in range(2)]
    one = run_forward(2, 1, zero.out, ends[0], common, experts, tables=slots[1])
    kept_one = dict(q_in=one.q, kv_in=one.kv, g_in=one.g, u_in=one.u)
    two = run_turn(
        3, one.out, zero.rows, one.resid, ends[0], zero.out, ends[1], kept_one, common, experts, tables
    )
    kept_two = dict(q_in=two.q, kv_in=two.kv, g_in=two.g, u_in=two.u)
    back = run_backward(
        4, 0, two.out, two.resid, two.entry, one.out, ends[0], kept_two, common, experts, slots[0]
    )
    earlier = dict(
        xs_a=two.xs, dgu_a=back.dgu, z_a=back.z, dy_a=back.dy, xs_b=one.xs, n1_a=two.n1, n1_b=one.n1,
        dp_a=back.dp, da_a=back.da, o_a=two.o, o_b=one.o, again_a=back.again, dgain_a=back.dgain,
    )
    last = run_final(5, 1, back.out, one.resid, back.entry, zero.out, kept_one, earlier, common, experts, slots[1])
    forward_one, forward_two = one.nexth, two.nexth
    backward_one, backward_two = back.dhin, last.dhin
    attn_sum, gain_sum = last.weight_sum, last.gain_sum
    on_first = section == 0
    ends_out = jnp.stack(
        [jnp.where(on_first, backward_one, forward_one), jnp.where(on_first, backward_two, forward_two)], axis=0
    )[None, :, None]
    return (
        ends_out,
        attn_sum[None, :, 0:256],
        attn_sum[None, :, 256:384],
        attn_sum[None, :, 384:512],
        attn_sum[None, :, 512:768],
        gain_sum[0:1],
        gain_sum[1:2],
        last.gate_up_sum[None, 0:2].astype(F32),
        last.gate_up_sum[None, 2:4].astype(F32),
        last.down_sum[None].astype(F32),
    )


def solution(mesh):
    tokens = P("section", None, "col", "row", None)
    mats = P("section", "col", "row")
    gain = P("section", None)
    experts = P("section", "col", None, None)
    by_row = P("section", "col", "row", None)
    return jax.shard_map(
        per_device,
        mesh=mesh,
        in_specs=(tokens, mats, mats, mats, mats, gain, gain, experts, experts, experts, tokens, tokens, P(None, "col", None)),
        out_specs=(tokens, mats, mats, mats, mats, gain, gain, by_row, by_row, P("section", "col", None, "row")),
        check_vma=False,
    )
```

```python
import math
import types

import jax
import jax.numpy as jnp
from jax import lax
from jax.experimental import pallas as pl
from jax.experimental.pallas import tpu as pltpu
from jax.sharding import PartitionSpec as P

D = 1024
FF = 512
HEAD = 64
TOK = 64
ROWS = 4
COLS = 16
EXPERTS = 32
CAP = 24
PACK = 256
SLOTS = COLS * CAP
QUADS = 4

SCORE_MUL = 0.015625
RESID_MUL = 0.22
NORM_EPS = 1e-06
ROPE_THETA = 10000.0
MESH = pl.DeviceIdType.MESH
BF = jnp.bfloat16
F32 = jnp.float32
VM = pl.BlockSpec(memory_space=pltpu.VMEM)
DMA = pltpu.SemaphoreType.DMA


def dot(a, b):
    return jnp.dot(a, b, preferred_element_type=F32)


def dot_rows(a, b):
    return lax.dot_general(a, b, (((0,), (0,)), ((), ())), preferred_element_type=F32)


def dot_cols(a, b):
    return lax.dot_general(a, b, (((1,), (1,)), ((), ())), preferred_element_type=F32)


class Place:
    def __init__(self):
        self.section = lax.axis_index("section")
        self.row = lax.axis_index("row")
        self.col = lax.axis_index("col")
        self.high = self.col // 8
        self.deep = lax.rem(self.col // 2, 4)
        self.core = lax.rem(self.col, 2)

    def row_at(self, step):
        return lax.rem(self.row + step + ROWS, ROWS)

    def row_peer(self, step):
        return (self.section, self.row_at(step), self.col)

    def at(self, high, deep, core=0):
        high = lax.rem(self.high + high, 2)
        deep = lax.rem(self.deep + deep + 4, 4)
        return high * 8 + deep * 2 + lax.rem(self.core + core, 2)

    def peer(self, high, deep, core=0):
        return (self.section, self.row, self.at(high, deep, core))

    def across(self):
        return (1 - self.section, self.row, self.col)


class Greeting:
    def __init__(self, partners):
        self.barrier = pltpu.get_barrier_semaphore()
        self.count = len(partners)
        for partner in partners:
            pl.semaphore_signal(self.barrier, inc=1, device_id=partner, device_id_type=MESH)

    def wait(self):
        pl.semaphore_wait(self.barrier, self.count)


class Sems:
    def __init__(self, sends, recvs, base=0):
        self.sends, self.recvs, self.base = sends, recvs, base

    def part(self, base):
        return Sems(self.sends, self.recvs, self.base + base)


def remote(src, dst, sems, index, device):
    return pltpu.make_async_remote_copy(
        src_ref=src, dst_ref=dst, send_sem=sems.sends.at[sems.base + index], recv_sem=sems.recvs.at[sems.base + index],
        device_id=device, device_id_type=MESH,
    )


def send(src, dst, sems, index, device):
    copy = remote(src, dst, sems, index, device)
    copy.start()
    return copy


def finish(copies):
    for copy in copies:
        copy.wait_send()


def row_partners(me):
    return [me.row_peer(step) for step in (1, 2, 3)]


def col_partners(me):
    return [me.peer(0, 1), me.peer(0, 2), me.peer(0, 3), me.peer(1, 0), me.peer(0, 0, 1)]


def all_chip_partners(me):
    return [me.peer(high, deep) for high in range(2) for deep in range(4) if high or deep]


CUTS = ((0, 32, True), (32, 32, False))
PARTS = len(CUTS)
ROW_SEMS = [DMA((3 * PARTS,))] * 2
COL_SEMS = [DMA((9 * PARTS,))] * 2 + [DMA((8 * PARTS,))] * 2
DEEPS = (0, -1, 1, 2)


class Cut:
    def __init__(self, index):
        low, rows, self.z_first = CUTS[index]
        self.index = index
        self.span = pl.ds(low, rows)
        self.low, self.high = pl.ds(low, rows // 2), pl.ds(low + rows // 2, rows // 2)
        self.first = index == 0

    def row(self, sems):
        return Sems(sems[0], sems[1], 3 * self.index)

    def col(self, sems):
        return Sems(sems[0], sems[1], 9 * self.index), Sems(sems[2], sems[3], 8 * self.index)

    def one(self, sems):
        return Sems(sems[0], sems[1], self.index)


ALL_CUTS = [Cut(index) for index in range(PARTS)]


def weave(*chains):
    chains = list(chains)
    while chains:
        chains = [chain for chain in chains if next(chain, "end") != "end"]


def gather_row(me, out, cut, sems):
    sems = cut.row(sems)
    own = out.at[me.row, cut.span]
    copies = []
    for step in (2, 1, 3):
        copies.append(send(own, own, sems, step - 1, me.row_peer(step)))
    yield
    for step in (1, 3, 2):
        block = out.at[me.row_at(-step), cut.span]
        remote(block, block, sems, step - 1, me.row_peer(step)).wait_recv()
    finish(copies)


def gather_col(me, out, cut, sems):
    main, side = cut.col(sems)
    over, near, up, down = me.peer(1, 0), me.peer(0, 0, 1), me.peer(0, 1), me.peer(0, 3)
    copies = []

    def block(high, which, core=0, span=cut.span):
        return out.at[me.at(high, DEEPS[which], core), span]

    def pass_on(item, sems, index, device):
        copies.append(send(item, item, sems, index, device))

    def arrived(item, sems, index):
        remote(item, item, sems, index, near).wait_recv()

    def share(high, which):
        pass_on(block(high, which), side, 4 * high + which, near)

    def ring_start(high, base):
        pass_on(block(high, 0), main, base, up)
        pass_on(block(high, 0), main, base + 1, down)

    def ring_next(high, base):
        arrived(block(high, 1), main, base)
        pass_on(block(high, 1, 0, cut.low), main, base + 2, up)
        arrived(block(high, 2), main, base + 1)
        pass_on(block(high, 2, 0, cut.high), main, base + 3, down)

    def ring_end(high, base):
        arrived(block(high, 3, 0, cut.low), main, base + 2)
        arrived(block(high, 3, 0, cut.high), main, base + 3)

    if cut.z_first:
        ring_start(0, 0)
        pass_on(block(0, 0), main, 4, over)
        share(0, 0)
        yield
        ring_next(0, 0)
        for which in (1, 2):
            pass_on(block(0, which), main, 4 + which, over)
            share(0, which)
        yield
        ring_end(0, 0)
        pass_on(block(0, 3), main, 7, over)
        share(0, 3)
        arrived(block(1, 0), main, 4)
        share(1, 0)
        yield
        for which in (1, 2, 3):
            arrived(block(1, which), main, 4 + which)
            share(1, which)
    else:
        pass_on(block(0, 0), main, 8, over)
        ring_start(0, 0)
        share(0, 0)
        yield
        arrived(block(1, 0), main, 8)
        ring_start(1, 4)
        share(1, 0)
        ring_next(0, 0)
        share(0, 1)
        share(0, 2)
        yield
        ring_end(0, 0)
        share(0, 3)
        ring_next(1, 4)
        share(1, 1)
        share(1, 2)
        yield
        ring_end(1, 4)
        share(1, 3)
    yield
    for high in range(2):
        for which in range(4):
            arrived(block(high, which, 1), side, 4 * high + which)
    finish(copies)


def sum_row(me, part, landing, cut, sems, done):
    sems = cut.row(sems)
    copies = []
    for step in (2, 1, 3):
        copies.append(
            send(part.at[me.row_at(step), cut.span], landing.at[step - 1, cut.span], sems, step - 1, me.row_peer(step))
        )
    yield
    total = part[me.row, cut.span].astype(F32)
    for copy, step in zip(copies[1:] + copies[:1], (1, 3, 2)):
        copy.wait_recv()
        total = total + landing[step - 1, cut.span].astype(F32)
    yield from done(total, cut)
    finish(copies)


def sum_col(me, part, halves, outgoing, landing, cut, sems, done):
    main, side = cut.col(sems)
    over, near, span = me.peer(1, 0), me.peer(0, 0, 1), cut.span
    first, away = {}, {}
    for high in (1, 0):
        for deep in (2, 1, 3, 0):
            index = 4 * high + deep
            first[index] = send(part.at[me.at(high, deep, 1), span], halves.at[index, span], side, index, near)

    def pair(high, deep):
        index = 4 * high + deep
        first[index].wait_recv()
        return part[me.at(high, deep), span].astype(F32) + halves[index, span].astype(F32)

    def pass_on(slot, value, device):
        outgoing[slot, span] = value.astype(BF)
        away[slot] = send(outgoing.at[slot, span], landing.at[slot, span], main, slot, device)

    def landed(slot):
        away[slot].wait_recv()
        return landing[slot, span].astype(F32)

    yield
    if cut.z_first:
        for high in (1, 0):
            for deep in (2, 1, 3):
                pass_on(3 * high + deep - 1, pair(high, deep), me.peer(0, deep))
        yield
        total = pair(1, 0)
        for slot in (3, 5, 4):
            total = total + landed(slot)
        pass_on(6, total, over)
        yield
        total = pair(0, 0)
        for slot in (0, 2, 1, 6):
            total = total + landed(slot)
    else:
        for deep in (2, 1, 3, 0):
            pass_on(deep, pair(1, deep), over)
        yield
        for deep in (2, 1, 3):
            pass_on(3 + deep, pair(0, deep) + landed(deep), me.peer(0, deep))
        yield
        total = pair(0, 0) + landed(0)
        for slot in (4, 6, 5):
            total = total + landed(slot)
    yield from done(total, cut)
    finish(list(first.values()) + list(away.values()))


def sum_col_scratch(width):
    return dict(
        halves=pltpu.VMEM((8, TOK, width), BF),
        outgoing=pltpu.VMEM((7, TOK, width), BF),
        landing=pltpu.VMEM((7, TOK, width), BF),
    )


def store(ref):
    def done(total, cut):
        ref[cut.span, :] = total
        yield

    return done


def after_attention(me, h_ref, gain, other, resid, out, sems):
    def done(total, cut):
        span = cut.span
        value = h_ref[me.row, span].astype(F32) + RESID_MUL * total
        resid[span, :] = value
        scale = lax.rsqrt(jnp.mean(value * value, axis=1, keepdims=True) + NORM_EPS)
        normed = (value * scale * gain[...]).astype(BF)
        if other is not None:
            normed = jnp.where(me.section == 0, normed, other[span, :])
        out[me.col, span] = normed
        yield from gather_col(me, out, cut, sems)

    return done


def after_experts(me, resid, coming, nexth, out, arrived, over_sems, sems):
    def done(total, cut):
        span = cut.span
        nexth[span, :] = (resid[span, :] + RESID_MUL * total).astype(BF)
        if out is not None:
            over = send(nexth.at[span], arrived.at[span], cut.one(over_sems), 0, me.across())
            yield
            over.wait_recv()
            out[me.row, span] = jnp.where(me.section == 0, coming[span, :], arrived[span, :])
            yield from gather_row(me, out, cut, sems)
            over.wait_send()
        else:
            yield

    return done


def after_experts_back(me, resid, entry, gain, dr, dgain, out, sems):
    def done(total, cut):
        span = cut.span
        value = resid[span, :]
        scale = lax.rsqrt(jnp.mean(value * value, axis=1, keepdims=True) + NORM_EPS)
        weighted = total * gain[...]
        inner = jnp.mean(weighted * value, axis=1, keepdims=True)
        grad = entry[span, :].astype(F32) + scale * weighted - value * (scale * scale * scale) * inner
        out[me.row, span] = (RESID_MUL * grad).astype(BF)
        gather = gather_row(me, out, cut, sems)
        next(gather)
        dr[span, :] = grad
        term = jnp.sum(total * value * scale, axis=0, keepdims=True)
        dgain[...] = term if cut.first else dgain[...] + term
        yield
        yield from gather

    return done


def after_attention_back(me, dr, coming, dhin, entry, out, arrived, over_sems, sems):
    def done(total, cut):
        span = cut.span
        dhin[span, :] = (total + dr[span, :]).astype(BF)
        if out is not None:
            over = send(dhin.at[span], arrived.at[span], cut.one(over_sems), 0, me.across())
            yield
            over.wait_recv()
            chosen = jnp.where(me.section == 0, arrived[span, :], coming[span, :])
            entry[span, :] = chosen
            out[me.col, span] = chosen
            yield from gather_col(me, out, cut, sems)
            over.wait_send()
        else:
            yield

    return done


def sum_gains(me, gains, out, one, two, three, sems):
    sems = Sems(*sems)
    near = send(gains, one, sems, 0, me.peer(0, 0, 1))
    yield
    near.wait_recv()
    two[0] = gains[...] + one[...]
    chips = []
    for high in range(2):
        for deep in range(4):
            if high or deep:
                index = high * 4 + deep
                chips.append(send(two.at[0], two.at[index], sems, index, me.peer(high, deep)))
    yield
    for copy in chips:
        copy.wait_recv()
    three[0] = jnp.sum(two[...], axis=0)
    rows = []
    for step in (1, 2, 3):
        rows.append(send(three.at[0], three.at[step], sems, 7 + step, me.row_peer(step)))
    yield
    for copy in rows:
        copy.wait_recv()
    out[...] = jnp.sum(three[...], axis=0)
    finish([near] + chips + rows)


class RingSum:
    def __init__(self, me, blocks, land, total_out, sems):
        self.me, self.blocks, self.total_out = me, blocks, total_out
        self.passing, self.final = land
        self.sems = Sems(*sems)
        half = blocks.shape[2] // 2
        self.low, self.high = pl.ds(0, half), pl.ds(half, half)
        self.up, self.down = me.row_peer(1), me.row_peer(3)
        self.near_up, self.near_down, self.far = me.row_at(1), me.row_at(3), me.row_at(2)
        self.copies = {}

    def begin(self, piece):
        part, blocks = self.sems.part(6 * piece), self.blocks
        self.copies[piece] = [
            send(blocks.at[piece, self.far, self.low], self.passing.at[piece, 0], part, 0, self.up),
            send(blocks.at[piece, self.far, self.high], self.passing.at[piece, 1], part, 1, self.down),
            send(blocks.at[piece, self.near_up, self.high], self.final.at[piece, 0, self.high], part, 2, self.up),
            send(blocks.at[piece, self.near_down, self.low], self.final.at[piece, 1, self.low], part, 3, self.down),
        ]

    def pass_on(self, piece):
        part, copies = self.sems.part(6 * piece), self.copies[piece]
        for side, near, span, peer in ((0, self.near_up, self.low, self.up), (1, self.near_down, self.high, self.down)):
            copies[side].wait_recv()
            value = self.blocks[piece, near, span].astype(F32) + self.passing[piece, side].astype(F32)
            self.blocks[piece, near, span] = value.astype(BF)
            copies.append(send(self.blocks.at[piece, near, span], self.final.at[piece, side, span], part, 4 + side, peer))

    def end(self, piece):
        for copy in self.copies[piece][2:]:
            copy.wait_recv()
        self.total_out[piece] = (
            self.blocks[piece, self.me.row].astype(F32)
            + self.final[piece, 0].astype(F32)
            + self.final[piece, 1].astype(F32)
        ).astype(BF)
        finish(self.copies[piece])


def reduce_scratch(pieces, rows, width):
    return [
        pltpu.VMEM((pieces, 2, rows // 2, width), BF),
        pltpu.VMEM((pieces, 2, rows, width), BF),
    ]


def sds(shape, kind):
    return jax.ShapeDtypeStruct(shape, kind)


def call_remote(body, ident, ins, outs, scratch, limit, flops=10**7):
    flat, places = [], {}
    for name, item in scratch.items():
        if isinstance(item, list):
            places[name] = (len(flat), len(item))
            flat += item
        else:
            places[name] = (len(flat), None)
            flat.append(item)
    names = list(ins) + list(outs)

    def kernel(*refs):
        given = dict(zip(names, refs))
        rest = refs[len(names):]
        for name, (start, count) in places.items():
            given[name] = rest[start] if count is None else list(rest[start:start + count])
        body(types.SimpleNamespace(**given))

    results = pl.pallas_call(
        kernel,
        out_shape=list(outs.values()),
        in_specs=[VM] * len(ins),
        out_specs=[VM] * len(outs),
        scratch_shapes=flat,
        compiler_params=pltpu.CompilerParams(
            collective_id=ident, has_side_effects=True, vmem_limit_bytes=limit * 2**20
        ),
        cost_estimate=pl.CostEstimate(flops=flops, bytes_accessed=40 * 10**6, transcendentals=0),
    )(*ins.values())
    return types.SimpleNamespace(**dict(zip(outs, results)))


TOKEN_ROWS = sds((TOK, D), BF)
TOKEN_WIDE = sds((TOK, D), F32)
ROW_BLOCKS = sds((ROWS, TOK, D), BF)
COL_BLOCKS = sds((COLS, TOK, D), BF)
GAIN = sds((1, D), F32)
HEADS = sds((PACK, 256), BF)
WIDE_SLOTS = sds((2, SLOTS, D), BF)
FF_SLOTS = sds((2, SLOTS, FF), BF)
LAND_ROW = pltpu.VMEM((3, TOK, D), BF)
ARRIVED = pltpu.VMEM((TOK, D), BF)
ACROSS = [DMA((PARTS,))] * 2
ROW_PART = pltpu.VMEM((ROWS, TOK, D), BF)
COL_PART = pltpu.VMEM((COLS, TOK, D), BF)
KEPT = pltpu.VMEM((QUADS, 2 * 96, D), BF)
ATTENTION_OUTS = dict(n1=sds((PACK, D), BF), q=HEADS, kv=HEADS, o=HEADS)
EXPERT_OUTS = dict(xs=WIDE_SLOTS, g=FF_SLOTS, u=FF_SLOTS)
BACK_OUTS = dict(dy=WIDE_SLOTS, dgu=WIDE_SLOTS, z=sds((2, SLOTS, FF), BF))
ATTENTION_BACK_OUTS = dict(dp=sds((PACK, 512), BF), again=GAIN)


def attention_body(r, slot):
    attention_kernel(
        slot, r.packed, r.w, r.attn_gain, r.cosine, r.sine, r.seg, r.seg_t, r.part_x, r.n1, r.q, r.kv, r.o
    )


def tables_of(r, slot):
    return [getattr(r, name + str(slot)) for name in ("table", "table_t", "gslot")]


def experts_body(r, slot):
    experts_kernel(r.rows, *tables_of(r, slot), r.wg, r.wu, r.wd, r.part, r.xs, r.g, r.u, r.kept)


def experts_back_body(r, slot, ready=None):
    experts_back_kernel(
        r.grad_rows, *tables_of(r, slot), r.g_in, r.u_in, r.wg, r.wu, r.wd, r.part_b, r.dy, r.dgu, r.z, r.kept, ready
    )


def attention_back_body(r, slot):
    attention_back_kernel(
        slot, r.da, r.packed_b, r.w, r.attn_gain, r.cosine, r.sine, r.seg, r.seg_t, r.q_in, r.kv_in,
        r.part_y, r.dp, r.again,
    )


def run_start(w, rg, x):
    def body(r):
        me = Place()
        greeting = Greeting(row_partners(me) + col_partners(me))
        r.w_out[me.col] = r.w[...]
        r.rg_out[me.col] = r.rg[...]
        r.x_out[me.row] = r.x[...]
        greeting.wait()
        weave(
            *[gather_col(me, r.w_out, cut, r.col_w) for cut in ALL_CUTS],
            *[gather_row(me, r.x_out, cut, r.row) for cut in ALL_CUTS],
            *[gather_col(me, r.rg_out, cut, r.col_rg) for cut in ALL_CUTS],
        )

    return call_remote(
        body, 0, dict(w=w, rg=rg, x=x),
        dict(w_out=sds((COLS, TOK, 768), BF), rg_out=sds((COLS,) + rg.shape, F32), x_out=ROW_BLOCKS),
        dict(row=ROW_SEMS, col_w=COL_SEMS, col_rg=COL_SEMS), 8,
    )


TABLE_OUTS = {
    name + str(slot): shape
    for slot in range(2)
    for name, shape in (
        ("table", sds((QUADS, 8 * CAP, 4 * TOK), BF)),
        ("table_t", sds((QUADS, 4 * TOK, 8 * CAP), BF)),
        ("gslot", sds((2, SLOTS, 1), F32)),
    )
}


def run_forward(ident, slot, packed, coming, common, experts, other=None, shared=None, tables=None):
    first = other is not None

    def body(r):
        me = Place()
        greeting = Greeting(row_partners(me) + col_partners(me) + [me.across()])
        attention_body(r, slot)
        greeting.wait()
        done = after_attention(me, r.packed, r.moe_gain, r.other if first else None, r.resid, r.rows, r.col)

        def make_tables():
            for index in range(2):
                yield
                tables_kernel(index, r.shared, *tables_of(r, index))

        weave(
            *[sum_row(me, r.part_x, r.landing_x, cut, r.row, done) for cut in ALL_CUTS],
            *([make_tables()] if first else []),
        )
        experts_body(r, slot)
        done = after_experts(me, r.resid, r.coming, r.nexth, r.out, r.arrived, r.over, r.row_b)
        weave(*[sum_col(me, r.part, r.halves, r.outgoing, r.landing, cut, r.col_b, done) for cut in ALL_CUTS])

    extra = dict(other=other, shared=shared) if first else tables
    return call_remote(
        body, ident, dict(packed=packed, coming=coming, **common, **experts, **extra),
        dict(
            resid=TOKEN_WIDE, rows=COL_BLOCKS, nexth=TOKEN_ROWS, out=ROW_BLOCKS,
            **ATTENTION_OUTS, **EXPERT_OUTS, **(TABLE_OUTS if first else {}),
        ),
        dict(
            part_x=ROW_PART, landing_x=LAND_ROW, row=ROW_SEMS, col=COL_SEMS,
            part=COL_PART, kept=KEPT, arrived=ARRIVED, row_b=ROW_SEMS, col_b=COL_SEMS, over=ACROSS, **sum_col_scratch(D),
        ),
        LIMITS[0], 4 * 10**9,
    )


def run_turn(ident, packed, grad_rows, resid_b, entry_in, packed_b, coming, kept_f, common, experts, tables):
    def body(r):
        me = Place()
        greeting = Greeting(row_partners(me) + col_partners(me) + [me.across()])
        attention_body(r, 0)
        experts_back_body(r, 1)
        greeting.wait()
        done_f = after_attention(me, r.packed, r.moe_gain, None, r.resid, r.rows, r.col)
        done_b = after_experts_back(me, r.resid_b, r.entry_in, r.moe_gain, r.dr, r.dgain, r.da, r.row_b)
        weave(
            *[sum_row(me, r.part_x, r.landing_x, cut, r.row, done_f) for cut in ALL_CUTS],
            *[sum_col(me, r.part_b, r.halves, r.outgoing, r.landing, cut, r.col_b, done_b) for cut in ALL_CUTS],
        )
        attention_back_body(r, 1)
        experts_body(r, 0)
        done_f = after_experts(me, r.resid, None, r.nexth, None, None, None, None)
        done_b = after_attention_back(me, r.dr, r.coming, r.dhin, r.entry, r.out, r.arrived, r.over, r.col_c)
        weave(
            *[sum_row(me, r.part_y, r.landing_y, cut, r.row_c, done_b) for cut in ALL_CUTS],
            *[sum_col(me, r.part, r.halves_b, r.outgoing_b, r.landing_b, cut, r.col_d, done_f) for cut in ALL_CUTS],
        )

    second = {name + "_b": item for name, item in sum_col_scratch(D).items()}
    return call_remote(
        body, ident,
        dict(
            packed=packed, grad_rows=grad_rows, resid_b=resid_b, entry_in=entry_in, packed_b=packed_b, coming=coming,
            **kept_f, **common, **experts, **tables,
        ),
        dict(
            resid=TOKEN_WIDE, nexth=TOKEN_ROWS, dhin=TOKEN_ROWS, entry=TOKEN_ROWS, out=COL_BLOCKS,
            **ATTENTION_OUTS, **EXPERT_OUTS,
        ),
        dict(
            part_x=ROW_PART, landing_x=LAND_ROW, row=ROW_SEMS, col=COL_SEMS, part_b=COL_PART, kept=KEPT,
            row_b=ROW_SEMS, col_b=COL_SEMS, **sum_col_scratch(D), **second,
            part_y=ROW_PART, landing_y=LAND_ROW, arrived=ARRIVED, row_c=ROW_SEMS, col_c=COL_SEMS, over=ACROSS,
            part=COL_PART, col_d=COL_SEMS,
            **{name: pltpu.VMEM(item.shape, item.dtype) for name, item in dict(
                rows=COL_BLOCKS, dr=TOKEN_WIDE, dgain=GAIN, da=ROW_BLOCKS, **BACK_OUTS, **ATTENTION_BACK_OUTS
            ).items()},
        ),
        LIMITS[1], 10**10,
    )


def run_backward(ident, slot, grad_rows, resid, entry_in, packed_b, coming, kept_f, common, experts, tables):
    def body(r):
        me = Place()
        greeting = Greeting(row_partners(me) + col_partners(me) + [me.across()])
        experts_back_body(r, slot)
        greeting.wait()
        done = after_experts_back(me, r.resid, r.entry_in, r.moe_gain, r.dr, r.dgain, r.da, r.row)
        weave(*[sum_col(me, r.part_b, r.halves, r.outgoing, r.landing, cut, r.col, done) for cut in ALL_CUTS])
        attention_back_body(r, slot)
        done = after_attention_back(me, r.dr, r.coming, r.dhin, r.entry, r.out, r.arrived, r.over, r.col_b)
        weave(*[sum_row(me, r.part_y, r.landing_x, cut, r.row_b, done) for cut in ALL_CUTS])

    return call_remote(
        body, ident,
        dict(
            grad_rows=grad_rows, resid=resid, entry_in=entry_in, packed_b=packed_b, coming=coming,
            **kept_f, **common, **experts, **tables,
        ),
        dict(
            dgain=GAIN, da=ROW_BLOCKS, dhin=TOKEN_ROWS, entry=TOKEN_ROWS, out=COL_BLOCKS,
            **BACK_OUTS, **ATTENTION_BACK_OUTS,
        ),
        dict(
            part_b=COL_PART, kept=KEPT, row=ROW_SEMS, col=COL_SEMS, **sum_col_scratch(D),
            dr=pltpu.VMEM((TOK, D), F32),
            part_y=ROW_PART, landing_x=LAND_ROW, arrived=ARRIVED, row_b=ROW_SEMS, col_b=COL_SEMS, over=ACROSS,
        ),
        LIMITS[2], 5 * 10**9,
    )


def run_final(ident, slot, grad_rows, resid, entry_in, packed_b, kept_f, earlier, common, experts, tables):
    def body(r):
        me = Place()
        greeting = Greeting(row_partners(me) + all_chip_partners(me) + [me.peer(0, 0, 1)])
        done = after_experts_back(me, r.resid, r.entry_in, r.moe_gain, r.dr, r.dgain, r.da, r.row)
        ring = RingSum(me, r.blocks, r.land_blocks, r.gate_up_sum, r.ring_sems)
        ring_down = RingSum(me, r.down, r.land_down, r.down_sum, r.ring_down_sems)

        def make(piece):
            kind, expert = divmod(piece, 2)
            span = slice(kind * FF, (kind + 1) * FF)
            value = dot_rows(r.xs_a[expert], r.dgu_a[expert, :, span]) + dot_rows(
                r.xs_b[expert], r.dgu[expert, :, span]
            )
            r.blocks[piece] = value.astype(BF).reshape(ROWS, 256, FF)
            ring.begin(piece)

        def make_down(expert):
            value = (dot_rows(r.z_a[expert], r.dy_a[expert]) + dot_rows(r.z[expert], r.dy[expert])).astype(BF)
            for row in range(ROWS):
                r.down[expert, row] = value[:, row * 256:(row + 1) * 256]
            ring_down.begin(expert)

        def ready():
            greeting.wait()
            make_down(0)

        def grads():
            make_down(1)
            yield
            ring_down.pass_on(0)
            make(0)
            yield
            ring_down.pass_on(1)
            yield
            make(1)
            ring.pass_on(0)
            yield
            make(2)
            yield
            make(3)

        experts_back_body(r, slot, ready)
        weave(
            *[sum_col(me, r.part_b, r.halves, r.outgoing, r.landing, cut, r.col, done) for cut in ALL_CUTS],
            grads(),
        )
        attention_back_body(r, slot)
        weight_part = r.part_b.at[:, :, 0:768]
        attention_weights_kernel(r.n1_a, r.n1_b, r.dp_a, r.dp, r.da_a, r.da, r.o_a, r.o_b, r.part_b)
        r.gains[0:1] = r.again_a[...] + r.again[...]
        r.gains[1:2] = r.dgain_a[...] + r.dgain[...]
        done = after_attention_back(me, r.dr, None, r.dhin, None, None, None, None, None)

        def rest():
            ring.pass_on(1)
            yield
            ring.pass_on(2)
            yield
            ring.pass_on(3)
            yield
            ring_down.end(0)
            ring_down.end(1)
            ring.end(0)
            yield
            for piece in (1, 2, 3):
                ring.end(piece)

        weave(
            *[sum_col(me, weight_part, r.halves_b, r.outgoing_b, r.landing_b, cut, r.col_b, store(r.weight_sum)) for cut in ALL_CUTS],
            sum_gains(me, r.gains, r.gain_sum, r.one, r.two, r.three, r.gain_sems),
            rest(),
            *[sum_row(me, r.part_y, r.landing_x, cut, r.row_b, done) for cut in ALL_CUTS],
        )

    second = {name + "_b": item for name, item in sum_col_scratch(768).items()}
    return call_remote(
        body, ident,
        dict(
            grad_rows=grad_rows, resid=resid, entry_in=entry_in, packed_b=packed_b,
            **kept_f, **earlier, **common, **experts, **tables,
        ),
        dict(
            dhin=TOKEN_ROWS, weight_sum=sds((TOK, 768), F32), gain_sum=sds((2, D), F32),
            gate_up_sum=sds((4, 256, FF), BF), down_sum=sds((2, FF, 256), BF),
        ),
        dict(
            blocks=pltpu.VMEM((4, ROWS, 256, FF), BF), land_blocks=reduce_scratch(4, 256, FF), ring_sems=[DMA((24,))] * 2,
            down=pltpu.VMEM((2, ROWS, FF, 256), BF), land_down=reduce_scratch(2, FF, 256), ring_down_sems=[DMA((12,))] * 2,
            part_b=COL_PART, kept=KEPT, row=ROW_SEMS, col=COL_SEMS, **sum_col_scratch(D), **second,
            part_y=ROW_PART, landing_x=LAND_ROW, row_b=ROW_SEMS, col_b=COL_SEMS,
            gains=pltpu.VMEM((2, D), F32),
            one=pltpu.VMEM((2, D), F32), two=pltpu.VMEM((8, 2, D), F32), three=pltpu.VMEM((4, 2, D), F32),
            gain_sems=[DMA((11,))] * 2,
            **{name: pltpu.VMEM(item.shape, item.dtype) for name, item in dict(
                dr=TOKEN_WIDE, dgain=GAIN, da=ROW_BLOCKS, **BACK_OUTS, **ATTENTION_BACK_OUTS
            ).items()},
        ),
        LIMITS[3], 10**10,
    )


LIMITS = (16, 26, 18, 34)


def swap_halves(value):
    width = value.shape[1]
    lane = lax.broadcasted_iota(jnp.int32, value.shape, 1)
    low = lax.rem(lane, HEAD) < HEAD // 2
    up = pltpu.roll(value, HEAD // 2, axis=1)
    down = pltpu.roll(value, width - HEAD // 2, axis=1)
    return low, up, down


def rope(value, cosine, sine):
    low, up, down = swap_halves(value)
    return value * cosine + jnp.where(low, -down, up) * sine


def rope_back(value, cosine, sine):
    low, up, down = swap_halves(value * sine)
    return value * cosine + jnp.where(low, down, -up)


def allowed_mask(seg, seg_t):
    shape = (PACK, PACK)
    query = lax.broadcasted_iota(jnp.int32, shape, 0)
    key = lax.broadcasted_iota(jnp.int32, shape, 1)
    return (seg == seg_t) & (key <= query)


def probabilities(q, k, allowed):
    scores = jnp.where(allowed, dot_cols(q, k) * SCORE_MUL, -1e30)
    weights = jnp.exp(scores - jnp.max(scores, axis=1, keepdims=True))
    return weights / jnp.sum(weights, axis=1, keepdims=True)


def attention_kernel(slot, x_ref, w, gain, cosine, sine, seg, seg_t, part, n1, q_out, kv_out, o_out):
    x = x_ref[...].reshape(PACK, D).astype(F32)
    scale = lax.rsqrt(jnp.mean(x * x, axis=1, keepdims=True) + NORM_EPS)
    normed = (x * scale * gain[...]).astype(BF)
    n1[...] = normed
    cos, sin = cosine[slot], sine[slot]
    pre = dot(normed, w[:, 0:512])
    q = jnp.concatenate(
        [rope(pre[:, 0:128], cos, sin), rope(pre[:, 128:256], cos, sin)], axis=1
    ).astype(BF)
    k = rope(pre[:, 256:384], cos, sin).astype(BF)
    v = pre[:, 384:512].astype(BF)
    q_out[...] = q
    kv_out[:, 0:128] = k
    kv_out[:, 128:256] = v
    allowed = allowed_mask(seg[slot], seg_t[slot])
    heads = []
    for head in range(4):
        at = (head // 2) * HEAD
        prob = probabilities(q[:, head * HEAD:(head + 1) * HEAD], k[:, at:at + HEAD], allowed)
        heads.append(dot(prob.astype(BF), v[:, at:at + HEAD]))
    mixed = jnp.concatenate(heads, axis=1).astype(BF)
    o_out[...] = mixed
    part[...] = dot_cols(mixed, w[:, 512:768]).astype(BF).reshape(ROWS, TOK, D)


def attention_back_kernel(
    slot, da, x_ref, w, gain, cosine, sine, seg, seg_t, q_ref, kv_ref, part, dp_out, dgain
):
    cos, sin = cosine[slot], sine[slot]
    do = dot(da[...].reshape(PACK, D), w[:, 512:768]).astype(BF)
    q = q_ref[...]
    kv = kv_ref[...]
    allowed = allowed_mask(seg[slot], seg_t[slot])
    dqs, dks, dvs = [], [None, None], [None, None]
    for head in range(4):
        group = head // 2
        at = group * HEAD
        qh = q[:, head * HEAD:(head + 1) * HEAD]
        kh = kv[:, at:at + HEAD]
        vh = kv[:, 128 + at:128 + at + HEAD]
        doh = do[:, head * HEAD:(head + 1) * HEAD]
        prob = probabilities(qh, kh, allowed)
        dv = dot_rows(prob.astype(BF), doh)
        dprob = dot_cols(doh, vh)
        ds = (prob * (dprob - jnp.sum(prob * dprob, axis=1, keepdims=True))).astype(BF)
        dqs.append(dot(ds, kh) * SCORE_MUL)
        dk = dot_rows(ds, qh) * SCORE_MUL
        dks[group] = dk if dks[group] is None else dks[group] + dk
        dvs[group] = dv if dvs[group] is None else dvs[group] + dv
    dp = jnp.concatenate(
        [
            rope_back(jnp.concatenate(dqs[0:2], axis=1), cos, sin),
            rope_back(jnp.concatenate(dqs[2:4], axis=1), cos, sin),
            rope_back(jnp.concatenate(dks, axis=1), cos, sin),
            jnp.concatenate(dvs, axis=1),
        ],
        axis=1,
    ).astype(BF)
    dp_out[...] = dp
    dn1 = dot_cols(dp, w[:, 0:512])
    x = x_ref[...].reshape(PACK, D).astype(F32)
    scale = lax.rsqrt(jnp.mean(x * x, axis=1, keepdims=True) + NORM_EPS)
    dgain[...] = jnp.sum(dn1 * x * scale, axis=0, keepdims=True)
    weighted = dn1 * gain[...]
    inner = jnp.mean(weighted * x, axis=1, keepdims=True)
    part[...] = (scale * weighted - x * (scale * scale * scale) * inner).astype(BF).reshape(ROWS, TOK, D)


def place_rows(table, rows, out):
    for quad in range(QUADS):
        value = dot(table[quad], rows[quad * 4:(quad + 1) * 4].reshape(4 * TOK, D)).astype(BF)
        out[0, quad * 96:(quad + 1) * 96, :] = value[0:96]
        out[1, quad * 96:(quad + 1) * 96, :] = value[96:192]


def return_rows(table, value, out):
    for quad in range(QUADS):
        out[quad * 4:(quad + 1) * 4] = dot(table[quad], value[quad]).astype(BF).reshape(4, TOK, D)


def keep_rows(out, expert, value):
    for quad in range(QUADS):
        out[quad, expert * 96:(expert + 1) * 96, :] = value[quad * 96:(quad + 1) * 96]


def experts_kernel(rows, table, table_t, gslot, wg, wu, wd, part, xs, g_out, u_out, kept):
    place_rows(table, rows, xs)
    for expert in range(2):
        x = xs[expert]
        g = dot(x, wg[expert])
        u = dot(x, wu[expert])
        g_out[expert] = g.astype(BF)
        u_out[expert] = u.astype(BF)
        z = (g * jax.nn.sigmoid(g) * u).astype(BF)
        y = dot(z, wd[expert]).astype(BF).astype(F32)
        keep_rows(kept, expert, (y * gslot[expert]).astype(BF))
    return_rows(table_t, kept, part)


def experts_back_kernel(
    rows, table, table_t, gslot, g_ref, u_ref, wg, wu, wd, part, dy_out, dgu_out, z_out, kept, ready=None
):
    place_rows(table, rows, dy_out)
    for expert in range(2):
        dy_out[expert] = ((RESID_MUL * gslot[expert]) * dy_out[expert].astype(F32)).astype(BF)
        if ready is not None:
            g, u = g_ref[expert].astype(F32), u_ref[expert].astype(F32)
            z_out[expert] = (g * jax.nn.sigmoid(g) * u).astype(BF)
    if ready is not None:
        ready()
    for expert in range(2):
        dz = dot_cols(dy_out[expert], wd[expert])
        g, u = g_ref[expert].astype(F32), u_ref[expert].astype(F32)
        sig = jax.nn.sigmoid(g)
        silu = g * sig
        if ready is None:
            z_out[expert] = (silu * u).astype(BF)
        dg = (dz * u * sig * (1.0 + g * (1.0 - sig))).astype(BF)
        du = (dz * silu).astype(BF)
        dgu_out[expert, :, 0:FF] = dg
        dgu_out[expert, :, FF:2 * FF] = du
        keep_rows(kept, expert, (dot_cols(dg, wg[expert]) + dot_cols(du, wu[expert])).astype(BF))
    return_rows(table_t, kept, part)


def attention_weights_kernel(na, nb, pa, pb, da_a, da_b, oa, ob, out):
    one = (dot_rows(na[...], pa[...]) + dot_rows(nb[...], pb[...])).astype(BF)
    two = (
        dot_rows(da_a[...].reshape(PACK, D), oa[...]) + dot_rows(da_b[...].reshape(PACK, D), ob[...])
    ).astype(BF)
    out[:, :, 0:512] = one.reshape(COLS, TOK, 512)
    out[:, :, 512:768] = two.reshape(COLS, TOK, 256)


def owner_kernel(lengths, routes, gates, rank_gate, cosine, sine, seg, seg_t):
    section = lax.axis_index("section")
    expert = lax.broadcasted_iota(jnp.int32, (EXPERTS, TOK), 0)
    before = (
        lax.broadcasted_iota(jnp.int32, (TOK, TOK), 0) < lax.broadcasted_iota(jnp.int32, (TOK, TOK), 1)
    ).astype(BF)
    place = lax.broadcasted_iota(jnp.int32, (PACK, 128), 0)
    place_t = lax.broadcasted_iota(jnp.int32, (8, PACK), 1)
    lane = lax.rem(lax.broadcasted_iota(jnp.int32, (PACK, 128), 1), HEAD // 2).astype(F32)
    frequency = jnp.exp(lane * (-2.0 / HEAD * math.log(ROPE_THETA)))
    for slot in range(2):
        micro = section if slot == 0 else 1 - section
        chosen = jnp.zeros((EXPERTS, TOK), F32)
        gate = jnp.zeros((EXPERTS, TOK), F32)
        for k in range(8):
            same = expert == routes[micro, k:k + 1, :]
            chosen = chosen + jnp.where(same, 1.0, 0.0)
            gate = gate + jnp.where(same, gates[micro, k:k + 1, :], 0.0)
        rank = jnp.where(chosen > 0.5, dot(chosen.astype(BF), before), -1.0)
        rank_gate[slot * EXPERTS:(slot + 1) * EXPERTS, :] = jnp.concatenate([rank, gate], axis=1)
        segment = jnp.zeros((PACK, 128), jnp.int32)
        segment_t = jnp.zeros((8, PACK), jnp.int32)
        start = jnp.zeros((PACK, 128), jnp.int32)
        end = jnp.int32(0)
        for k in range(4):
            size = lengths[micro, k]
            end = end + size
            segment = segment + jnp.where(place >= end, 1, 0)
            segment_t = segment_t + jnp.where(place_t >= end, 1, 0)
            start = start + jnp.where(place >= end, size, 0)
        angles = (place - start).astype(F32) * frequency
        cosine[slot] = jnp.cos(angles)
        sine[slot] = jnp.sin(angles)
        seg[slot] = segment[:, 0:1]
        seg_t[slot] = segment_t[0:1, :]


def run_owner(lengths, routes, gates):
    return pl.pallas_call(
        owner_kernel,
        out_shape=[
            sds((2 * EXPERTS, 128), F32), sds((2, PACK, 128), F32), sds((2, PACK, 128), F32),
            sds((2, PACK, 1), jnp.int32), sds((2, 1, PACK), jnp.int32),
        ],
        in_specs=[pl.BlockSpec(memory_space=pltpu.SMEM), VM, VM],
        out_specs=[VM] * 5,
        compiler_params=pltpu.CompilerParams(vmem_limit_bytes=8 * 2**20),
    )(lengths, routes, gates)


def tables_kernel(slot, shared, table, table_t, gslot):
    col = lax.axis_index("col")
    shape = (4 * CAP, 4 * TOK)
    line = lax.broadcasted_iota(jnp.int32, shape, 0)
    column = lax.broadcasted_iota(jnp.int32, shape, 1)
    own_group = (line // CAP) == (column // TOK)
    wanted = lax.rem(line, CAP).astype(F32)
    for quad in range(QUADS):
        for expert in range(2):
            rows = [
                shared[4 * quad + index, pl.ds(slot * EXPERTS + 2 * col + expert, 1), :] for index in range(4)
            ]
            rank = jnp.concatenate([row[:, 0:TOK] for row in rows], axis=1)
            gate = jnp.concatenate([row[:, TOK:2 * TOK] for row in rows], axis=1)
            mark = jnp.where(own_group & (rank == wanted), 1.0, 0.0)
            table[quad, expert * 96:(expert + 1) * 96, :] = mark.astype(BF)
            table_t[quad, :, expert * 96:(expert + 1) * 96] = mark.T.astype(BF)
            gslot[expert, quad * 96:(quad + 1) * 96, :] = jnp.sum(mark * gate, axis=1, keepdims=True)


def per_device(
    ends_in, q_weight, key_projection, value_projection, out_weight, attn_gain, moe_gain,
    gate_weight, up_weight, down_weight, routes, gates, lengths,
):
    section = lax.axis_index("section")
    ends = ends_in[0, :, 0]
    rank_gate, cosine, sine, seg, seg_t = run_owner(
        lengths[:, 0], jnp.swapaxes(routes[0, :, 0], 1, 2), jnp.swapaxes(gates[0, :, 0], 1, 2)
    )
    own = jnp.concatenate([q_weight[0], key_projection[0], value_projection[0], out_weight[0]], axis=1)
    started = run_start(own, rank_gate, ends[0])
    experts = dict(wg=gate_weight[0], wu=up_weight[0], wd=down_weight[0])
    common = dict(
        w=started.w_out.reshape(D, 768), attn_gain=attn_gain, moe_gain=moe_gain,
        cosine=cosine, sine=sine, seg=seg, seg_t=seg_t,
    )

    zero = run_forward(1, 0, started.x_out, ends[1], common, experts, other=ends[0], shared=started.rg_out)
    tables = {name: getattr(zero, name) for name in TABLE_OUTS}
    slots = [{name: item for name, item in tables.items() if name[-1] == str(slot)} for slot in range(2)]
    one = run_forward(2, 1, zero.out, ends[0], common, experts, tables=slots[1])
    kept_one = dict(q_in=one.q, kv_in=one.kv, g_in=one.g, u_in=one.u)
    two = run_turn(
        3, one.out, zero.rows, one.resid, ends[0], zero.out, ends[1], kept_one, common, experts, tables
    )
    kept_two = dict(q_in=two.q, kv_in=two.kv, g_in=two.g, u_in=two.u)
    back = run_backward(
        4, 0, two.out, two.resid, two.entry, one.out, ends[0], kept_two, common, experts, slots[0]
    )
    earlier = dict(
        xs_a=two.xs, dgu_a=back.dgu, z_a=back.z, dy_a=back.dy, xs_b=one.xs, n1_a=two.n1, n1_b=one.n1,
        dp_a=back.dp, da_a=back.da, o_a=two.o, o_b=one.o, again_a=back.again, dgain_a=back.dgain,
    )
    last = run_final(5, 1, back.out, one.resid, back.entry, zero.out, kept_one, earlier, common, experts, slots[1])
    forward_one, forward_two = one.nexth, two.nexth
    backward_one, backward_two = back.dhin, last.dhin
    attn_sum, gain_sum = last.weight_sum, last.gain_sum
    on_first = section == 0
    ends_out = jnp.stack(
        [jnp.where(on_first, backward_one, forward_one), jnp.where(on_first, backward_two, forward_two)], axis=0
    )[None, :, None]
    return (
        ends_out,
        attn_sum[None, :, 0:256],
        attn_sum[None, :, 256:384],
        attn_sum[None, :, 384:512],
        attn_sum[None, :, 512:768],
        gain_sum[0:1],
        gain_sum[1:2],
        last.gate_up_sum[None, 0:2].astype(F32),
        last.gate_up_sum[None, 2:4].astype(F32),
        last.down_sum[None].astype(F32),
    )


def solution(mesh):
    tokens = P("section", None, "col", "row", None)
    mats = P("section", "col", "row")
    gain = P("section", None)
    experts = P("section", "col", None, None)
    by_row = P("section", "col", "row", None)
    return jax.shard_map(
        per_device,
        mesh=mesh,
        in_specs=(tokens, mats, mats, mats, mats, gain, gain, experts, experts, experts, tokens, tokens, P(None, "col", None)),
        out_specs=(tokens, mats, mats, mats, mats, gain, gain, by_row, by_row, P("section", "col", None, "row")),
        check_vma=False,
    )
```
